256 devices in a mesh: dp: 16 (over x_lo, z), fsdp: 16 (over x_hi, y, core).
Axes of the slice: x: 4 (x_hi: 2, x_lo: 2; x = x_hi * 2 + x_lo), y: 4, z: 8, core: 2. Of those that a mesh axis runs over, the one named last changes fastest.
Arguments:
- patches: bfloat16 [65536, 1792], P(('dp', 'fsdp')), may hold values from -12 to 12
- queries: bfloat16 [65536, 896], P(('dp', 'fsdp')), may hold values from -16 to 16
- keys: bfloat16 [65536, 896], P(('dp', 'fsdp')), may hold values from -16 to 16
- upstream: bfloat16 [65536, 1792], P(('dp', 'fsdp')), may hold values from -1 to 1
- value_weight: float32 [1792, 896], P('fsdp'), may hold values from -1 to 1
- output_weight: float32 [896, 1792], P('fsdp'), may hold values from -0.1875 to 0.1875
- value_first: float32 [1792, 896], P('fsdp'), may hold values from -6 to 6
- output_first: float32 [896, 1792], P('fsdp'), may hold values from -6 to 6
- value_second: float32 [1792, 896], P('fsdp'), may hold values from 1 to 50
- output_second: float32 [896, 1792], P('fsdp'), may hold values from 1 to 50
Outputs:
- value_weight_new: float32 [1792, 896], P('fsdp')
- output_weight_new: float32 [896, 1792], P('fsdp')
- value_first_new: float32 [1792, 896], P('fsdp')
- output_first_new: float32 [896, 1792], P('fsdp')
- value_second_new: float32 [1792, 896], P('fsdp')
- output_second_new: float32 [896, 1792], P('fsdp')
The draws below stay inside these ranges and needn't reach their ends.
All inputs are finite; a program needn't handle non-finite values.
Results may differ from the reference program's by a relative error of at most 0.022.
Values may be sent and summed in bfloat16 or wider, within the bound.
A program may use at most 128 MiB of HBM per device.

```python
import math
import jax
import jax.numpy as jnp
from jax import lax

D = 1792
HEADS = 8
HD = 112
SEQ = 256
HID = 896
TOK_DEV = 256
TOKENS = 65536
N_DP = 16
N_FSDP = 16


def shared_keys(key, strength):
    normal_part = jnp.clip(jax.random.normal(jax.random.fold_in(key, 11), (TOKENS, HID), jnp.float32), -4.0, 4.0)
    position = jnp.arange(TOKENS) % SEQ
    chosen = strength * ((position == 10) | (position == 11)).astype(jnp.float32)[:, None]
    return normal_part * (1.0 - chosen)


def rising(count, low):
    return low + jnp.arange(count).astype(jnp.float32) / (count - 1.0)


def draw_keys(key, part):
    result = shared_keys(key, 0.0)
    return result.astype(jnp.bfloat16)


def draw_queries(key, part):
    key = jax.random.fold_in(key, 3)
    own = jnp.clip(jax.random.normal(key, (TOKENS, HID), jnp.float32), -4.0, 4.0)
    return own.astype(jnp.bfloat16)


def draw_patches(key, part):
    key = jax.random.fold_in(key, 5)
    own = jnp.clip(jax.random.normal(key, (TOKENS, D), jnp.float32), -6.0, 6.0)
    scales = rising(D, 0.5)
    return (own * scales[None, :]).astype(jnp.bfloat16)


def draw_value_weight(key, part):
    key = jax.random.fold_in(key, 7)
    own = jnp.clip(jax.random.normal(key, (D, HID), jnp.float32), -6.0, 6.0)
    scales = rising(HID, 0.5)
    return own * scales[None, :] * D ** (-0.5)


def block_levels(key, dims, pieces, smallest, top_value):
    loudness = 1.0
    for axis_at, blocks in pieces:
        steps = jax.random.uniform(jax.random.fold_in(jax.random.fold_in(key, 6), axis_at), (blocks,), jnp.float32, smallest / len(pieces), top_value / len(pieces))
        loudness = loudness * jnp.repeat(jnp.exp(steps), dims[axis_at] // blocks).reshape((-1,) + (1,) * (len(dims) - 1 - axis_at))
    return loudness


def noise(rng, shape, spread, most, cuts=(), kind=jnp.bfloat16):
    gain = block_levels(rng, shape, cuts, -0.22, 0.18) if cuts else 1.0
    values = jax.random.normal(rng, shape, jnp.float32) * spread * gain
    return jnp.minimum(jnp.maximum(values, -most), most).astype(kind)


def setup_inputs(seed: int = 0) -> dict:
    arg_keys = jax.random.split(jax.random.key(seed), 11)
    return {
        "patches": draw_patches(jax.random.fold_in(arg_keys[10], 71), 0),
        "queries": draw_queries(jax.random.fold_in(arg_keys[10], 71), 0),
        "keys": draw_keys(jax.random.fold_in(arg_keys[10], 71), 0),
        "upstream": noise(arg_keys[3], (TOKENS, D), (16 * TOKENS ** -0.5), 1.0, ((0, 256),)),
        "value_weight": draw_value_weight(jax.random.fold_in(arg_keys[10], 71), 0),
        "output_weight": noise(arg_keys[5], (HID, D), HID ** -0.5, 0.1875, ((0, 16),), jnp.float32),
        "value_first": noise(arg_keys[6], (D, HID), 1.0, 6.0, ((0, 16),), jnp.float32),
        "output_first": noise(arg_keys[7], (HID, D), 1.0, 6.0, ((0, 16),), jnp.float32),
        "value_second": jnp.clip(jnp.exp(math.log(50.0) - 3.912023 * jax.random.uniform(arg_keys[8], (D, HID), jnp.float32) ** block_levels(arg_keys[8], (D, HID), ((0, 16),), -0.2, 0.2)), 1.0, 50.0),
        "output_second": jnp.clip(jnp.exp(math.log(50.0) - 3.912023 * jax.random.uniform(arg_keys[9], (HID, D), jnp.float32) ** block_levels(arg_keys[9], (HID, D), ((0, 16),), -0.2, 0.2)), 1.0, 50.0),
    }


learn_rate = 0.001
weight_decay = 0.1
beta_one = 0.9
beta_two = 0.999
adam_eps = 1e-08
first_fix = 0.9999734386011124
second_fix = 0.0952078528862911
rho_scale = 0.05

def norm_rows(rows):
    rows = rows.astype(jnp.float32)
    centred = rows - lax.optimization_barrier(jnp.mean(rows, axis=-1, keepdims=True))
    return centred * lax.rsqrt(lax.optimization_barrier(jnp.mean(centred * centred, axis=-1, keepdims=True)) + 1e-06)

def attention_weights(queries, keys):
    query_heads = queries.astype(jnp.float32).reshape(-1, SEQ, HEADS, HD)
    key_heads = keys.astype(jnp.float32).reshape(-1, SEQ, HEADS, HD)
    scores = jnp.einsum('bqhd,bkhd->bhqk', query_heads, key_heads) * HD ** (-0.5)
    scores = scores - lax.optimization_barrier(jnp.max(scores, axis=-1, keepdims=True))
    expo = jnp.exp(scores)
    return (expo / lax.optimization_barrier(jnp.sum(expo, axis=-1, keepdims=True))).astype(jnp.bfloat16)

def apply_heads(attention, values):
    rows = values.shape[0]
    heads = values.astype(jnp.float32).reshape(-1, SEQ, HEADS, HD)
    mixed = jnp.einsum('bhqk,bkhd->bqhd', attention.astype(jnp.float32), heads)
    return mixed.reshape(rows, HEADS * HD).astype(jnp.bfloat16)

def apply_back(attention, d_mixed):
    rows = d_mixed.shape[0]
    heads = d_mixed.astype(jnp.float32).reshape(-1, SEQ, HEADS, HD)
    back = jnp.einsum('bhqk,bqhd->bkhd', attention.astype(jnp.float32), heads)
    return back.reshape(rows, HEADS * HD).astype(jnp.bfloat16)

def local_grads(normed, patches, attention, upstream, values, output_b):
    mixed = apply_heads(attention, values)
    outcome = patches.astype(jnp.float32) + jnp.dot(mixed, output_b, preferred_element_type=jnp.float32)
    centred = outcome - lax.optimization_barrier(jnp.mean(outcome, axis=-1, keepdims=True))
    inverse = lax.rsqrt(lax.optimization_barrier(jnp.mean(centred * centred, axis=-1, keepdims=True)) + 1e-06)
    normal_out = centred * inverse
    signal = upstream.astype(jnp.float32)
    d_outcome = inverse * (signal - lax.optimization_barrier(jnp.mean(signal, axis=-1, keepdims=True)) - normal_out * lax.optimization_barrier(jnp.mean(signal * normal_out, axis=-1, keepdims=True)))
    d_outcome = d_outcome.astype(jnp.bfloat16)
    grad_output = jnp.dot(mixed.T, d_outcome, preferred_element_type=jnp.float32)
    d_mixed = jnp.dot(d_outcome, output_b.T, preferred_element_type=jnp.float32).astype(jnp.bfloat16)
    d_values = apply_back(attention, d_mixed)
    grad_value = jnp.dot(normed.T, d_values, preferred_element_type=jnp.float32)
    return (grad_value, grad_output)

def rounded(term):
    return lax.optimization_barrier(term.astype(jnp.bfloat16)).astype(jnp.float32)

def adam_update(weight, first, second, gradient):
    first_new = beta_one * first + (1.0 - beta_one) * gradient
    second_new = beta_two * second + (1.0 - beta_two) * gradient * gradient
    update = first_new / first_fix / (jnp.sqrt(second_new / second_fix) + adam_eps) + weight_decay * weight
    return (weight - learn_rate * update, first_new, second_new)

def reference(patches, queries, keys, upstream, value_weight, output_weight, value_first, output_first, value_second, output_second):
    devices_all = N_DP * N_FSDP
    blocks = (patches.reshape(devices_all, TOK_DEV, D), queries.reshape(devices_all, TOK_DEV, HID), keys.reshape(devices_all, TOK_DEV, HID), upstream.reshape(devices_all, TOK_DEV, D))

    def summed(value_b, output_b):

        def advance(sums_so_far, device_rows):
            rows_in, rows_query, rows_key, rows_up = device_rows
            normed = norm_rows(rows_in).astype(jnp.bfloat16)
            attention = attention_weights(rows_query, rows_key)
            values = jnp.dot(normed, value_b, preferred_element_type=jnp.float32).astype(jnp.bfloat16)
            grad_value, grad_output = local_grads(normed, rows_in, attention, rows_up, values, output_b)
            return ((sums_so_far[0] + rounded(grad_value), sums_so_far[1] + rounded(grad_output)), None)
        initial = (jnp.zeros((D, HID), jnp.float32), jnp.zeros((HID, D), jnp.float32))
        result, _ = lax.scan(advance, initial, blocks)
        return result
    first_value, first_output = summed(value_weight.astype(jnp.bfloat16), output_weight.astype(jnp.bfloat16))
    mean_square = (jnp.sum(first_value * first_value) + jnp.sum(first_output * first_output)) / (2.0 * D * HID)
    stretch = rho_scale / jnp.sqrt(mean_square + 1e-06)
    shifted_value = (value_weight + stretch * first_value).astype(jnp.bfloat16)
    shifted_output = (output_weight + stretch * first_output).astype(jnp.bfloat16)
    second_value, second_output = summed(shifted_value, shifted_output)
    value_new, value_first_new, value_second_new = adam_update(value_weight, value_first, value_second, second_value)
    output_new, output_first_new, output_second_new = adam_update(output_weight, output_first, output_second, second_output)
    return (value_new, output_new, value_first_new, output_first_new, value_second_new, output_second_new)
```

```python
import functools

import jax
import jax.numpy as jnp
from jax import lax
from jax.experimental import pallas as pl
from jax.experimental.pallas import tpu as pltpu
from jax.sharding import PartitionSpec as P

HEADS = 8
HD = 112
SEQ = 256
D = 1792
HID = 896
BLOCKS = 7
WIDTHS = (512, 384)
MESH = pl.DeviceIdType.MESH
BF = jnp.bfloat16
F32 = jnp.float32


learn_rate = 0.001
weight_decay = 0.1
beta_one = 0.9
beta_two = 0.999
adam_eps = 1e-08
first_fix = 0.9999734386011124
second_fix = 0.0952078528862911
rho_scale = 0.05


def place():
    dp = lax.axis_index("dp")
    fs = lax.axis_index("fsdp")
    return (fs // 8) * 2 + dp // 8, (fs // 2) % 4, dp % 8, fs % 2


def device(x, y, z, c):
    return ((x % 2) * 8 + z, (x // 2) * 8 + y * 2 + c)


def slot(x):
    return (x % 2) * 2 + x // 2


class Net:
    def __init__(self):
        self.x, self.y, self.z, self.c = place()

    def core(self):
        return device(self.x, self.y, self.z, 1 - self.c)

    def along(self, axis, step):
        if axis == "x":
            return device((self.x + step) % 4, self.y, self.z, self.c)
        if axis == "y":
            return device(self.x, (self.y + step) % 4, self.z, self.c)
        return device(self.x, self.y, (self.z + step) % 8, self.c)

    def spot(self, axis, step=0):
        if axis == "x":
            return slot((self.x + step) % 4)
        if axis == "y":
            return (self.y + step) % 4
        return (self.z + step) % 8

    def barrier(self):
        sem = pltpu.get_barrier_semaphore()
        targets = [self.core()]
        targets += [self.along("x", s) for s in (1, 2, 3)]
        targets += [self.along("y", s) for s in (1, 2, 3)]
        targets += [self.along("z", s) for s in range(1, 8)]
        for t in targets:
            pl.semaphore_signal(sem, inc=1, device_id=t, device_id_type=MESH)
        pl.semaphore_wait(sem, len(targets))


def push(src, dst, send, recv, target):
    copy = pltpu.make_async_remote_copy(
        src_ref=src, dst_ref=dst, send_sem=send, recv_sem=recv, device_id=target, device_id_type=MESH
    )
    copy.start()
    return copy


def add_blocks(count, write, *reads):
    def step(i, carry):
        total = reads[0](i).astype(F32)
        for read in reads[1:]:
            total = total + read(i).astype(F32)
        write(i, total.astype(BF))
        return carry

    lax.fori_loop(0, count, step, 0)


def ordered(part):
    return ("x", "y") if part == 0 else ("y", "x")


def grid_at(ref, part, first, second):
    return ref.at[first, second] if part == 0 else ref.at[second, first]


def reduce_scratch():
    shapes = []
    for w in WIDTHS:
        shapes += [
            pltpu.VMEM((4, 4, BLOCKS, 16, w), BF),
            pltpu.VMEM((4, 4, BLOCKS, 16, w), BF),
            pltpu.VMEM((2, 2, BLOCKS, 16, w), BF),
            pltpu.VMEM((2, 4, BLOCKS, 16, w), BF),
            pltpu.VMEM((4, BLOCKS, 16, w), BF),
            pltpu.VMEM((3, BLOCKS, 16, w), BF),
            pltpu.VMEM((BLOCKS, 16, w), BF),
            pltpu.VMEM((7, 16, w), BF),
            pltpu.SemaphoreType.DMA((2, 4 + 2 + 4 + 3 + 7)),
        ]
    return shapes


def reduce_all(net, grads, outs, scratch):
    state = []
    for part in (0, 1):
        state.append(scratch[part * 9:part * 9 + 9])
    rows = []
    cores = [[], []]
    for step in (2, 1, 3, 0):
        for part in (0, 1):
            other, sums, far, mine, _, _, _, _, sem = state[part]
            first = ordered(part)[0]
            i = net.spot(first, step)
            j = len(cores[part])
            if part == 0:
                src, dst = grads[part].at[i, :, 1 - net.c], other.at[i]
            else:
                src, dst = grads[part].at[:, i, 1 - net.c], other.at[:, i]
            cores[part].append(push(src, dst, sem.at[0, j], sem.at[1, j], net.core()))
    waits = []

    def half_of(ref, part, i, h):
        return ref.at[i, pl.ds(2 * h, 2)] if part == 0 else ref.at[pl.ds(2 * h, 2), i]

    near = [[None] * 6, [None] * 6]
    for j, step in enumerate((2, 1, 3, 0)):
        for part in (0, 1):
            other, sums, far, mine, _, _, _, _, sem = state[part]
            first = ordered(part)[0]
            i = net.spot(first, step)
            cores[part][j].wait_recv()
            g = grads[part]
            if part == 0:
                def write(k, v):
                    sums[i, k] = v
                add_blocks(4, write, lambda k: g[i, k, net.c], lambda k: other[i, k])
            else:
                def write(k, v):
                    sums[k, i] = v
                add_blocks(4, write, lambda k: g[k, i, net.c], lambda k: other[k, i])
            right, left = net.along(first, 1), net.along(first, 3)
            if step == 2:
                near[part][0] = push(half_of(sums, part, i, 0), far.at[0], sem.at[0, 4], sem.at[1, 4], right)
                near[part][1] = push(half_of(sums, part, i, 1), far.at[1], sem.at[0, 5], sem.at[1, 5], left)
            if step == 1:
                near[part][2] = push(half_of(sums, part, i, 1), mine.at[0, pl.ds(2, 2)], sem.at[0, 6], sem.at[1, 6], right)
            if step == 3:
                near[part][3] = push(half_of(sums, part, i, 0), mine.at[1, pl.ds(0, 2)], sem.at[0, 7], sem.at[1, 7], left)
    for part in (0, 1):
        other, sums, far, mine, _, _, _, _, sem = state[part]
        first = ordered(part)[0]
        right, left = net.along(first, 1), net.along(first, 3)
        r, l = net.spot(first, 1), net.spot(first, 3)
        near[part][0].wait_recv()
        if part == 0:
            def write(k, v):
                sums[r, k] = v
            add_blocks(2, write, lambda k: sums[r, k], lambda k: far[0, k])
        else:
            def write(k, v):
                sums[k, r] = v
            add_blocks(2, write, lambda k: sums[k, r], lambda k: far[0, k])
        near[part][4] = push(half_of(sums, part, r, 0), mine.at[0, pl.ds(0, 2)], sem.at[0, 8], sem.at[1, 8], right)
        near[part][1].wait_recv()
        if part == 0:
            def write(k, v):
                sums[l, k + 2] = v
            add_blocks(2, write, lambda k: sums[l, k + 2], lambda k: far[1, k])
        else:
            def write(k, v):
                sums[k + 2, l] = v
            add_blocks(2, write, lambda k: sums[k + 2, l], lambda k: far[1, k])
        near[part][5] = push(half_of(sums, part, l, 1), mine.at[1, pl.ds(2, 2)], sem.at[0, 9], sem.at[1, 9], left)
    second_copies = [[], []]
    for part in (0, 1):
        other, sums, far, mine, row, from_row, _, _, sem = state[part]
        first, second = ordered(part)
        me = net.spot(first)
        for k in (2, 3, 4, 5):
            near[part][k].wait_recv()

        def write(k, v):
            row[k] = v
        if part == 0:
            add_blocks(4, write, lambda k: sums[me, k], lambda k: mine[0, k], lambda k: mine[1, k])
        else:
            add_blocks(4, write, lambda k: sums[k, me], lambda k: mine[0, k], lambda k: mine[1, k])
        for d in (2, 1, 3):
            second_copies[part].append(
                push(row.at[net.spot(second, d)], from_row.at[d - 1], sem.at[0, 9 + d], sem.at[1, 9 + d], net.along(second, d))
            )
    for part in (0, 1):
        other, sums, far, mine, row, from_row, line, from_line, sem = state[part]
        second = ordered(part)[1]
        me = net.spot(second)
        for copy in second_copies[part]:
            copy.wait_recv()

        def write(k, v):
            line[k] = v
        add_blocks(BLOCKS, write, lambda k: row[me, k], lambda k: from_row[0, k], lambda k: from_row[1, k], lambda k: from_row[2, k])
        for d in (4, 3, 5, 2, 6, 1, 7):
            z = net.spot("z", d)

            @pl.when(z != 7)
            def _():
                push(line.at[z], from_line.at[d - 1], sem.at[0, 12 + d], sem.at[1, 12 + d], net.along("z", d))
    for part in (0, 1):
        other, sums, far, mine, row, from_row, line, from_line, sem = state[part]

        @pl.when(net.z != 7)
        def _():
            for d in range(1, 8):
                pltpu.make_async_remote_copy(
                    src_ref=line.at[0], dst_ref=from_line.at[d - 1], send_sem=sem.at[0, 12 + d], recv_sem=sem.at[1, 12 + d],
                    device_id=net.along("z", d), device_id_type=MESH,
                ).wait_recv()
            total = line[net.z].astype(F32)
            for d in range(7):
                total = total + from_line[d].astype(F32)
            outs[part][...] = total.astype(BF)

    def drain():
        for part in (0, 1):
            other, sums, far, mine, row, from_row, line, from_line, sem = state[part]
            for copy in cores[part] + near[part] + second_copies[part]:
                copy.wait_send()
            for d in range(1, 8):
                @pl.when(net.spot("z", d) != 7)
                def _():
                    pltpu.make_async_remote_copy(
                        src_ref=line.at[0], dst_ref=from_line.at[d - 1], send_sem=sem.at[0, 12 + d], recv_sem=sem.at[1, 12 + d],
                        device_id=net.along("z", d), device_id_type=MESH,
                    ).wait_send()
    return drain


def gather_scratch():
    return [pltpu.SemaphoreType.DMA((2, 3 + 6 + 8)) for _ in WIDTHS]


def gather_all(net, fulls, sems):
    seconds = [[], []]
    for part in (0, 1):
        second = ordered(part)[1]
        own = fulls[part].at[net.spot("x"), net.spot("y"), net.c]
        for d in (2, 1, 3):
            seconds[part].append(push(own, own, sems[part].at[0, d - 1], sems[part].at[1, d - 1], net.along(second, d)))

    def line(part, i, h):
        ref = fulls[part]
        return ref.at[i, pl.ds(2 * h, 2), net.c] if part == 0 else ref.at[pl.ds(2 * h, 2), i, net.c]

    def whole(part, i):
        ref = fulls[part]
        return ref.at[i, :, net.c] if part == 0 else ref.at[:, i, net.c]

    copies = [[], []]
    cores = [[], []]
    for part in (0, 1):
        first = ordered(part)[0]
        for copy in seconds[part]:
            copy.wait_recv()
        right, left = net.along(first, 1), net.along(first, 3)
        me = net.spot(first)
        sem = sems[part]
        for j, (h, to) in enumerate(((0, right), (1, left), (1, right), (0, left))):
            copies[part].append(push(line(part, me, h), line(part, me, h), sem.at[0, 3 + j], sem.at[1, 3 + j], to))
        cores[part].append(push(whole(part, me), whole(part, me), sem.at[0, 9], sem.at[1, 9], net.core()))
    for part in (0, 1):
        first = ordered(part)[0]
        right, left = net.along(first, 1), net.along(first, 3)
        r, l = net.spot(first, 1), net.spot(first, 3)
        sem = sems[part]
        copies[part][0].wait_recv()
        copies[part].append(push(line(part, l, 0), line(part, l, 0), sem.at[0, 7], sem.at[1, 7], right))
        copies[part][1].wait_recv()
        copies[part].append(push(line(part, r, 1), line(part, r, 1), sem.at[0, 8], sem.at[1, 8], left))
        cores[part].append(push(line(part, l, 0), line(part, l, 0), sem.at[0, 10], sem.at[1, 10], net.core()))
        cores[part].append(push(line(part, r, 1), line(part, r, 1), sem.at[0, 11], sem.at[1, 11], net.core()))
    for part in (0, 1):
        first = ordered(part)[0]
        r, l, far = net.spot(first, 1), net.spot(first, 3), net.spot(first, 2)
        sem = sems[part]
        for k, i, h in ((2, l, 1), (3, r, 0), (4, far, 0), (5, far, 1)):
            copies[part][k].wait_recv()
            cores[part].append(push(line(part, i, h), line(part, i, h), sem.at[0, 10 + k], sem.at[1, 10 + k], net.core()))
    for part in (0, 1):
        for copy in cores[part]:
            copy.wait_recv()
        for copy in seconds[part] + copies[part] + cores[part]:
            copy.wait_send()


def weights_kernel(own_a, own_b, full_a, full_b, sem_a, sem_b, copy_sem):
    net = Net()
    net.barrier()
    fulls = (full_a, full_b)
    for part, own in enumerate((own_a, own_b)):
        copy = pltpu.make_async_copy(own.at[net.x % 2], fulls[part].at[net.spot("x"), net.spot("y"), net.c], copy_sem.at[part])
        copy.start()
        copy.wait()
    gather_all(net, fulls, (sem_a, sem_b))


def spread_line(net, fulls, outs, sems):
    for part in (0, 1):
        @pl.when(net.z != 7)
        def _():
            dst = fulls[part].at[net.spot("x"), net.spot("y"), net.c, net.z]
            dst[...] = outs[part][...]
            for d in (4, 3, 5, 2, 6, 1, 7):
                push(dst, dst, sems[part].at[0, d - 1], sems[part].at[1, d - 1], net.along("z", d))


def wait_line(net, fulls, sems, recv):
    for part in (0, 1):
        for d in range(1, 8):
            z = net.z if not recv else (net.z + 8 - d) % 8
            block = fulls[part].at[net.spot("x"), net.spot("y"), net.c, jnp.minimum(z, 6)]

            @pl.when(z != 7)
            def _():
                copy = pltpu.make_async_remote_copy(
                    src_ref=block, dst_ref=block, send_sem=sems[part].at[0, d - 1], recv_sem=sems[part].at[1, d - 1],
                    device_id=net.along("z", d), device_id_type=MESH,
                )
                if recv:
                    copy.wait_recv()
                else:
                    copy.wait_send()


def middle_kernel(grad_a, grad_b, full_a, full_b, out_a, out_b, line_a, line_b, sem_a, sem_b, *scratch):
    net = Net()
    net.barrier()
    fulls, outs = (full_a, full_b), (out_a, out_b)
    drain = reduce_all(net, (grad_a, grad_b), outs, scratch)
    spread_line(net, fulls, outs, (line_a, line_b))
    wait_line(net, fulls, (line_a, line_b), True)
    gather_all(net, fulls, (sem_a, sem_b))
    wait_line(net, fulls, (line_a, line_b), False)
    drain()


def last_kernel(grad_a, grad_b, owned_a, owned_b, out_a, out_b, line_a, line_b, pair_a, pair_b, *scratch):
    net = Net()
    net.barrier()
    owned, outs = (owned_a, owned_b), (out_a, out_b)
    drain = reduce_all(net, (grad_a, grad_b), outs, scratch)
    half = net.x % 2
    partner = device(net.x + 1 - 2 * half, net.y, net.z, net.c)

    def block(part, z):
        return owned[part].at[half, jnp.minimum(z, 6)]

    def line_copy(part, d, z):
        sems = (line_a, line_b)[part]
        return pltpu.make_async_remote_copy(
            src_ref=block(part, z), dst_ref=block(part, z), send_sem=sems.at[0, d - 1], recv_sem=sems.at[1, d - 1],
            device_id=net.along("z", d), device_id_type=MESH,
        )

    def pair_copy(part, d, z):
        sems = (pair_a, pair_b)[part]
        return pltpu.make_async_remote_copy(
            src_ref=block(part, z), dst_ref=block(part, z), send_sem=sems.at[0, d], recv_sem=sems.at[1, d],
            device_id=partner, device_id_type=MESH,
        )

    for part in (0, 1):
        @pl.when(net.z != 7)
        def _():
            owned[part][half, net.z] = outs[part][...]
            for d in (4, 3, 5, 2, 6, 1, 7):
                line_copy(part, d, net.z).start()
            pair_copy(part, 0, net.z).start()
    for d in (1, 7, 2, 6, 3, 5, 4):
        z = (net.z + 8 - d) % 8

        @pl.when(z != 7)
        def _():
            for part in (0, 1):
                line_copy(part, d, z).wait_recv()
                pair_copy(part, d, z).start()
    for d in range(8):
        z = (net.z + 8 - d) % 8

        @pl.when(z != 7)
        def _():
            for part in (0, 1):
                pair_copy(part, d, z).wait()
    for part in (0, 1):
        @pl.when(net.z != 7)
        def _():
            for d in range(1, 8):
                line_copy(part, d, net.z).wait_send()
    drain()


def vmem(n):
    return [pl.BlockSpec(memory_space=pltpu.VMEM)] * n


def params(cid):
    return pltpu.CompilerParams(collective_id=cid, has_side_effects=True, vmem_limit_bytes=60 * 2**20)


def full_shapes():
    return tuple(jax.ShapeDtypeStruct((4, 4, 2, BLOCKS, 16, w), BF) for w in WIDTHS)


def gather_weights(own):
    a, b = own[..., :WIDTHS[0]], own[..., WIDTHS[0]:]
    return pl.pallas_call(
        weights_kernel,
        out_shape=full_shapes(),
        in_specs=vmem(2),
        out_specs=vmem(2),
        scratch_shapes=gather_scratch() + [pltpu.SemaphoreType.DMA((2,))],
        name="gather_weights",
        compiler_params=params(0),
    )(a, b)


def line_sems(n=7):
    return [pltpu.SemaphoreType.DMA((2, n)) for _ in WIDTHS]


def block_scratch():
    return [pltpu.VMEM((16, w), BF) for w in WIDTHS]


def sum_and_gather(grads):
    return pl.pallas_call(
        middle_kernel,
        out_shape=full_shapes(),
        in_specs=vmem(2),
        out_specs=vmem(2),
        scratch_shapes=block_scratch() + line_sems() + gather_scratch() + reduce_scratch(),
        name="sum_and_gather",
        compiler_params=params(1),
    )(*grads)


def sum_owned(grads):
    return pl.pallas_call(
        last_kernel,
        out_shape=tuple(jax.ShapeDtypeStruct((2, BLOCKS, 16, w), BF) for w in WIDTHS),
        in_specs=vmem(2),
        out_specs=vmem(2),
        scratch_shapes=block_scratch() + line_sems() + line_sems(8) + reduce_scratch(),
        name="sum_owned",
        compiler_params=params(2),
    )(*grads)


def norm_rows(rows):
    rows = rows.astype(F32)
    centred = rows - jnp.mean(rows, axis=-1, keepdims=True)
    return centred * lax.rsqrt(jnp.mean(centred * centred, axis=-1, keepdims=True) + 1e-06)


def attention_weights(queries, keys):
    query_heads = queries.reshape(-1, SEQ, HEADS, HD)
    key_heads = keys.reshape(-1, SEQ, HEADS, HD)
    scores = jnp.einsum("bqhd,bkhd->bhqk", query_heads, key_heads, preferred_element_type=F32) * HD ** (-0.5)
    scores = scores - jnp.max(scores, axis=-1, keepdims=True)
    expo = jnp.exp(scores)
    return (expo / jnp.sum(expo, axis=-1, keepdims=True)).astype(BF)


def apply_heads(attention, values):
    rows = values.shape[0]
    heads = values.reshape(-1, SEQ, HEADS, HD)
    mixed = jnp.einsum("bhqk,bkhd->bqhd", attention, heads, preferred_element_type=F32)
    return mixed.reshape(rows, HEADS * HD).astype(BF)


def apply_back(attention, d_mixed):
    rows = d_mixed.shape[0]
    heads = d_mixed.reshape(-1, SEQ, HEADS, HD)
    back = jnp.einsum("bhqk,bqhd->bkhd", attention, heads, preferred_element_type=F32)
    return back.reshape(rows, HEADS * HD).astype(BF)


def contract_rows(left, right):
    return lax.dot_general(left, right, (((0,), (0,)), ((), ())), preferred_element_type=F32)


def local_grads(normed, patches, attention, upstream, values, output_b):
    mixed = apply_heads(attention, values)
    outcome = patches.astype(F32) + jnp.dot(mixed, output_b, preferred_element_type=F32)
    centred = outcome - jnp.mean(outcome, axis=-1, keepdims=True)
    inverse = lax.rsqrt(jnp.mean(centred * centred, axis=-1, keepdims=True) + 1e-06)
    normal_out = centred * inverse
    signal = upstream.astype(F32)
    d_outcome = inverse * (
        signal
        - jnp.mean(signal, axis=-1, keepdims=True)
        - normal_out * jnp.mean(signal * normal_out, axis=-1, keepdims=True)
    )
    d_outcome = d_outcome.astype(BF)
    grad_output = contract_rows(mixed, d_outcome)
    d_mixed = lax.dot_general(
        d_outcome, output_b, (((1,), (1,)), ((), ())), preferred_element_type=F32
    ).astype(BF)
    d_values = apply_back(attention, d_mixed)
    grad_value = contract_rows(normed, d_values)
    return grad_value.astype(BF), grad_output.astype(BF)


def fold_output(rows, lead):
    half = rows.reshape(lead + (56, 2, HID))
    return jnp.swapaxes(half, -3, -2).reshape(lead + (BLOCKS, 16, HID))


def unfold_output(blocks):
    folded = blocks.reshape(-1, 2, 56, HID)
    return jnp.swapaxes(folded, 1, 2).reshape(-1, D)


def pack(grad_value, grad_output):
    value = grad_value.reshape(2, 4, 2, BLOCKS, 16, HID)
    output = fold_output(grad_output, (2, 4, 2))
    both = jnp.concatenate([value, output], axis=0)
    return both[..., :WIDTHS[0]], both[..., WIDTHS[0]:]


def unpack(fulls):
    both = jnp.concatenate(fulls, axis=-1)
    return both[:2].reshape(D, HID), unfold_output(both[2:])


def adam_update(weight, first, second, gradient):
    first_new = beta_one * first + (1.0 - beta_one) * gradient
    second_new = beta_two * second + (1.0 - beta_two) * gradient * gradient
    update = (
        first_new / first_fix / (jnp.sqrt(second_new / second_fix) + adam_eps)
        + weight_decay * weight
    )
    return (weight - learn_rate * update, first_new, second_new)


def on_device(
    patches,
    queries,
    keys,
    upstream,
    value_weight,
    output_weight,
    value_first,
    output_first,
    value_second,
    output_second,
):
    own = jnp.stack([
        value_weight.astype(BF).reshape(BLOCKS, 16, HID),
        fold_output(output_weight.astype(BF), ()),
    ])
    value_full, output_full = unpack(gather_weights(own))
    normed = norm_rows(patches).astype(BF)
    attention = attention_weights(queries, keys)
    base = jnp.dot(normed, value_full, preferred_element_type=F32)
    grads = local_grads(normed, patches, attention, upstream, base.astype(BF), output_full)
    value_sum, output_sum = unpack(sum_and_gather(pack(*grads)))
    squares = jnp.sum(value_sum.astype(F32) ** 2) + jnp.sum(output_sum.astype(F32) ** 2)
    stretch = rho_scale / jnp.sqrt(squares / (2.0 * D * HID) + 1e-06)
    values = base + stretch * jnp.dot(normed, value_sum, preferred_element_type=F32)
    output_shifted = (output_full.astype(F32) + stretch * output_sum.astype(F32)).astype(BF)
    grads = local_grads(normed, patches, attention, upstream, values.astype(BF), output_shifted)
    owned = jnp.concatenate(sum_owned(pack(*grads)), axis=-1).astype(F32)
    value_new, value_first_new, value_second_new = adam_update(
        value_weight, value_first, value_second, owned[0].reshape(112, HID)
    )
    output_new, output_first_new, output_second_new = adam_update(
        output_weight, output_first, output_second, unfold_output(owned[1])
    )
    return (
        value_new,
        output_new,
        value_first_new,
        output_first_new,
        value_second_new,
        output_second_new,
    )


def solution(mesh):
    return jax.shard_map(
        on_device,
        mesh=mesh,
        in_specs=(P(("dp", "fsdp"), None),) * 4 + (P("fsdp", None),) * 6,
        out_specs=(P("fsdp", None),) * 6,
        check_vma=False,
    )
```

```python
import jax
import jax.numpy as jnp
from jax import lax
from jax.experimental import pallas as pl
from jax.experimental.pallas import tpu as pltpu
from jax.sharding import PartitionSpec as P

HEADS = 8
HD = 112
SEQ = 256
D = 1792
HID = 896
BLOCKS = 7
WIDTHS = (512, 384)
MESH = pl.DeviceIdType.MESH
BF = jnp.bfloat16
F32 = jnp.float32


learn_rate = 0.001
weight_decay = 0.1
beta_one = 0.9
beta_two = 0.999
adam_eps = 1e-08
first_fix = 0.9999734386011124
second_fix = 0.0952078528862911
rho_scale = 0.05


def place():
    dp = lax.axis_index("dp")
    fs = lax.axis_index("fsdp")
    return (fs // 8) * 2 + dp // 8, (fs // 2) % 4, dp % 8, fs % 2


def device(x, y, z, c):
    return ((x % 2) * 8 + z, (x // 2) * 8 + y * 2 + c)


def slot(x):
    return (x % 2) * 2 + x // 2


class Net:
    def __init__(self):
        self.x, self.y, self.z, self.c = place()

    def core(self):
        return device(self.x, self.y, self.z, 1 - self.c)

    def along(self, axis, step):
        if axis == "x":
            return device((self.x + step) % 4, self.y, self.z, self.c)
        if axis == "y":
            return device(self.x, (self.y + step) % 4, self.z, self.c)
        return device(self.x, self.y, (self.z + step) % 8, self.c)

    def spot(self, axis, step=0):
        if axis == "x":
            return slot((self.x + step) % 4)
        if axis == "y":
            return (self.y + step) % 4
        return (self.z + step) % 8

    def barrier(self):
        sem = pltpu.get_barrier_semaphore()
        targets = [self.core()]
        targets += [self.along("x", s) for s in (1, 2, 3)]
        targets += [self.along("y", s) for s in (1, 2, 3)]
        targets += [self.along("z", s) for s in range(1, 8)]
        for t in targets:
            pl.semaphore_signal(sem, inc=1, device_id=t, device_id_type=MESH)
        pl.semaphore_wait(sem, len(targets))


def push(src, dst, send, recv, target):
    copy = pltpu.make_async_remote_copy(
        src_ref=src, dst_ref=dst, send_sem=send, recv_sem=recv, device_id=target, device_id_type=MESH
    )
    copy.start()
    return copy


def add_blocks(count, write, *reads):
    def step(i, carry):
        total = reads[0](i).astype(F32)
        for read in reads[1:]:
            total = total + read(i).astype(F32)
        write(i, total.astype(BF))
        return carry

    lax.fori_loop(0, count, step, 0)


def ordered(part):
    return ("x", "y") if part == 0 else ("y", "x")


def grid_at(ref, part, first, second):
    return ref.at[first, second] if part == 0 else ref.at[second, first]


def reduce_scratch():
    shapes = []
    for w in WIDTHS:
        shapes += [
            pltpu.VMEM((4, 4, BLOCKS, 16, w), BF),
            pltpu.VMEM((4, 4, BLOCKS, 16, w), BF),
            pltpu.VMEM((2, 2, BLOCKS, 16, w), BF),
            pltpu.VMEM((2, 4, BLOCKS, 16, w), BF),
            pltpu.VMEM((4, BLOCKS, 16, w), BF),
            pltpu.VMEM((3, BLOCKS, 16, w), BF),
            pltpu.VMEM((BLOCKS, 16, w), BF),
            pltpu.VMEM((7, 16, w), BF),
            pltpu.SemaphoreType.DMA((2, 4 + 2 + 4 + 3 + 7)),
        ]
    return shapes


def reduce_all(net, grads, outs, scratch, make):
    make(1 - net.c)
    state = []
    for part in (0, 1):
        state.append(scratch[part * 9:part * 9 + 9])
    cores = [[], []]
    for step in (2, 1, 3, 0):
        for part in (0, 1):
            other, sums, far, mine, _, _, _, _, sem = state[part]
            first = ordered(part)[0]
            i = net.spot(first, step)
            j = len(cores[part])
            if part == 0:
                src, dst = grads[part].at[i, :, 1 - net.c], other.at[i]
            else:
                src, dst = grads[part].at[:, i, 1 - net.c], other.at[:, i]
            cores[part].append(push(src, dst, sem.at[0, j], sem.at[1, j], net.core()))
    make(net.c)

    def half_of(ref, part, i, h):
        return ref.at[i, pl.ds(2 * h, 2)] if part == 0 else ref.at[pl.ds(2 * h, 2), i]

    near = [[None] * 6, [None] * 6]
    for j, step in enumerate((2, 1, 3, 0)):
        for part in (0, 1):
            other, sums, far, mine, _, _, _, _, sem = state[part]
            first = ordered(part)[0]
            i = net.spot(first, step)
            cores[part][j].wait_recv()
            g = grads[part]
            if part == 0:
                def write(k, v):
                    sums[i, k] = v
                add_blocks(4, write, lambda k: g[i, k, net.c], lambda k: other[i, k])
            else:
                def write(k, v):
                    sums[k, i] = v
                add_blocks(4, write, lambda k: g[k, i, net.c], lambda k: other[k, i])
            right, left = net.along(first, 1), net.along(first, 3)
            if step == 2:
                near[part][0] = push(half_of(sums, part, i, 0), far.at[0], sem.at[0, 4], sem.at[1, 4], right)
                near[part][1] = push(half_of(sums, part, i, 1), far.at[1], sem.at[0, 5], sem.at[1, 5], left)
            if step == 1:
                near[part][2] = push(half_of(sums, part, i, 1), mine.at[0, pl.ds(2, 2)], sem.at[0, 6], sem.at[1, 6], right)
            if step == 3:
                near[part][3] = push(half_of(sums, part, i, 0), mine.at[1, pl.ds(0, 2)], sem.at[0, 7], sem.at[1, 7], left)
    for part in (0, 1):
        other, sums, far, mine, _, _, _, _, sem = state[part]
        first = ordered(part)[0]
        right, left = net.along(first, 1), net.along(first, 3)
        r, l = net.spot(first, 1), net.spot(first, 3)
        near[part][0].wait_recv()
        if part == 0:
            def write(k, v):
                sums[r, k] = v
            add_blocks(2, write, lambda k: sums[r, k], lambda k: far[0, k])
        else:
            def write(k, v):
                sums[k, r] = v
            add_blocks(2, write, lambda k: sums[k, r], lambda k: far[0, k])
        near[part][4] = push(half_of(sums, part, r, 0), mine.at[0, pl.ds(0, 2)], sem.at[0, 8], sem.at[1, 8], right)
        near[part][1].wait_recv()
        if part == 0:
            def write(k, v):
                sums[l, k + 2] = v
            add_blocks(2, write, lambda k: sums[l, k + 2], lambda k: far[1, k])
        else:
            def write(k, v):
                sums[k + 2, l] = v
            add_blocks(2, write, lambda k: sums[k + 2, l], lambda k: far[1, k])
        near[part][5] = push(half_of(sums, part, l, 1), mine.at[1, pl.ds(2, 2)], sem.at[0, 9], sem.at[1, 9], left)
    second_copies = [[], []]
    for part in (0, 1):
        other, sums, far, mine, row, from_row, _, _, sem = state[part]
        first, second = ordered(part)
        me = net.spot(first)
        for k in (2, 3, 4, 5):
            near[part][k].wait_recv()

        def write(k, v):
            row[k] = v
        if part == 0:
            add_blocks(4, write, lambda k: sums[me, k], lambda k: mine[0, k], lambda k: mine[1, k])
        else:
            add_blocks(4, write, lambda k: sums[k, me], lambda k: mine[0, k], lambda k: mine[1, k])
        for d in (2, 1, 3):
            second_copies[part].append(
                push(row.at[net.spot(second, d)], from_row.at[d - 1], sem.at[0, 9 + d], sem.at[1, 9 + d], net.along(second, d))
            )
    for part in (0, 1):
        other, sums, far, mine, row, from_row, line, from_line, sem = state[part]
        second = ordered(part)[1]
        me = net.spot(second)
        for copy in second_copies[part]:
            copy.wait_recv()

        def write(k, v):
            line[k] = v
        add_blocks(BLOCKS, write, lambda k: row[me, k], lambda k: from_row[0, k], lambda k: from_row[1, k], lambda k: from_row[2, k])
        for d in (4, 3, 5, 2, 6, 1, 7):
            z = net.spot("z", d)

            @pl.when(z != 7)
            def _():
                push(line.at[z], from_line.at[d - 1], sem.at[0, 12 + d], sem.at[1, 12 + d], net.along("z", d))
    for part in (0, 1):
        other, sums, far, mine, row, from_row, line, from_line, sem = state[part]

        @pl.when(net.z != 7)
        def _():
            for d in range(1, 8):
                pltpu.make_async_remote_copy(
                    src_ref=line.at[0], dst_ref=from_line.at[d - 1], send_sem=sem.at[0, 12 + d], recv_sem=sem.at[1, 12 + d],
                    device_id=net.along("z", d), device_id_type=MESH,
                ).wait_recv()
            total = line[net.z].astype(F32)
            for d in range(7):
                total = total + from_line[d].astype(F32)
            outs[part][...] = total.astype(BF)

    def drain():
        for part in (0, 1):
            other, sums, far, mine, row, from_row, line, from_line, sem = state[part]
            for copy in cores[part] + near[part] + second_copies[part]:
                copy.wait_send()
            for d in range(1, 8):
                @pl.when(net.spot("z", d) != 7)
                def _():
                    pltpu.make_async_remote_copy(
                        src_ref=line.at[0], dst_ref=from_line.at[d - 1], send_sem=sem.at[0, 12 + d], recv_sem=sem.at[1, 12 + d],
                        device_id=net.along("z", d), device_id_type=MESH,
                    ).wait_send()
    return drain


def gather_scratch():
    return [pltpu.SemaphoreType.DMA((2, 3 + 6 + 8)) for _ in WIDTHS]


def gather_all(net, fulls, sems, between=()):
    seconds = [[], []]
    for part in (0, 1):
        second = ordered(part)[1]
        own = fulls[part].at[net.spot("x"), net.spot("y"), net.c]
        for d in (2, 1, 3):
            seconds[part].append(push(own, own, sems[part].at[0, d - 1], sems[part].at[1, d - 1], net.along(second, d)))

    def line(part, i, h):
        ref = fulls[part]
        return ref.at[i, pl.ds(2 * h, 2), net.c] if part == 0 else ref.at[pl.ds(2 * h, 2), i, net.c]

    def whole(part, i):
        ref = fulls[part]
        return ref.at[i, :, net.c] if part == 0 else ref.at[:, i, net.c]

    copies = [[], []]
    cores = [[], []]
    if between:
        between[0]()
    for part in (0, 1):
        first = ordered(part)[0]
        for copy in seconds[part]:
            copy.wait_recv()
        right, left = net.along(first, 1), net.along(first, 3)
        me = net.spot(first)
        sem = sems[part]
        for j, (h, to) in enumerate(((0, right), (1, left), (1, right), (0, left))):
            copies[part].append(push(line(part, me, h), line(part, me, h), sem.at[0, 3 + j], sem.at[1, 3 + j], to))
        cores[part].append(push(whole(part, me), whole(part, me), sem.at[0, 9], sem.at[1, 9], net.core()))
    if between:
        between[1]()
    for part in (0, 1):
        first = ordered(part)[0]
        right, left = net.along(first, 1), net.along(first, 3)
        r, l = net.spot(first, 1), net.spot(first, 3)
        sem = sems[part]
        copies[part][0].wait_recv()
        copies[part].append(push(line(part, l, 0), line(part, l, 0), sem.at[0, 7], sem.at[1, 7], right))
        copies[part][1].wait_recv()
        copies[part].append(push(line(part, r, 1), line(part, r, 1), sem.at[0, 8], sem.at[1, 8], left))
        cores[part].append(push(line(part, l, 0), line(part, l, 0), sem.at[0, 10], sem.at[1, 10], net.core()))
        cores[part].append(push(line(part, r, 1), line(part, r, 1), sem.at[0, 11], sem.at[1, 11], net.core()))
    for part in (0, 1):
        first = ordered(part)[0]
        r, l, far = net.spot(first, 1), net.spot(first, 3), net.spot(first, 2)
        sem = sems[part]
        for k, i, h in ((2, l, 1), (3, r, 0), (4, far, 0), (5, far, 1)):
            copies[part][k].wait_recv()
            cores[part].append(push(line(part, i, h), line(part, i, h), sem.at[0, 10 + k], sem.at[1, 10 + k], net.core()))
    for part in (0, 1):
        for copy in cores[part]:
            copy.wait_recv()
        for copy in seconds[part] + copies[part] + cores[part]:
            copy.wait_send()


def spread_line(net, fulls, outs, sems):
    for part in (0, 1):
        @pl.when(net.z != 7)
        def _():
            dst = fulls[part].at[net.spot("x"), net.spot("y"), net.c, net.z]
            dst[...] = outs[part][...]
            for d in (4, 3, 5, 2, 6, 1, 7):
                push(dst, dst, sems[part].at[0, d - 1], sems[part].at[1, d - 1], net.along("z", d))


def wait_line(net, fulls, sems, recv):
    for part in (0, 1):
        for d in range(1, 8):
            z = net.z if not recv else (net.z + 8 - d) % 8
            block = fulls[part].at[net.spot("x"), net.spot("y"), net.c, jnp.minimum(z, 6)]

            @pl.when(z != 7)
            def _():
                copy = pltpu.make_async_remote_copy(
                    src_ref=block, dst_ref=block, send_sem=sems[part].at[0, d - 1], recv_sem=sems[part].at[1, d - 1],
                    device_id=net.along("z", d), device_id_type=MESH,
                )
                if recv:
                    copy.wait_recv()
                else:
                    copy.wait_send()


def share_owned(net, outs, owned, sems, pairs):
    half = net.x % 2
    partner = device(net.x + 1 - 2 * half, net.y, net.z, net.c)

    def block(part, z):
        return owned[part].at[half, jnp.minimum(z, 6)]

    def line_copy(part, d, z):
        return pltpu.make_async_remote_copy(
            src_ref=block(part, z), dst_ref=block(part, z), send_sem=sems[part].at[0, d - 1],
            recv_sem=sems[part].at[1, d - 1], device_id=net.along("z", d), device_id_type=MESH,
        )

    def pair_copy(part, d, z):
        return pltpu.make_async_remote_copy(
            src_ref=block(part, z), dst_ref=block(part, z), send_sem=pairs[part].at[0, d],
            recv_sem=pairs[part].at[1, d], device_id=partner, device_id_type=MESH,
        )

    for part in (0, 1):
        @pl.when(net.z != 7)
        def _():
            owned[part][half, net.z] = outs[part][...]
            for d in (4, 3, 5, 2, 6, 1, 7):
                line_copy(part, d, net.z).start()
            pair_copy(part, 0, net.z).start()
    for d in (1, 7, 2, 6, 3, 5, 4):
        z = (net.z + 8 - d) % 8

        @pl.when(z != 7)
        def _():
            for part in (0, 1):
                line_copy(part, d, z).wait_recv()
                pair_copy(part, d, z).start()
    for d in range(8):
        z = (net.z + 8 - d) % 8

        @pl.when(z != 7)
        def _():
            for part in (0, 1):
                pair_copy(part, d, z).wait()
    for part in (0, 1):
        @pl.when(net.z != 7)
        def _():
            for d in range(1, 8):
                line_copy(part, d, net.z).wait_send()


def loop(count, body):
    def step(i, carry):
        body(i)
        return carry

    lax.fori_loop(0, count, step, 0)


STARTS = (0, WIDTHS[0])


def norm_patches(patches, normed, normed_t):
    def norm(i):
        at = pl.ds(pl.multiple_of(i * 32, 32), 32)
        rows = patches[at, :].astype(F32)
        centred = rows - jnp.mean(rows, axis=-1, keepdims=True)
        scale = lax.rsqrt(jnp.mean(centred * centred, axis=-1, keepdims=True) + 1e-06)
        normed[at, :] = (centred * scale).astype(BF)

    loop(8, norm)

    def turn(j):
        block = normed[:, pl.ds(pl.multiple_of(j * 128, 128), 128)]
        normed_t[pl.ds(j * 8, 8)] = block.T.reshape(8, 16, SEQ)

    loop(14, turn)


def attend(queries, keys, attention, attention_t):
    for h in range(HEADS):
        q = queries[:, h * HD:(h + 1) * HD]
        k = keys[:, h * HD:(h + 1) * HD]
        scores = lax.dot_general(q, k, (((1,), (1,)), ((), ())), preferred_element_type=F32) * HD ** (-0.5)
        expo = jnp.exp(scores - jnp.max(scores, axis=-1, keepdims=True))
        weights = (expo / jnp.sum(expo, axis=-1, keepdims=True)).astype(BF)
        attention[h] = weights
        attention_t[h] = weights.T


def project(normed, fulls, write):
    for part in (0, 1):
        w, at = WIDTHS[part], STARTS[part]
        total = jnp.dot(normed[:, :HID], fulls[part][0].reshape(HID, w), preferred_element_type=F32)
        total = total + jnp.dot(normed[:, HID:], fulls[part][1].reshape(HID, w), preferred_element_type=F32)
        write(slice(at, at + w), total)


def unfold(full, i):
    both = full[2 + i // 4, i % 4].astype(F32)
    both = both.reshape(2, 112, both.shape[-1])
    left = jnp.concatenate([both[0, :56], both[1, :56]], axis=0)
    right = jnp.concatenate([both[0, 56:], both[1, 56:]], axis=0)
    return left, right


def set_output(fulls, output, stretch):
    def step(i):
        for part in (0, 1):
            w = WIDTHS[part]
            for half, rows in enumerate(unfold(fulls[part], i)):
                at = (pl.ds(i * BLOCKS, BLOCKS), slice(None), slice(half * HID + STARTS[part], half * HID + STARTS[part] + w))
                if stretch is not None:
                    rows = output[at].astype(F32).reshape(112, w) + stretch * rows
                output[at] = rows.astype(BF).reshape(BLOCKS, 16, w)

    loop(8, step)


def sum_squares(fulls):
    def step(i, totals):
        out = []
        for part in (0, 1):
            block = fulls[part][i // 4, i % 4].astype(F32)
            block = block.reshape(2 * BLOCKS, 16, WIDTHS[part])
            out.append(totals[part] + jnp.sum(block * block, axis=0))
        return tuple(out)

    totals = lax.fori_loop(0, 16, step, tuple(jnp.zeros((16, w), F32) for w in WIDTHS))
    parts = [jnp.sum(jnp.sum(t, axis=0, keepdims=True), axis=1, keepdims=True) for t in totals]
    return parts[0] + parts[1]


def backward(patches, upstream, attention, attention_t, output, values, mixed, mixed_t, outcome, d_outcome, d_values):
    for h in range(HEADS):
        at = slice(h * HD, (h + 1) * HD)
        mixed[:, at] = jnp.dot(attention[h], values[:, at], preferred_element_type=F32).astype(BF)

    def turn(j):
        block = mixed[:, pl.ds(pl.multiple_of(j * 128, 128), 128)].astype(F32)
        mixed_t[pl.ds(j * 16, 16)] = block.T.reshape(16, 8, SEQ)

    loop(7, turn)

    def columns(n):
        at = pl.ds(pl.multiple_of(n * 256, 256), 256)
        outcome[:, at] = patches[:, at].astype(F32) + jnp.dot(
            mixed[...], output[:, :, at].reshape(HID, 256), preferred_element_type=F32
        )

    loop(7, columns)

    def rows(i):
        at = pl.ds(pl.multiple_of(i * 32, 32), 32)
        total = outcome[at, :]
        centred = total - jnp.mean(total, axis=-1, keepdims=True)
        inverse = lax.rsqrt(jnp.mean(centred * centred, axis=-1, keepdims=True) + 1e-06)
        normal = centred * inverse
        signal = upstream[at, :].astype(F32)
        grad = inverse * (
            signal
            - jnp.mean(signal, axis=-1, keepdims=True)
            - normal * jnp.mean(signal * normal, axis=-1, keepdims=True)
        )
        d_outcome[at, :] = grad.astype(BF)

    loop(8, rows)
    d_mixed = lax.dot_general(
        d_outcome[...], output[...].reshape(HID, D), (((1,), (1,)), ((), ())), preferred_element_type=F32
    ).astype(BF)
    values[...] = d_mixed
    for h in range(HEADS):
        at = slice(h * HD, (h + 1) * HD)
        d_values[:, at] = jnp.dot(attention_t[h], values[:, at], preferred_element_type=F32).astype(BF)


def write_grads(core, normed_t, mixed_t, d_outcome, d_values, grads):
    for hi in (0, 1):
        rows = [mixed_t[pl.ds((hi * 8 + y * 2 + core) * BLOCKS, BLOCKS)].reshape(56, SEQ) for y in range(4)]
        left = jnp.concatenate(rows, axis=0).astype(BF)
        got = jnp.dot(left, d_outcome[...], preferred_element_type=F32).reshape(4, 56, D)
        got = jnp.concatenate([got[:, :, :HID], got[:, :, HID:]], axis=1).astype(BF).reshape(4, BLOCKS, 16, HID)
        for part in (0, 1):
            grads[part][2 + hi, :, core] = got[..., STARTS[part]:STARTS[part] + WIDTHS[part]]
    for hi in (0, 1):
        rows = [normed_t[pl.ds((hi * 8 + y * 2 + core) * BLOCKS, BLOCKS)] for y in range(4)]
        left = jnp.concatenate(rows, axis=0).reshape(448, SEQ)
        got = jnp.dot(left, d_values[...], preferred_element_type=F32).astype(BF).reshape(4, BLOCKS, 16, HID)
        for part in (0, 1):
            grads[part][hi, :, core] = got[..., STARTS[part]:STARTS[part] + WIDTHS[part]]


def kernel(
    patches, queries, keys, upstream, own,
    value_grad, output_grad,
    full_a, full_b, grad_a, grad_b, owned_a, owned_b,
    normed, normed_t, attention, attention_t, base, values, output,
    mixed, mixed_t, outcome, d_outcome, d_values,
    sem_a, sem_b, again_a, again_b, out_a, out_b, line_a, line_b, last_a, last_b, pair_a, pair_b, *scratch,
):
    net = Net()
    net.barrier()
    fulls, grads, outs, owned = (full_a, full_b), (grad_a, grad_b), (out_a, out_b), (owned_a, owned_b)
    for part in (0, 1):
        fulls[part][net.spot("x"), net.spot("y"), net.c] = own[net.x % 2, :, :, STARTS[part]:STARTS[part] + WIDTHS[part]]
    gather_all(
        net, fulls, (sem_a, sem_b),
        (lambda: norm_patches(patches, normed, normed_t), lambda: attend(queries, keys, attention, attention_t)),
    )
    set_output(fulls, output, None)

    def write_base(at, total):
        base[:, at] = total
        values[:, at] = total.astype(BF)

    project(normed, fulls, write_base)

    def back():
        backward(patches, upstream, attention, attention_t, output, values, mixed, mixed_t, outcome, d_outcome, d_values)

    def make(core):
        write_grads(core, normed_t, mixed_t, d_outcome, d_values, grads)

    back()
    drain = reduce_all(net, grads, outs, scratch, make)
    spread_line(net, fulls, outs, (line_a, line_b))
    wait_line(net, fulls, (line_a, line_b), True)
    gather_all(net, fulls, (again_a, again_b))
    wait_line(net, fulls, (line_a, line_b), False)
    drain()
    mean_square = sum_squares(fulls) / (2.0 * D * HID)
    stretch = rho_scale / jnp.sqrt(mean_square + 1e-06)
    set_output(fulls, output, stretch)

    def write_values(at, total):
        values[:, at] = (base[:, at] + stretch * total).astype(BF)

    project(normed, fulls, write_values)
    back()
    drain = reduce_all(net, grads, outs, scratch, make)
    share_owned(net, outs, owned, (last_a, last_b), (pair_a, pair_b))
    drain()
    for part in (0, 1):
        w, at = WIDTHS[part], STARTS[part]
        value_grad[:, :, at:at + w] = owned[part][0]
        rows = owned[part][1].astype(F32).reshape(112, w)
        output_grad[:, at:at + w] = rows[:56]
        output_grad[:, HID + at:HID + at + w] = rows[56:]


def vmem(n):
    return [pl.BlockSpec(memory_space=pltpu.VMEM)] * n


def line_sems(n=7):
    return [pltpu.SemaphoreType.DMA((2, n)) for _ in WIDTHS]


def gradients(patches, queries, keys, upstream, own):
    rows = patches.shape[0]
    return pl.pallas_call(
        kernel,
        out_shape=(
            jax.ShapeDtypeStruct((BLOCKS, 16, HID), BF),
            jax.ShapeDtypeStruct((56, D), F32),
        ),
        in_specs=vmem(5),
        out_specs=vmem(2),
        scratch_shapes=(
            [pltpu.VMEM((4, 4, 2, BLOCKS, 16, w), BF) for w in WIDTHS]
            + [pltpu.VMEM((4, 4, 2, BLOCKS, 16, w), BF) for w in WIDTHS]
            + [pltpu.VMEM((2, BLOCKS, 16, w), BF) for w in WIDTHS]
            + [
                pltpu.VMEM((rows, D), BF),
                pltpu.VMEM((112, 16, rows), BF),
                pltpu.VMEM((HEADS, SEQ, SEQ), BF),
                pltpu.VMEM((HEADS, SEQ, SEQ), BF),
                pltpu.VMEM((rows, HID), F32),
                pltpu.VMEM((rows, HID), BF),
                pltpu.VMEM((56, 16, D), BF),
                pltpu.VMEM((rows, HID), BF),
                pltpu.VMEM((112, 8, rows), F32),
                pltpu.VMEM((rows, D), F32),
                pltpu.VMEM((rows, D), BF),
                pltpu.VMEM((rows, HID), BF),
            ]
            + gather_scratch() + gather_scratch()
            + [pltpu.VMEM((16, w), BF) for w in WIDTHS]
            + line_sems() + line_sems() + line_sems(8)
            + reduce_scratch()
        ),
        name="gradients",
        compiler_params=pltpu.CompilerParams(
            collective_id=0, has_side_effects=True, vmem_limit_bytes=60 * 2**20
        ),
    )(patches, queries, keys, upstream, own)


def fold_output(rows):
    half = rows.reshape(56, 2, HID)
    return jnp.swapaxes(half, 0, 1).reshape(BLOCKS, 16, HID)


def adam_update(weight, first, second, gradient):
    first_new = beta_one * first + (1.0 - beta_one) * gradient
    second_new = beta_two * second + (1.0 - beta_two) * gradient * gradient
    update = (
        first_new / first_fix / (jnp.sqrt(second_new / second_fix) + adam_eps)
        + weight_decay * weight
    )
    return (weight - learn_rate * update, first_new, second_new)


def on_device(
    patches,
    queries,
    keys,
    upstream,
    value_weight,
    output_weight,
    value_first,
    output_first,
    value_second,
    output_second,
):
    own = jnp.stack([
        value_weight.astype(BF).reshape(BLOCKS, 16, HID),
        fold_output(output_weight.astype(BF)),
    ])
    value_grad, output_grad = gradients(patches, queries, keys, upstream, own)
    value_new, value_first_new, value_second_new = adam_update(
        value_weight, value_first, value_second, value_grad.reshape(112, HID).astype(F32)
    )
    output_new, output_first_new, output_second_new = adam_update(
        output_weight, output_first, output_second, output_grad
    )
    return (
        value_new,
        output_new,
        value_first_new,
        output_first_new,
        value_second_new,
        output_second_new,
    )


def solution(mesh):
    return jax.shard_map(
        on_device,
        mesh=mesh,
        in_specs=(P(("dp", "fsdp"), None),) * 4 + (P("fsdp", None),) * 6,
        out_specs=(P("fsdp", None),) * 6,
        check_vma=False,
    )
```

```python
import jax
import jax.numpy as jnp
from jax import lax
from jax.experimental import pallas as pl
from jax.experimental.pallas import tpu as pltpu
from jax.sharding import PartitionSpec as P

HEADS = 8
HD = 112
SEQ = 256
D = 1792
HID = 896
BLOCKS = 7
WIDTHS = (384, 384, 128)
PARTS = (0, 1, 2)
MESH = pl.DeviceIdType.MESH
BF = jnp.bfloat16
F32 = jnp.float32


learn_rate = 0.001
weight_decay = 0.1
beta_one = 0.9
beta_two = 0.999
adam_eps = 1e-08
first_fix = 0.9999734386011124
second_fix = 0.0952078528862911
rho_scale = 0.05


def place():
    dp = lax.axis_index("dp")
    fs = lax.axis_index("fsdp")
    return (fs // 8) * 2 + dp // 8, (fs // 2) % 4, dp % 8, fs % 2


def device(x, y, z, c):
    return ((x % 2) * 8 + z, (x // 2) * 8 + y * 2 + c)


def slot(x):
    return (x % 2) * 2 + x // 2


class Net:
    def __init__(self):
        self.x, self.y, self.z, self.c = place()

    def core(self):
        return device(self.x, self.y, self.z, 1 - self.c)

    def along(self, axis, step):
        if axis == "x":
            return device((self.x + step) % 4, self.y, self.z, self.c)
        if axis == "y":
            return device(self.x, (self.y + step) % 4, self.z, self.c)
        return device(self.x, self.y, (self.z + step) % 8, self.c)

    def across(self, i, j):
        return device((self.x + i) % 4, (self.y + j) % 4, self.z, self.c)

    def spot(self, axis, step=0):
        if axis == "x":
            return slot((self.x + step) % 4)
        if axis == "y":
            return (self.y + step) % 4
        return (self.z + step) % 8

    def barrier(self):
        sem = pltpu.get_barrier_semaphore()
        targets = [self.core()]
        targets += [self.along("x", s) for s in (1, 2, 3)]
        targets += [self.along("y", s) for s in (1, 2, 3)]
        targets += [self.along("z", s) for s in range(1, 8)]
        targets += [self.across(i, j) for i in (1, 2, 3) for j in (1, 2, 3)]
        for t in targets:
            pl.semaphore_signal(sem, inc=1, device_id=t, device_id_type=MESH)
        pl.semaphore_wait(sem, len(targets))


def push(src, dst, send, recv, target):
    copy = pltpu.make_async_remote_copy(
        src_ref=src, dst_ref=dst, send_sem=send, recv_sem=recv, device_id=target, device_id_type=MESH
    )
    copy.start()
    return copy


def add_blocks(count, write, *reads):
    def step(i, carry):
        total = reads[0](i).astype(F32)
        for read in reads[1:]:
            total = total + read(i).astype(F32)
        write(i, total.astype(BF))
        return carry

    lax.fori_loop(0, count, step, 0)


def ordered(part):
    return ("x", "y") if part == 0 else ("y", "x")


def grid_at(ref, part, first, second):
    return ref.at[first, second] if part == 0 else ref.at[second, first]


def reduce_scratch():
    shapes = []
    for w in WIDTHS[:2]:
        shapes += [
            pltpu.VMEM((4, 4, BLOCKS, 16, w), BF),
            pltpu.VMEM((4, 4, BLOCKS, 16, w), BF),
            pltpu.VMEM((2, 2, BLOCKS, 16, w), BF),
            pltpu.VMEM((2, 4, BLOCKS, 16, w), BF),
            pltpu.VMEM((4, BLOCKS, 16, w), BF),
            pltpu.VMEM((3, BLOCKS, 16, w), BF),
            pltpu.VMEM((BLOCKS, 16, w), BF),
            pltpu.VMEM((7, 16, w), BF),
            pltpu.SemaphoreType.DMA((2, 4 + 2 + 4 + 3 + 7)),
        ]
    w = WIDTHS[2]
    return shapes + [
        pltpu.VMEM((4, 4, BLOCKS, 16, w), BF),
        pltpu.VMEM((4, 4, BLOCKS, 16, w), BF),
        pltpu.VMEM((2, 2, 4, 16, w), BF),
        pltpu.VMEM((2, 3, 4, 4, 16, w), BF),
        pltpu.VMEM((4, 4, 16, w), BF),
        pltpu.VMEM((15, 16, w), BF),
        pltpu.SemaphoreType.DMA((2, 1 + 8 + 15)),
    ]


ACROSS = [(i, j) for i in range(4) for j in range(4) if (i, j) != (0, 0)]


class LineFirst:
    def __init__(self, net, grads, out, scratch):
        self.net, self.grads, self.out = net, grads, out
        self.other, self.sums, self.far, self.ring, self.plane, self.from_plane, self.sem = scratch

    def exchange(self):
        net = self.net
        self.core = push(self.grads.at[:, :, 1 - net.c], self.other, self.sem.at[0, 0], self.sem.at[1, 0], net.core())

    def add_cores(self):
        net = self.net
        self.core.wait_recv()
        g, other, sums = self.grads, self.other, self.sums

        def write(i, v):
            sums[i // 4, i % 4] = v

        add_blocks(16, write, lambda i: g[i // 4, i % 4, net.c], lambda i: other[i // 4, i % 4])

    def copy(self, k, way, j):
        j = jnp.minimum(j, 6)
        if k == 0:
            src, dst = self.sums.at[pl.ds(2 * way, 2), :, j], self.far.at[way]
        else:
            src, dst = self.sums.at[:, :, j], self.ring.at[way, k - 1]
        at = 1 + 2 * k + way
        return pltpu.make_async_remote_copy(
            src_ref=src, dst_ref=dst, send_sem=self.sem.at[0, at], recv_sem=self.sem.at[1, at],
            device_id=self.net.along("z", (1, 7)[way]), device_id_type=MESH,
        )

    def sent(self, k, way):
        return (self.net.z + ((4 - k) if way == 0 else (4 + k))) % 8

    def got(self, k, way):
        return (self.net.z + ((3 - k) if way == 0 else (5 + k))) % 8

    def send(self, k):
        for way in (0, 1):
            j = self.sent(k, way)

            @pl.when(j != 7)
            def _():
                self.copy(k, way, j).start()

    def receive(self, k):
        for way in (0, 1):
            j = self.got(k, way)
            at = jnp.minimum(j, 6)

            @pl.when(j != 7)
            def _():
                self.copy(k, way, j).wait_recv()
                if k == 0:
                    rows = slice(2 * way, 2 * way + 2)
                    self.sums[rows, :, at] = (self.sums[rows, :, at].astype(F32) + self.far[way].astype(F32)).astype(BF)
                elif k < 3:
                    self.sums[:, :, at] = (self.sums[:, :, at].astype(F32) + self.ring[way, k - 1].astype(F32)).astype(BF)

    def plane_copy(self, e):
        i, j = ACROSS[e]
        net = self.net
        return pltpu.make_async_remote_copy(
            src_ref=self.plane.at[net.spot("x", i), net.spot("y", j)], dst_ref=self.from_plane.at[e],
            send_sem=self.sem.at[0, 9 + e], recv_sem=self.sem.at[1, 9 + e], device_id=net.across(i, j), device_id_type=MESH,
        )

    def cross(self):
        net = self.net

        @pl.when(net.z != 7)
        def _():
            self.plane[...] = (
                self.sums[:, :, net.z].astype(F32) + self.ring[0, 2].astype(F32) + self.ring[1, 2].astype(F32)
            ).astype(BF)
            for e in range(15):
                self.plane_copy(e).start()

    def finish(self):
        net = self.net

        @pl.when(net.z != 7)
        def _():
            for e in range(15):
                self.plane_copy(e).wait_recv()
            total = self.plane[net.spot("x"), net.spot("y")].astype(F32)
            for e in range(15):
                total = total + self.from_plane[e].astype(F32)
            self.out[...] = total.astype(BF)

    def drain(self):
        self.core.wait_send()
        for k in range(4):
            for way in (0, 1):
                j = self.sent(k, way)

                @pl.when(j != 7)
                def _():
                    self.copy(k, way, j).wait_send()

        @pl.when(self.net.z != 7)
        def _():
            for e in range(15):
                self.plane_copy(e).wait_send()


def reduce_all(net, grads, outs, scratch, make):
    make(1 - net.c)
    ring = LineFirst(net, grads[2], outs[2], scratch[18:])
    ring.exchange()
    state = []
    for part in (0, 1):
        state.append(scratch[part * 9:part * 9 + 9])
    cores = [[], []]
    for step in (2, 1, 3, 0):
        for part in (0, 1):
            other, sums, far, mine, _, _, _, _, sem = state[part]
            first = ordered(part)[0]
            i = net.spot(first, step)
            j = len(cores[part])
            if part == 0:
                src, dst = grads[part].at[i, :, 1 - net.c], other.at[i]
            else:
                src, dst = grads[part].at[:, i, 1 - net.c], other.at[:, i]
            cores[part].append(push(src, dst, sem.at[0, j], sem.at[1, j], net.core()))
    make(net.c)
    ring.add_cores()
    ring.send(0)

    def half_of(ref, part, i, h):
        return ref.at[i, pl.ds(2 * h, 2)] if part == 0 else ref.at[pl.ds(2 * h, 2), i]

    near = [[None] * 6, [None] * 6]
    for j, step in enumerate((2, 1, 3, 0)):
        for part in (0, 1):
            other, sums, far, mine, _, _, _, _, sem = state[part]
            first = ordered(part)[0]
            i = net.spot(first, step)
            cores[part][j].wait_recv()
            g = grads[part]
            if part == 0:
                def write(k, v):
                    sums[i, k] = v
                add_blocks(4, write, lambda k: g[i, k, net.c], lambda k: other[i, k])
            else:
                def write(k, v):
                    sums[k, i] = v
                add_blocks(4, write, lambda k: g[k, i, net.c], lambda k: other[k, i])
            right, left = net.along(first, 1), net.along(first, 3)
            if step == 2:
                near[part][0] = push(half_of(sums, part, i, 0), far.at[0], sem.at[0, 4], sem.at[1, 4], right)
                near[part][1] = push(half_of(sums, part, i, 1), far.at[1], sem.at[0, 5], sem.at[1, 5], left)
            if step == 1:
                near[part][2] = push(half_of(sums, part, i, 1), mine.at[0, pl.ds(2, 2)], sem.at[0, 6], sem.at[1, 6], right)
            if step == 3:
                near[part][3] = push(half_of(sums, part, i, 0), mine.at[1, pl.ds(0, 2)], sem.at[0, 7], sem.at[1, 7], left)
        if j < 2:
            ring.receive(j)
            ring.send(j + 1)
    for part in (0, 1):
        other, sums, far, mine, _, _, _, _, sem = state[part]
        first = ordered(part)[0]
        right, left = net.along(first, 1), net.along(first, 3)
        r, l = net.spot(first, 1), net.spot(first, 3)
        near[part][0].wait_recv()
        if part == 0:
            def write(k, v):
                sums[r, k] = v
            add_blocks(2, write, lambda k: sums[r, k], lambda k: far[0, k])
        else:
            def write(k, v):
                sums[k, r] = v
            add_blocks(2, write, lambda k: sums[k, r], lambda k: far[0, k])
        near[part][4] = push(half_of(sums, part, r, 0), mine.at[0, pl.ds(0, 2)], sem.at[0, 8], sem.at[1, 8], right)
        near[part][1].wait_recv()
        if part == 0:
            def write(k, v):
                sums[l, k + 2] = v
            add_blocks(2, write, lambda k: sums[l, k + 2], lambda k: far[1, k])
        else:
            def write(k, v):
                sums[k + 2, l] = v
            add_blocks(2, write, lambda k: sums[k + 2, l], lambda k: far[1, k])
        near[part][5] = push(half_of(sums, part, l, 1), mine.at[1, pl.ds(2, 2)], sem.at[0, 9], sem.at[1, 9], left)
    ring.receive(2)
    ring.send(3)
    second_copies = [[], []]
    for part in (0, 1):
        other, sums, far, mine, row, from_row, _, _, sem = state[part]
        first, second = ordered(part)
        me = net.spot(first)
        for k in (2, 3, 4, 5):
            near[part][k].wait_recv()

        def write(k, v):
            row[k] = v
        if part == 0:
            add_blocks(4, write, lambda k: sums[me, k], lambda k: mine[0, k], lambda k: mine[1, k])
        else:
            add_blocks(4, write, lambda k: sums[k, me], lambda k: mine[0, k], lambda k: mine[1, k])
        for d in (2, 1, 3):
            second_copies[part].append(
                push(row.at[net.spot(second, d)], from_row.at[d - 1], sem.at[0, 9 + d], sem.at[1, 9 + d], net.along(second, d))
            )
    ring.receive(3)
    ring.cross()
    for part in (0, 1):
        other, sums, far, mine, row, from_row, line, from_line, sem = state[part]
        second = ordered(part)[1]
        me = net.spot(second)
        for copy in second_copies[part]:
            copy.wait_recv()

        def write(k, v):
            line[k] = v
        add_blocks(BLOCKS, write, lambda k: row[me, k], lambda k: from_row[0, k], lambda k: from_row[1, k], lambda k: from_row[2, k])
        for d in (4, 3, 5, 2, 6, 1, 7):
            z = net.spot("z", d)

            @pl.when(z != 7)
            def _():
                push(line.at[z], from_line.at[d - 1], sem.at[0, 12 + d], sem.at[1, 12 + d], net.along("z", d))
    ring.finish()
    for part in (0, 1):
        other, sums, far, mine, row, from_row, line, from_line, sem = state[part]

        @pl.when(net.z != 7)
        def _():
            for d in range(1, 8):
                pltpu.make_async_remote_copy(
                    src_ref=line.at[0], dst_ref=from_line.at[d - 1], send_sem=sem.at[0, 12 + d], recv_sem=sem.at[1, 12 + d],
                    device_id=net.along("z", d), device_id_type=MESH,
                ).wait_recv()
            total = line[net.z].astype(F32)
            for d in range(7):
                total = total + from_line[d].astype(F32)
            outs[part][...] = total.astype(BF)

    def drain():
        ring.drain()
        for part in (0, 1):
            other, sums, far, mine, row, from_row, line, from_line, sem = state[part]
            for copy in cores[part] + near[part] + second_copies[part]:
                copy.wait_send()
            for d in range(1, 8):
                @pl.when(net.spot("z", d) != 7)
                def _():
                    pltpu.make_async_remote_copy(
                        src_ref=line.at[0], dst_ref=from_line.at[d - 1], send_sem=sem.at[0, 12 + d], recv_sem=sem.at[1, 12 + d],
                        device_id=net.along("z", d), device_id_type=MESH,
                    ).wait_send()
    return drain


def gather_scratch():
    return [pltpu.SemaphoreType.DMA((2, 3 + 6 + 8)) for _ in WIDTHS[:2]] + [pltpu.SemaphoreType.DMA((2, 15 + 8 + 9))]


class LineLast:
    def __init__(self, net, full, sem):
        self.net, self.full, self.sem = net, full, sem

    def own(self, e):
        i, j = ACROSS[e]
        net = self.net
        block = self.full.at[net.spot("x"), net.spot("y"), net.c, jnp.minimum(net.z, 6)]
        return pltpu.make_async_remote_copy(
            src_ref=block, dst_ref=block, send_sem=self.sem.at[0, e], recv_sem=self.sem.at[1, e],
            device_id=net.across(i, j), device_id_type=MESH,
        )

    def start(self):
        @pl.when(self.net.z != 7)
        def _():
            for e in range(15):
                self.own(e).start()

    def block(self, j, k, way):
        j = jnp.minimum(j, 6)
        if k == 4:
            return self.full.at[pl.ds(2 * way, 2), :, self.net.c, j]
        return self.full.at[:, :, self.net.c, j]

    def copy(self, k, way, j):
        at = 15 + 2 * (k - 1) + way
        block = self.block(j, k, way)
        return pltpu.make_async_remote_copy(
            src_ref=block, dst_ref=block, send_sem=self.sem.at[0, at], recv_sem=self.sem.at[1, at],
            device_id=self.net.along("z", (1, 7)[way]), device_id_type=MESH,
        )

    def core(self, k, way, j):
        at = 23 if k == 0 else 24 + 2 * (k - 1) + way
        block = self.block(j, k, way)
        return pltpu.make_async_remote_copy(
            src_ref=block, dst_ref=block, send_sem=self.sem.at[0, at], recv_sem=self.sem.at[1, at],
            device_id=self.net.core(), device_id_type=MESH,
        )

    def sent(self, k, way):
        return (self.net.z + ((9 - k) if way == 0 else (k - 1))) % 8

    def got(self, k, way):
        return (self.net.z + ((8 - k) if way == 0 else k)) % 8

    def send(self, k):
        for way in (0, 1):
            j = self.sent(k, way)

            @pl.when(j != 7)
            def _():
                self.copy(k, way, j).start()

    def first(self):
        net = self.net

        @pl.when(net.z != 7)
        def _():
            for e in range(15):
                self.own(e).wait_recv()
            self.core(0, 0, net.z).start()

        self.send(1)

    def step(self, k):
        for way in (0, 1):
            j = self.got(k, way)

            @pl.when(j != 7)
            def _():
                self.copy(k, way, j).wait_recv()
                self.core(k, way, j).start()

        if k < 4:
            self.send(k + 1)

    def finish(self):
        net = self.net

        @pl.when(net.z != 7)
        def _():
            self.core(0, 0, net.z).wait()
            for e in range(15):
                self.own(e).wait_send()

        for k in (1, 2, 3, 4):
            for way in (0, 1):
                j = self.got(k, way)

                @pl.when(j != 7)
                def _():
                    self.core(k, way, j).wait()

                i = self.sent(k, way)

                @pl.when(i != 7)
                def _():
                    self.copy(k, way, i).wait_send()


def gather_all(net, fulls, sems, ring, between=()):
    between = list(between) + [lambda: None] * 4
    seconds = [[], []]
    for part in (0, 1):
        second = ordered(part)[1]
        own = fulls[part].at[net.spot("x"), net.spot("y"), net.c]
        for d in (2, 1, 3):
            seconds[part].append(push(own, own, sems[part].at[0, d - 1], sems[part].at[1, d - 1], net.along(second, d)))

    def line(part, i, h):
        ref = fulls[part]
        return ref.at[i, pl.ds(2 * h, 2), net.c] if part == 0 else ref.at[pl.ds(2 * h, 2), i, net.c]

    def whole(part, i):
        ref = fulls[part]
        return ref.at[i, :, net.c] if part == 0 else ref.at[:, i, net.c]

    copies = [[], []]
    cores = [[], []]
    between[0]()
    ring.first()
    for part in (0, 1):
        first = ordered(part)[0]
        for copy in seconds[part]:
            copy.wait_recv()
        right, left = net.along(first, 1), net.along(first, 3)
        me = net.spot(first)
        sem = sems[part]
        for j, (h, to) in enumerate(((0, right), (1, left), (1, right), (0, left))):
            copies[part].append(push(line(part, me, h), line(part, me, h), sem.at[0, 3 + j], sem.at[1, 3 + j], to))
        cores[part].append(push(whole(part, me), whole(part, me), sem.at[0, 9], sem.at[1, 9], net.core()))
    between[1]()
    ring.step(1)
    between[2]()
    ring.step(2)
    for part in (0, 1):
        first = ordered(part)[0]
        right, left = net.along(first, 1), net.along(first, 3)
        r, l = net.spot(first, 1), net.spot(first, 3)
        sem = sems[part]
        copies[part][0].wait_recv()
        copies[part].append(push(line(part, l, 0), line(part, l, 0), sem.at[0, 7], sem.at[1, 7], right))
        copies[part][1].wait_recv()
        copies[part].append(push(line(part, r, 1), line(part, r, 1), sem.at[0, 8], sem.at[1, 8], left))
        cores[part].append(push(line(part, l, 0), line(part, l, 0), sem.at[0, 10], sem.at[1, 10], net.core()))
        cores[part].append(push(line(part, r, 1), line(part, r, 1), sem.at[0, 11], sem.at[1, 11], net.core()))
    between[3]()
    ring.step(3)
    for k in (2, 3, 4, 5):
        if k == 4:
            ring.step(4)
        for part in (0, 1):
            first = ordered(part)[0]
            r, l, far = net.spot(first, 1), net.spot(first, 3), net.spot(first, 2)
            sem = sems[part]
            i, h = ((l, 1), (r, 0), (far, 0), (far, 1))[k - 2]
            copies[part][k].wait_recv()
            cores[part].append(push(line(part, i, h), line(part, i, h), sem.at[0, 10 + k], sem.at[1, 10 + k], net.core()))
    for part in (0, 1):
        for copy in cores[part]:
            copy.wait_recv()
        for copy in seconds[part] + copies[part] + cores[part]:
            copy.wait_send()
    ring.finish()


def spread_line(net, fulls, outs, sems):
    for part in (0, 1):
        @pl.when(net.z != 7)
        def _():
            dst = fulls[part].at[net.spot("x"), net.spot("y"), net.c, net.z]
            dst[...] = outs[part][...]
            for d in (4, 3, 5, 2, 6, 1, 7):
                push(dst, dst, sems[part].at[0, d - 1], sems[part].at[1, d - 1], net.along("z", d))


def wait_line(net, fulls, sems, recv):
    for part in (0, 1):
        for d in range(1, 8):
            z = net.z if not recv else (net.z + 8 - d) % 8
            block = fulls[part].at[net.spot("x"), net.spot("y"), net.c, jnp.minimum(z, 6)]

            @pl.when(z != 7)
            def _():
                copy = pltpu.make_async_remote_copy(
                    src_ref=block, dst_ref=block, send_sem=sems[part].at[0, d - 1], recv_sem=sems[part].at[1, d - 1],
                    device_id=net.along("z", d), device_id_type=MESH,
                )
                if recv:
                    copy.wait_recv()
                else:
                    copy.wait_send()


def share_owned(net, outs, owned, sems, pairs):
    half = net.x % 2
    partner = device(net.x + 1 - 2 * half, net.y, net.z, net.c)

    def block(part, z):
        return owned[part].at[half, jnp.minimum(z, 6)]

    def line_copy(part, d, z):
        return pltpu.make_async_remote_copy(
            src_ref=block(part, z), dst_ref=block(part, z), send_sem=sems[part].at[0, d - 1],
            recv_sem=sems[part].at[1, d - 1], device_id=net.along("z", d), device_id_type=MESH,
        )

    def pair_copy(part, d, z):
        return pltpu.make_async_remote_copy(
            src_ref=block(part, z), dst_ref=block(part, z), send_sem=pairs[part].at[0, d],
            recv_sem=pairs[part].at[1, d], device_id=partner, device_id_type=MESH,
        )

    for part in PARTS:
        @pl.when(net.z != 7)
        def _():
            owned[part][half, net.z] = outs[part][...]
            for d in (4, 3, 5, 2, 6, 1, 7):
                line_copy(part, d, net.z).start()
            pair_copy(part, 0, net.z).start()
    for d in (1, 7, 2, 6, 3, 5, 4):
        z = (net.z + 8 - d) % 8

        @pl.when(z != 7)
        def _():
            for part in PARTS:
                line_copy(part, d, z).wait_recv()
                pair_copy(part, d, z).start()
    for d in range(8):
        z = (net.z + 8 - d) % 8

        @pl.when(z != 7)
        def _():
            for part in PARTS:
                pair_copy(part, d, z).wait()
    for part in PARTS:
        @pl.when(net.z != 7)
        def _():
            for d in range(1, 8):
                line_copy(part, d, net.z).wait_send()


def loop(count, body):
    def step(i, carry):
        body(i)
        return carry

    lax.fori_loop(0, count, step, 0)


STARTS = (0, WIDTHS[0], WIDTHS[0] + WIDTHS[1])


def norm_patches(patches, normed, normed_t):
    def norm(i):
        at = pl.ds(pl.multiple_of(i * 32, 32), 32)
        rows = patches[at, :].astype(F32)
        centred = rows - jnp.mean(rows, axis=-1, keepdims=True)
        scale = lax.rsqrt(jnp.mean(centred * centred, axis=-1, keepdims=True) + 1e-06)
        normed[at, :] = (centred * scale).astype(BF)

    loop(8, norm)

    def turn(j):
        block = normed[:, pl.ds(pl.multiple_of(j * 128, 128), 128)]
        normed_t[pl.ds(j * 8, 8)] = block.T.reshape(8, 16, SEQ)

    loop(14, turn)


def attend(queries, keys, attention, attention_t, heads):
    for h in heads:
        q = queries[:, h * HD:(h + 1) * HD]
        k = keys[:, h * HD:(h + 1) * HD]
        scores = lax.dot_general(q, k, (((1,), (1,)), ((), ())), preferred_element_type=F32) * HD ** (-0.5)
        expo = jnp.exp(scores - jnp.max(scores, axis=-1, keepdims=True))
        weights = (expo / jnp.sum(expo, axis=-1, keepdims=True)).astype(BF)
        attention[h] = weights
        attention_t[h] = weights.T


def project(normed, fulls, write):
    for part in PARTS:
        w, at = WIDTHS[part], STARTS[part]
        total = jnp.dot(normed[:, :HID], fulls[part][0].reshape(HID, w), preferred_element_type=F32)
        total = total + jnp.dot(normed[:, HID:], fulls[part][1].reshape(HID, w), preferred_element_type=F32)
        write(slice(at, at + w), total)


def unfold(full, i):
    both = full[2 + i // 4, i % 4].astype(F32)
    both = both.reshape(2, 112, both.shape[-1])
    left = jnp.concatenate([both[0, :56], both[1, :56]], axis=0)
    right = jnp.concatenate([both[0, 56:], both[1, 56:]], axis=0)
    return left, right


def set_output(fulls, output, stretch):
    def step(i):
        for part in PARTS:
            w = WIDTHS[part]
            for half, rows in enumerate(unfold(fulls[part], i)):
                at = (pl.ds(i * BLOCKS, BLOCKS), slice(None), slice(half * HID + STARTS[part], half * HID + STARTS[part] + w))
                if stretch is not None:
                    rows = output[at].astype(F32).reshape(112, w) + stretch * rows
                output[at] = rows.astype(BF).reshape(BLOCKS, 16, w)

    loop(8, step)


def sum_squares(fulls):
    def step(i, totals):
        out = []
        for part in PARTS:
            block = fulls[part][i // 4, i % 4].astype(F32)
            block = block.reshape(2 * BLOCKS, 16, WIDTHS[part])
            out.append(totals[part] + jnp.sum(block * block, axis=0))
        return tuple(out)

    totals = lax.fori_loop(0, 16, step, tuple(jnp.zeros((16, w), F32) for w in WIDTHS))
    parts = [jnp.sum(jnp.sum(t, axis=0, keepdims=True), axis=1, keepdims=True) for t in totals]
    return parts[0] + parts[1] + parts[2]


def backward(patches, upstream, attention, attention_t, output, values, mixed, mixed_t, outcome, d_outcome, d_values):
    for h in range(HEADS):
        at = slice(h * HD, (h + 1) * HD)
        mixed[:, at] = jnp.dot(attention[h], values[:, at], preferred_element_type=F32).astype(BF)

    def turn(j):
        block = mixed[:, pl.ds(pl.multiple_of(j * 128, 128), 128)].astype(F32)
        mixed_t[pl.ds(j * 16, 16)] = block.T.reshape(16, 8, SEQ)

    loop(7, turn)

    def columns(n):
        at = pl.ds(pl.multiple_of(n * 256, 256), 256)
        outcome[:, at] = patches[:, at].astype(F32) + jnp.dot(
            mixed[...], output[:, :, at].reshape(HID, 256), preferred_element_type=F32
        )

    loop(7, columns)

    def rows(i):
        at = pl.ds(pl.multiple_of(i * 32, 32), 32)
        total = outcome[at, :]
        centred = total - jnp.mean(total, axis=-1, keepdims=True)
        inverse = lax.rsqrt(jnp.mean(centred * centred, axis=-1, keepdims=True) + 1e-06)
        normal = centred * inverse
        signal = upstream[at, :].astype(F32)
        grad = inverse * (
            signal
            - jnp.mean(signal, axis=-1, keepdims=True)
            - normal * jnp.mean(signal * normal, axis=-1, keepdims=True)
        )
        d_outcome[at, :] = grad.astype(BF)

    loop(8, rows)
    d_mixed = lax.dot_general(
        d_outcome[...], output[...].reshape(HID, D), (((1,), (1,)), ((), ())), preferred_element_type=F32
    ).astype(BF)
    values[...] = d_mixed
    for h in range(HEADS):
        at = slice(h * HD, (h + 1) * HD)
        d_values[:, at] = jnp.dot(attention_t[h], values[:, at], preferred_element_type=F32).astype(BF)


def write_grads(core, normed_t, mixed_t, d_outcome, d_values, grads):
    for hi in (0, 1):
        rows = [mixed_t[pl.ds((hi * 8 + y * 2 + core) * BLOCKS, BLOCKS)].reshape(56, SEQ) for y in range(4)]
        left = jnp.concatenate(rows, axis=0).astype(BF)
        got = jnp.dot(left, d_outcome[...], preferred_element_type=F32).reshape(4, 56, D)
        got = jnp.concatenate([got[:, :, :HID], got[:, :, HID:]], axis=1).astype(BF).reshape(4, BLOCKS, 16, HID)
        for part in PARTS:
            grads[part][2 + hi, :, core] = got[..., STARTS[part]:STARTS[part] + WIDTHS[part]]
    for hi in (0, 1):
        rows = [normed_t[pl.ds((hi * 8 + y * 2 + core) * BLOCKS, BLOCKS)] for y in range(4)]
        left = jnp.concatenate(rows, axis=0).reshape(448, SEQ)
        got = jnp.dot(left, d_values[...], preferred_element_type=F32).astype(BF).reshape(4, BLOCKS, 16, HID)
        for part in PARTS:
            grads[part][hi, :, core] = got[..., STARTS[part]:STARTS[part] + WIDTHS[part]]


def kernel(
    patches, queries, keys, upstream, own,
    value_grad, output_grad,
    full_a, full_b, full_c, grad_a, grad_b, grad_c, owned_a, owned_b, owned_c, out_a, out_b, out_c,
    normed, normed_t, attention, attention_t, base, values, output,
    mixed, mixed_t, outcome, d_outcome, d_values,
    sem_a, sem_b, sem_c, line_a, line_b, _, last_a, last_b, last_c, pair_a, pair_b, pair_c, *scratch,
):
    net = Net()
    net.barrier()
    fulls, grads, outs = (full_a, full_b, full_c), (grad_a, grad_b, grad_c), (out_a, out_b, out_c)
    owned, sems = (owned_a, owned_b, owned_c), (sem_a, sem_b)
    for part in (0, 1):
        fulls[part][net.spot("x"), net.spot("y"), net.c] = own[net.x % 2, :, :, STARTS[part]:STARTS[part] + WIDTHS[part]]

    @pl.when(net.z != 7)
    def _():
        full_c[net.spot("x"), net.spot("y"), net.c, net.z] = own[net.x % 2, net.z, :, STARTS[2]:]

    ring = LineLast(net, full_c, sem_c)
    ring.start()
    gather_all(
        net, fulls, sems, ring,
        (
            lambda: norm_patches(patches, normed, normed_t),
            lambda: attend(queries, keys, attention, attention_t, range(3)),
            lambda: attend(queries, keys, attention, attention_t, range(3, 6)),
            lambda: attend(queries, keys, attention, attention_t, range(6, 8)),
        ),
    )
    set_output(fulls, output, None)

    def write_base(at, total):
        base[:, at] = total
        values[:, at] = total.astype(BF)

    project(normed, fulls, write_base)

    def back():
        backward(patches, upstream, attention, attention_t, output, values, mixed, mixed_t, outcome, d_outcome, d_values)

    def make(core):
        write_grads(core, normed_t, mixed_t, d_outcome, d_values, grads)

    back()
    drain = reduce_all(net, grads, outs, scratch, make)

    @pl.when(net.z != 7)
    def _():
        full_c[net.spot("x"), net.spot("y"), net.c, net.z] = out_c[...]

    spread_line(net, fulls, outs, (line_a, line_b))
    ring.start()
    wait_line(net, fulls, (line_a, line_b), True)
    gather_all(net, fulls, sems, ring)
    wait_line(net, fulls, (line_a, line_b), False)
    drain()
    mean_square = sum_squares(fulls) / (2.0 * D * HID)
    stretch = rho_scale / jnp.sqrt(mean_square + 1e-06)
    set_output(fulls, output, stretch)

    def write_values(at, total):
        values[:, at] = (base[:, at] + stretch * total).astype(BF)

    project(normed, fulls, write_values)
    back()
    drain = reduce_all(net, grads, outs, scratch, make)
    share_owned(net, outs, owned, (last_a, last_b, last_c), (pair_a, pair_b, pair_c))
    drain()
    for part in PARTS:
        w, at = WIDTHS[part], STARTS[part]
        value_grad[:, :, at:at + w] = owned[part][0]
        rows = owned[part][1].astype(F32).reshape(112, w)
        output_grad[:, at:at + w] = rows[:56]
        output_grad[:, HID + at:HID + at + w] = rows[56:]


def vmem(n):
    return [pl.BlockSpec(memory_space=pltpu.VMEM)] * n


def gradients(patches, queries, keys, upstream, own):
    rows = patches.shape[0]
    return pl.pallas_call(
        kernel,
        out_shape=(
            jax.ShapeDtypeStruct((BLOCKS, 16, HID), BF),
            jax.ShapeDtypeStruct((56, D), F32),
        ),
        in_specs=vmem(5),
        out_specs=vmem(2),
        scratch_shapes=(
            [pltpu.VMEM((4, 4, 2, BLOCKS, 16, w), BF) for w in WIDTHS]
            + [pltpu.VMEM((4, 4, 2, BLOCKS, 16, w), BF) for w in WIDTHS]
            + [pltpu.VMEM((2, BLOCKS, 16, w), BF) for w in WIDTHS]
            + [pltpu.VMEM((16, w), BF) for w in WIDTHS]
            + [
                pltpu.VMEM((rows, D), BF),
                pltpu.VMEM((112, 16, rows), BF),
                pltpu.VMEM((HEADS, SEQ, SEQ), BF),
                pltpu.VMEM((HEADS, SEQ, SEQ), BF),
                pltpu.VMEM((rows, HID), F32),
                pltpu.VMEM((rows, HID), BF),
                pltpu.VMEM((56, 16, D), BF),
                pltpu.VMEM((rows, HID), BF),
                pltpu.VMEM((112, 8, rows), F32),
                pltpu.VMEM((rows, D), F32),
                pltpu.VMEM((rows, D), BF),
                pltpu.VMEM((rows, HID), BF),
            ]
            + gather_scratch()
            + [pltpu.SemaphoreType.DMA((2, 7)) for _ in WIDTHS]
            + [pltpu.SemaphoreType.DMA((2, 7)) for _ in WIDTHS]
            + [pltpu.SemaphoreType.DMA((2, 8)) for _ in WIDTHS]
            + reduce_scratch()
        ),
        name="gradients",
        compiler_params=pltpu.CompilerParams(
            collective_id=0, has_side_effects=True, vmem_limit_bytes=60 * 2**20
        ),
    )(patches, queries, keys, upstream, own)


def fold_output(rows):
    half = rows.reshape(56, 2, HID)
    return jnp.swapaxes(half, 0, 1).reshape(BLOCKS, 16, HID)


def adam_update(weight, first, second, gradient):
    first_new = beta_one * first + (1.0 - beta_one) * gradient
    second_new = beta_two * second + (1.0 - beta_two) * gradient * gradient
    update = (
        first_new / first_fix / (jnp.sqrt(second_new / second_fix) + adam_eps)
        + weight_decay * weight
    )
    return (weight - learn_rate * update, first_new, second_new)


def on_device(
    patches,
    queries,
    keys,
    upstream,
    value_weight,
    output_weight,
    value_first,
    output_first,
    value_second,
    output_second,
):
    own = jnp.stack([
        value_weight.astype(BF).reshape(BLOCKS, 16, HID),
        fold_output(output_weight.astype(BF)),
    ])
    value_grad, output_grad = gradients(patches, queries, keys, upstream, own)
    value_new, value_first_new, value_second_new = adam_update(
        value_weight, value_first, value_second, value_grad.reshape(112, HID).astype(F32)
    )
    output_new, output_first_new, output_second_new = adam_update(
        output_weight, output_first, output_second, output_grad
    )
    return (
        value_new,
        output_new,
        value_first_new,
        output_first_new,
        value_second_new,
        output_second_new,
    )


def solution(mesh):
    return jax.shard_map(
        on_device,
        mesh=mesh,
        in_specs=(P(("dp", "fsdp"), None),) * 4 + (P("fsdp", None),) * 6,
        out_specs=(P("fsdp", None),) * 6,
        check_vma=False,
    )
```

```python
import jax
import jax.numpy as jnp
from jax import lax
from jax.experimental import pallas as pl
from jax.experimental.pallas import tpu as pltpu
from jax.sharding import PartitionSpec as P

HEADS = 8
HD = 112
SEQ = 256
D = 1792
HID = 896
BLOCKS = 7
WIDTHS = (384, 384, 128)
PARTS = (0, 1, 2)
MESH = pl.DeviceIdType.MESH
BF = jnp.bfloat16
F32 = jnp.float32


learn_rate = 0.001
weight_decay = 0.1
beta_one = 0.9
beta_two = 0.999
adam_eps = 1e-08
first_fix = 0.9999734386011124
second_fix = 0.0952078528862911
rho_scale = 0.05


def place():
    dp = lax.axis_index("dp")
    fs = lax.axis_index("fsdp")
    return (fs // 8) * 2 + dp // 8, (fs // 2) % 4, dp % 8, fs % 2


def device(x, y, z, c):
    return ((x % 2) * 8 + z, (x // 2) * 8 + y * 2 + c)


def slot(x):
    return (x % 2) * 2 + x // 2


class Net:
    def __init__(self):
        self.x, self.y, self.z, self.c = place()

    def core(self):
        return device(self.x, self.y, self.z, 1 - self.c)

    def along(self, axis, step):
        if axis == "x":
            return device((self.x + step) % 4, self.y, self.z, self.c)
        if axis == "y":
            return device(self.x, (self.y + step) % 4, self.z, self.c)
        return device(self.x, self.y, (self.z + step) % 8, self.c)

    def across(self, i, j):
        return device((self.x + i) % 4, (self.y + j) % 4, self.z, self.c)

    def spot(self, axis, step=0):
        if axis == "x":
            return slot((self.x + step) % 4)
        if axis == "y":
            return (self.y + step) % 4
        return (self.z + step) % 8

    def greet(self):
        sem = pltpu.get_barrier_semaphore()
        targets = [self.core()]
        targets += [self.along("x", s) for s in (1, 2, 3)]
        targets += [self.along("y", s) for s in (1, 2, 3)]
        targets += [self.along("z", s) for s in range(1, 8)]
        targets += [self.across(i, j) for i in (1, 2, 3) for j in (1, 2, 3)]
        for t in targets:
            pl.semaphore_signal(sem, inc=1, device_id=t, device_id_type=MESH)
        return len(targets)

    def meet(self, count):
        pl.semaphore_wait(pltpu.get_barrier_semaphore(), count)


def push(src, dst, send, recv, target):
    copy = pltpu.make_async_remote_copy(
        src_ref=src, dst_ref=dst, send_sem=send, recv_sem=recv, device_id=target, device_id_type=MESH
    )
    copy.start()
    return copy


def add_blocks(count, write, *reads):
    def step(i, carry):
        total = reads[0](i).astype(F32)
        for read in reads[1:]:
            total = total + read(i).astype(F32)
        write(i, total.astype(BF))
        return carry

    lax.fori_loop(0, count, step, 0)


def ordered(part):
    return ("x", "y") if part == 0 else ("y", "x")


def grid_at(ref, part, first, second):
    return ref.at[first, second] if part == 0 else ref.at[second, first]


def reduce_scratch():
    shapes = []
    for w in WIDTHS[:2]:
        shapes += [
            pltpu.VMEM((4, 4, BLOCKS, 16, w), BF),
            pltpu.VMEM((4, 4, BLOCKS, 16, w), BF),
            pltpu.VMEM((2, 2, BLOCKS, 16, w), BF),
            pltpu.VMEM((2, 4, BLOCKS, 16, w), BF),
            pltpu.VMEM((4, BLOCKS, 16, w), BF),
            pltpu.VMEM((3, BLOCKS, 16, w), BF),
            pltpu.VMEM((BLOCKS, 16, w), BF),
            pltpu.VMEM((7, 16, w), BF),
            pltpu.SemaphoreType.DMA((2, 4 + 2 + 4 + 3 + 7)),
        ]
    w = WIDTHS[2]
    return shapes + [
        pltpu.VMEM((4, 4, BLOCKS, 16, w), BF),
        pltpu.VMEM((4, 4, BLOCKS, 16, w), BF),
        pltpu.VMEM((2, 2, 4, 16, w), BF),
        pltpu.VMEM((2, 3, 4, 4, 16, w), BF),
        pltpu.VMEM((4, 4, 16, w), BF),
        pltpu.VMEM((15, 16, w), BF),
        pltpu.SemaphoreType.DMA((2, 1 + 8 + 15)),
    ]


ACROSS = [(i, j) for i in range(4) for j in range(4) if (i, j) != (0, 0)]


class LineFirst:
    def __init__(self, net, grads, out, scratch):
        self.net, self.grads, self.out = net, grads, out
        self.other, self.sums, self.far, self.ring, self.plane, self.from_plane, self.sem = scratch

    def exchange(self):
        net = self.net
        self.core = push(self.grads.at[:, :, 1 - net.c], self.other, self.sem.at[0, 0], self.sem.at[1, 0], net.core())

    def add_cores(self):
        net = self.net
        self.core.wait_recv()
        g, other, sums = self.grads, self.other, self.sums

        def write(i, v):
            sums[i // 4, i % 4] = v

        add_blocks(16, write, lambda i: g[i // 4, i % 4, net.c], lambda i: other[i // 4, i % 4])

    def copy(self, k, way, j):
        j = jnp.minimum(j, 6)
        if k == 0:
            src, dst = self.sums.at[pl.ds(2 * way, 2), :, j], self.far.at[way]
        else:
            src, dst = self.sums.at[:, :, j], self.ring.at[way, k - 1]
        at = 1 + 2 * k + way
        return pltpu.make_async_remote_copy(
            src_ref=src, dst_ref=dst, send_sem=self.sem.at[0, at], recv_sem=self.sem.at[1, at],
            device_id=self.net.along("z", (1, 7)[way]), device_id_type=MESH,
        )

    def sent(self, k, way):
        return (self.net.z + ((4 - k) if way == 0 else (4 + k))) % 8

    def got(self, k, way):
        return (self.net.z + ((3 - k) if way == 0 else (5 + k))) % 8

    def send(self, k):
        for way in (0, 1):
            j = self.sent(k, way)

            @pl.when(j != 7)
            def _():
                self.copy(k, way, j).start()

    def receive(self, k):
        for way in (0, 1):
            j = self.got(k, way)
            at = jnp.minimum(j, 6)

            @pl.when(j != 7)
            def _():
                self.copy(k, way, j).wait_recv()
                if k == 0:
                    rows = slice(2 * way, 2 * way + 2)
                    self.sums[rows, :, at] = (self.sums[rows, :, at].astype(F32) + self.far[way].astype(F32)).astype(BF)
                elif k < 3:
                    self.sums[:, :, at] = (self.sums[:, :, at].astype(F32) + self.ring[way, k - 1].astype(F32)).astype(BF)

    def plane_copy(self, e):
        i, j = ACROSS[e]
        net = self.net
        return pltpu.make_async_remote_copy(
            src_ref=self.plane.at[net.spot("x", i), net.spot("y", j)], dst_ref=self.from_plane.at[e],
            send_sem=self.sem.at[0, 9 + e], recv_sem=self.sem.at[1, 9 + e], device_id=net.across(i, j), device_id_type=MESH,
        )

    def cross(self):
        net = self.net

        @pl.when(net.z != 7)
        def _():
            self.plane[...] = (
                self.sums[:, :, net.z].astype(F32) + self.ring[0, 2].astype(F32) + self.ring[1, 2].astype(F32)
            ).astype(BF)
            for e in range(15):
                self.plane_copy(e).start()

    def finish(self):
        net = self.net

        @pl.when(net.z != 7)
        def _():
            for e in range(15):
                self.plane_copy(e).wait_recv()
            total = self.plane[net.spot("x"), net.spot("y")].astype(F32)
            for e in range(15):
                total = total + self.from_plane[e].astype(F32)
            self.out[...] = total.astype(BF)

    def drain(self):
        self.core.wait_send()
        for k in range(4):
            for way in (0, 1):
                j = self.sent(k, way)

                @pl.when(j != 7)
                def _():
                    self.copy(k, way, j).wait_send()

        @pl.when(self.net.z != 7)
        def _():
            for e in range(15):
                self.plane_copy(e).wait_send()


def reduce_all(net, grads, outs, scratch, make):
    make(1 - net.c)
    ring = LineFirst(net, grads[2], outs[2], scratch[18:])
    ring.exchange()
    state = []
    for part in (0, 1):
        state.append(scratch[part * 9:part * 9 + 9])
    cores = [[], []]
    for step in (2, 1, 3, 0):
        for part in (0, 1):
            other, sums, far, mine, _, _, _, _, sem = state[part]
            first = ordered(part)[0]
            i = net.spot(first, step)
            j = len(cores[part])
            if part == 0:
                src, dst = grads[part].at[i, :, 1 - net.c], other.at[i]
            else:
                src, dst = grads[part].at[:, i, 1 - net.c], other.at[:, i]
            cores[part].append(push(src, dst, sem.at[0, j], sem.at[1, j], net.core()))
    make(net.c)
    ring.add_cores()
    ring.send(0)

    def half_of(ref, part, i, h):
        return ref.at[i, pl.ds(2 * h, 2)] if part == 0 else ref.at[pl.ds(2 * h, 2), i]

    near = [[None] * 6, [None] * 6]
    for j, step in enumerate((2, 1, 3, 0)):
        for part in (0, 1):
            other, sums, far, mine, _, _, _, _, sem = state[part]
            first = ordered(part)[0]
            i = net.spot(first, step)
            cores[part][j].wait_recv()
            g = grads[part]
            if part == 0:
                def write(k, v):
                    sums[i, k] = v
                add_blocks(4, write, lambda k: g[i, k, net.c], lambda k: other[i, k])
            else:
                def write(k, v):
                    sums[k, i] = v
                add_blocks(4, write, lambda k: g[k, i, net.c], lambda k: other[k, i])
            right, left = net.along(first, 1), net.along(first, 3)
            if step == 2:
                near[part][0] = push(half_of(sums, part, i, 0), far.at[0], sem.at[0, 4], sem.at[1, 4], right)
                near[part][1] = push(half_of(sums, part, i, 1), far.at[1], sem.at[0, 5], sem.at[1, 5], left)
            if step == 1:
                near[part][2] = push(half_of(sums, part, i, 1), mine.at[0, pl.ds(2, 2)], sem.at[0, 6], sem.at[1, 6], right)
            if step == 3:
                near[part][3] = push(half_of(sums, part, i, 0), mine.at[1, pl.ds(0, 2)], sem.at[0, 7], sem.at[1, 7], left)
        if j == 1:
            ring.receive(0)
            ring.send(1)
    for part in (0, 1):
        other, sums, far, mine, _, _, _, _, sem = state[part]
        first = ordered(part)[0]
        right, left = net.along(first, 1), net.along(first, 3)
        r, l = net.spot(first, 1), net.spot(first, 3)
        near[part][0].wait_recv()
        if part == 0:
            def write(k, v):
                sums[r, k] = v
            add_blocks(2, write, lambda k: sums[r, k], lambda k: far[0, k])
        else:
            def write(k, v):
                sums[k, r] = v
            add_blocks(2, write, lambda k: sums[k, r], lambda k: far[0, k])
        near[part][4] = push(half_of(sums, part, r, 0), mine.at[0, pl.ds(0, 2)], sem.at[0, 8], sem.at[1, 8], right)
        near[part][1].wait_recv()
        if part == 0:
            def write(k, v):
                sums[l, k + 2] = v
            add_blocks(2, write, lambda k: sums[l, k + 2], lambda k: far[1, k])
        else:
            def write(k, v):
                sums[k + 2, l] = v
            add_blocks(2, write, lambda k: sums[k + 2, l], lambda k: far[1, k])
        near[part][5] = push(half_of(sums, part, l, 1), mine.at[1, pl.ds(2, 2)], sem.at[0, 9], sem.at[1, 9], left)
    for k in (1, 2):
        ring.receive(k)
        ring.send(k + 1)
    second_copies = [[], []]
    for part in (0, 1):
        other, sums, far, mine, row, from_row, _, _, sem = state[part]
        first, second = ordered(part)
        me = net.spot(first)
        for k in (2, 3, 4, 5):
            near[part][k].wait_recv()

        def write(k, v):
            row[k] = v
        if part == 0:
            add_blocks(4, write, lambda k: sums[me, k], lambda k: mine[0, k], lambda k: mine[1, k])
        else:
            add_blocks(4, write, lambda k: sums[k, me], lambda k: mine[0, k], lambda k: mine[1, k])
        for d in (2, 1, 3):
            second_copies[part].append(
                push(row.at[net.spot(second, d)], from_row.at[d - 1], sem.at[0, 9 + d], sem.at[1, 9 + d], net.along(second, d))
            )
    ring.receive(3)
    ring.cross()
    for part in (0, 1):
        other, sums, far, mine, row, from_row, line, from_line, sem = state[part]
        second = ordered(part)[1]
        me = net.spot(second)
        for copy in second_copies[part]:
            copy.wait_recv()

        def write(k, v):
            line[k] = v
        add_blocks(BLOCKS, write, lambda k: row[me, k], lambda k: from_row[0, k], lambda k: from_row[1, k], lambda k: from_row[2, k])
        for d in (4, 3, 5, 2, 6, 1, 7):
            z = net.spot("z", d)

            @pl.when(z != 7)
            def _():
                push(line.at[z], from_line.at[d - 1], sem.at[0, 12 + d], sem.at[1, 12 + d], net.along("z", d))
    ring.finish()
    for part in (0, 1):
        other, sums, far, mine, row, from_row, line, from_line, sem = state[part]

        @pl.when(net.z != 7)
        def _():
            for d in range(1, 8):
                pltpu.make_async_remote_copy(
                    src_ref=line.at[0], dst_ref=from_line.at[d - 1], send_sem=sem.at[0, 12 + d], recv_sem=sem.at[1, 12 + d],
                    device_id=net.along("z", d), device_id_type=MESH,
                ).wait_recv()
            total = line[net.z].astype(F32)
            for d in range(7):
                total = total + from_line[d].astype(F32)
            outs[part][...] = total.astype(BF)

    def drain():
        ring.drain()
        for part in (0, 1):
            other, sums, far, mine, row, from_row, line, from_line, sem = state[part]
            for copy in cores[part] + near[part] + second_copies[part]:
                copy.wait_send()
            for d in range(1, 8):
                @pl.when(net.spot("z", d) != 7)
                def _():
                    pltpu.make_async_remote_copy(
                        src_ref=line.at[0], dst_ref=from_line.at[d - 1], send_sem=sem.at[0, 12 + d], recv_sem=sem.at[1, 12 + d],
                        device_id=net.along("z", d), device_id_type=MESH,
                    ).wait_send()
    return drain


def gather_scratch():
    return [pltpu.SemaphoreType.DMA((2, 16)) for _ in WIDTHS[:2]] + [pltpu.SemaphoreType.DMA((2, 15 + 8 + 9))]


class LineLast:
    def __init__(self, net, full, sem):
        self.net, self.full, self.sem = net, full, sem

    def own(self, e):
        i, j = ACROSS[e]
        net = self.net
        block = self.full.at[net.spot("x"), net.spot("y"), net.c, jnp.minimum(net.z, 6)]
        return pltpu.make_async_remote_copy(
            src_ref=block, dst_ref=block, send_sem=self.sem.at[0, e], recv_sem=self.sem.at[1, e],
            device_id=net.across(i, j), device_id_type=MESH,
        )

    def start(self):
        @pl.when(self.net.z != 7)
        def _():
            for e in range(15):
                self.own(e).start()

    def block(self, j, k, way):
        j = jnp.minimum(j, 6)
        if k == 4:
            return self.full.at[pl.ds(2 * way, 2), :, self.net.c, j]
        return self.full.at[:, :, self.net.c, j]

    def copy(self, k, way, j):
        at = 15 + 2 * (k - 1) + way
        block = self.block(j, k, way)
        return pltpu.make_async_remote_copy(
            src_ref=block, dst_ref=block, send_sem=self.sem.at[0, at], recv_sem=self.sem.at[1, at],
            device_id=self.net.along("z", (1, 7)[way]), device_id_type=MESH,
        )

    def core(self, k, way, j):
        at = 23 if k == 0 else 24 + 2 * (k - 1) + way
        block = self.block(j, k, way)
        return pltpu.make_async_remote_copy(
            src_ref=block, dst_ref=block, send_sem=self.sem.at[0, at], recv_sem=self.sem.at[1, at],
            device_id=self.net.core(), device_id_type=MESH,
        )

    def sent(self, k, way):
        return (self.net.z + ((9 - k) if way == 0 else (k - 1))) % 8

    def got(self, k, way):
        return (self.net.z + ((8 - k) if way == 0 else k)) % 8

    def send(self, k):
        for way in (0, 1):
            j = self.sent(k, way)

            @pl.when(j != 7)
            def _():
                self.copy(k, way, j).start()

    def first(self):
        net = self.net

        @pl.when(net.z != 7)
        def _():
            for e in range(15):
                self.own(e).wait_recv()
            self.core(0, 0, net.z).start()

        self.send(1)

    def step(self, k):
        for way in (0, 1):
            j = self.got(k, way)

            @pl.when(j != 7)
            def _():
                self.copy(k, way, j).wait_recv()
                self.core(k, way, j).start()

        if k < 4:
            self.send(k + 1)

    def finish(self):
        net = self.net

        @pl.when(net.z != 7)
        def _():
            self.core(0, 0, net.z).wait()
            for e in range(15):
                self.own(e).wait_send()

        for k in (1, 2, 3, 4):
            for way in (0, 1):
                j = self.got(k, way)

                @pl.when(j != 7)
                def _():
                    self.core(k, way, j).wait()

                i = self.sent(k, way)

                @pl.when(i != 7)
                def _():
                    self.copy(k, way, i).wait_send()


def second_copy(net, fulls, sems, part, d, source):
    second = ordered(part)[1]
    x, y = net.spot("x"), net.spot("y")
    if source:
        x = net.spot("x", 4 - d) if second == "x" else x
        y = net.spot("y", 4 - d) if second == "y" else y
    chunk = fulls[part].at[x, y, net.c]
    return pltpu.make_async_remote_copy(
        src_ref=chunk, dst_ref=chunk, send_sem=sems[part].at[0, d - 1], recv_sem=sems[part].at[1, d - 1],
        device_id=net.along(second, d), device_id_type=MESH,
    )


def gather_all(net, fulls, sems, ring, between=(), started=False):
    between = list(between) + [lambda: None] * 4

    def piece(part, i, h):
        at = slice(None) if h is None else pl.ds(2 * h, 2)
        return fulls[part].at[i, at, net.c] if part == 0 else fulls[part].at[at, i, net.c]

    def send(part, step, h, at, to):
        block = piece(part, net.spot(ordered(part)[0], step), h)
        return push(block, block, sems[part].at[0, at], sems[part].at[1, at], to)

    def ends(part):
        first = ordered(part)[0]
        return net.along(first, 1), net.along(first, 3)

    rights, lefts, cores = [[], []], [[], []], [[], []]
    between[0]()
    if not started:
        ring.first()
    for part in (0, 1):
        right, left = ends(part)
        for d in (1, 2, 3):
            second_copy(net, fulls, sems, part, d, True).wait_recv()
        rights[part].append(send(part, 0, 0, 3, right))
        lefts[part].append(send(part, 0, 1, 4, left))
        rights[part].append(send(part, 0, 1, 5, right))
        lefts[part].append(send(part, 0, 0, 6, left))
        cores[part].append(send(part, 0, None, 9, net.core()))
    between[1]()
    ring.step(1)
    between[2]()
    for part in (0, 1):
        right, left = ends(part)
        rights[part][0].wait_recv()
        rights[part].append(send(part, 3, 0, 7, right))
        lefts[part][0].wait_recv()
        lefts[part].append(send(part, 1, 1, 8, left))
        cores[part].append(send(part, 3, 0, 10, net.core()))
        cores[part].append(send(part, 1, 1, 11, net.core()))
    ring.step(2)
    between[3]()
    ring.step(3)
    for part in (0, 1):
        rights[part][1].wait_recv()
        cores[part].append(send(part, 3, 1, 12, net.core()))
        lefts[part][1].wait_recv()
        cores[part].append(send(part, 1, 0, 13, net.core()))
    ring.step(4)
    for part in (0, 1):
        rights[part][2].wait_recv()
        cores[part].append(send(part, 2, 0, 14, net.core()))
        lefts[part][2].wait_recv()
        cores[part].append(send(part, 2, 1, 15, net.core()))
    for part in (0, 1):
        for copy in cores[part]:
            copy.wait_recv()
        for copy in rights[part] + lefts[part] + cores[part]:
            copy.wait_send()
        for d in (1, 2, 3):
            second_copy(net, fulls, sems, part, d, False).wait_send()
    ring.finish()


def line_copy(net, fulls, lines, part, d, z):
    block = fulls[part].at[net.spot("x"), net.spot("y"), net.c, jnp.minimum(z, 6)]
    return pltpu.make_async_remote_copy(
        src_ref=block, dst_ref=block, send_sem=lines[part].at[0, d - 1], recv_sem=lines[part].at[1, d - 1],
        device_id=net.along("z", d), device_id_type=MESH,
    )


def spread_line(net, fulls, outs, sems, lines, ring):
    def onward(part, z):
        block = fulls[part].at[net.spot("x"), net.spot("y"), net.c, jnp.minimum(z, 6)]
        for d in (2, 1, 3):
            push(block, block, sems[part].at[0, d - 1], sems[part].at[1, d - 1], net.along(ordered(part)[1], d))

    @pl.when(net.z != 7)
    def _():
        for part in (0, 1):
            fulls[part][net.spot("x"), net.spot("y"), net.c, net.z] = outs[part][...]
        for d in (4, 3, 5, 2, 6, 1, 7):
            for part in (0, 1):
                line_copy(net, fulls, lines, part, d, net.z).start()
        for part in (0, 1):
            onward(part, net.z)

    for d in (1, 7, 2, 6, 3, 5, 4):
        z = (net.z + 8 - d) % 8
        if d == 3:
            ring.first()

        @pl.when(z != 7)
        def _():
            for part in (0, 1):
                line_copy(net, fulls, lines, part, d, z).wait_recv()
                onward(part, z)


def drain_line(net, fulls, lines):
    @pl.when(net.z != 7)
    def _():
        for part in (0, 1):
            for d in range(1, 8):
                line_copy(net, fulls, lines, part, d, net.z).wait_send()


def share_owned(net, outs, owned, sems, pairs):
    half = net.x % 2
    partner = device(net.x + 1 - 2 * half, net.y, net.z, net.c)

    def block(part, z):
        return owned[part].at[half, jnp.minimum(z, 6)]

    def line_copy(part, d, z):
        return pltpu.make_async_remote_copy(
            src_ref=block(part, z), dst_ref=block(part, z), send_sem=sems[part].at[0, d - 1],
            recv_sem=sems[part].at[1, d - 1], device_id=net.along("z", d), device_id_type=MESH,
        )

    def pair_copy(part, d, z):
        return pltpu.make_async_remote_copy(
            src_ref=block(part, z), dst_ref=block(part, z), send_sem=pairs[part].at[0, d],
            recv_sem=pairs[part].at[1, d], device_id=partner, device_id_type=MESH,
        )

    for part in PARTS:
        @pl.when(net.z != 7)
        def _():
            owned[part][half, net.z] = outs[part][...]
            for d in (4, 3, 5, 2, 6, 1, 7):
                line_copy(part, d, net.z).start()
            pair_copy(part, 0, net.z).start()
    for d in (1, 7, 2, 6, 3, 5, 4):
        z = (net.z + 8 - d) % 8

        @pl.when(z != 7)
        def _():
            for part in PARTS:
                line_copy(part, d, z).wait_recv()
                pair_copy(part, d, z).start()
    for d in range(8):
        z = (net.z + 8 - d) % 8

        @pl.when(z != 7)
        def _():
            for part in PARTS:
                pair_copy(part, d, z).wait()
    for part in PARTS:
        @pl.when(net.z != 7)
        def _():
            for d in range(1, 8):
                line_copy(part, d, net.z).wait_send()


def loop(count, body):
    def step(i, carry):
        body(i)
        return carry

    lax.fori_loop(0, count, step, 0)


STARTS = (0, WIDTHS[0], WIDTHS[0] + WIDTHS[1])


def mean_signal(upstream, signal_mean):
    def step(i):
        at = pl.ds(pl.multiple_of(i * 64, 64), 64)
        mean = jnp.mean(upstream[at, :].astype(F32), axis=-1, keepdims=True)
        signal_mean[at, :] = jnp.broadcast_to(mean, (64, 128))

    loop(4, step)


def norm_patches(patches, normed, normed_t):
    def norm(i):
        at = pl.ds(pl.multiple_of(i * 32, 32), 32)
        rows = patches[at, :].astype(F32)
        centred = rows - jnp.mean(rows, axis=-1, keepdims=True)
        scale = lax.rsqrt(jnp.mean(centred * centred, axis=-1, keepdims=True) + 1e-06)
        normed[at, :] = (centred * scale).astype(BF)

    loop(8, norm)

    def turn(j):
        block = normed[:, pl.ds(pl.multiple_of(j * 128, 128), 128)]
        normed_t[pl.ds(j * 8, 8)] = block.T.reshape(8, 16, SEQ)

    loop(14, turn)


def attend(queries, keys, attention, attention_t, heads):
    for h in heads:
        q = queries[:, h * HD:(h + 1) * HD]
        k = keys[:, h * HD:(h + 1) * HD]
        scores = lax.dot_general(q, k, (((1,), (1,)), ((), ())), preferred_element_type=F32) * HD ** (-0.5)
        expo = jnp.exp(scores - jnp.max(scores, axis=-1, keepdims=True))
        weights = (expo / jnp.sum(expo, axis=-1, keepdims=True)).astype(BF)
        attention[h] = weights
        attention_t[h] = weights.T


def project(normed, fulls, write):
    for part in PARTS:
        w, at = WIDTHS[part], STARTS[part]
        total = jnp.dot(normed[:, :HID], fulls[part][0].reshape(HID, w), preferred_element_type=F32)
        total = total + jnp.dot(normed[:, HID:], fulls[part][1].reshape(HID, w), preferred_element_type=F32)
        write(slice(at, at + w), total)


def unfold(full, i):
    both = full[2 + i // 4, i % 4].astype(F32)
    both = both.reshape(2, 112, both.shape[-1])
    left = jnp.concatenate([both[0, :56], both[1, :56]], axis=0)
    right = jnp.concatenate([both[0, 56:], both[1, 56:]], axis=0)
    return left, right


def set_output(fulls, output, stretch):
    def step(i):
        for part in PARTS:
            w = WIDTHS[part]
            for half, rows in enumerate(unfold(fulls[part], i)):
                at = (pl.ds(i * BLOCKS, BLOCKS), slice(None), slice(half * HID + STARTS[part], half * HID + STARTS[part] + w))
                if stretch is not None:
                    rows = output[at].astype(F32).reshape(112, w) + stretch * rows
                output[at] = rows.astype(BF).reshape(BLOCKS, 16, w)

    loop(8, step)


def sum_squares(fulls):
    def step(i, totals):
        out = []
        for part in PARTS:
            block = fulls[part][i // 4, i % 4].astype(F32)
            block = block.reshape(2 * BLOCKS, 16, WIDTHS[part])
            out.append(totals[part] + jnp.sum(block * block, axis=0))
        return tuple(out)

    totals = lax.fori_loop(0, 16, step, tuple(jnp.zeros((16, w), F32) for w in WIDTHS))
    parts = [jnp.sum(jnp.sum(t, axis=0, keepdims=True), axis=1, keepdims=True) for t in totals]
    return parts[0] + parts[1] + parts[2]


def backward(patches, upstream, signal_mean, attention, attention_t, output, values, mixed, mixed_t, outcome, d_outcome, d_values):
    for h in range(HEADS):
        at = slice(h * HD, (h + 1) * HD)
        mixed[:, at] = jnp.dot(attention[h], values[:, at], preferred_element_type=F32).astype(BF)

    def turn(j):
        block = mixed[:, pl.ds(pl.multiple_of(j * 128, 128), 128)].astype(F32)
        mixed_t[pl.ds(j * 16, 16)] = block.T.reshape(16, 8, SEQ)

    loop(7, turn)

    outcome[...] = patches[...].astype(F32) + jnp.dot(
        mixed[...], output[...].reshape(HID, D), preferred_element_type=F32
    )

    def rows(i):
        at = pl.ds(pl.multiple_of(i * 128, 128), 128)
        tiles = [slice(j * 128, j * 128 + 128) for j in range(14)]
        total = outcome[at, tiles[0]]
        for tile in tiles[1:]:
            total = total + outcome[at, tile]
        mean = jnp.sum(total, axis=-1, keepdims=True) / D
        squares, cross = jnp.zeros((128, 128), F32), jnp.zeros((128, 128), F32)
        for tile in tiles:
            centred = outcome[at, tile] - mean
            squares = squares + centred * centred
            cross = cross + centred * upstream[at, tile].astype(F32)
        inverse = lax.rsqrt(jnp.sum(squares, axis=-1, keepdims=True) / D + 1e-06)
        slope = inverse * inverse * (jnp.sum(cross, axis=-1, keepdims=True) / D)
        level = signal_mean[at, 0:1]
        for tile in tiles:
            centred = outcome[at, tile] - mean
            d_outcome[at, tile] = (inverse * (upstream[at, tile].astype(F32) - level - centred * slope)).astype(BF)

    loop(2, rows)
    d_mixed = lax.dot_general(
        d_outcome[...], output[...].reshape(HID, D), (((1,), (1,)), ((), ())), preferred_element_type=F32
    ).astype(BF)
    values[...] = d_mixed
    for h in range(HEADS):
        at = slice(h * HD, (h + 1) * HD)
        d_values[:, at] = jnp.dot(attention_t[h], values[:, at], preferred_element_type=F32).astype(BF)


def write_grads(core, normed_t, mixed_t, d_outcome, d_values, grads):
    for hi in (0, 1):
        rows = [mixed_t[pl.ds((hi * 8 + y * 2 + core) * BLOCKS, BLOCKS)].reshape(56, SEQ) for y in range(4)]
        left = jnp.concatenate(rows, axis=0).astype(BF)
        got = jnp.dot(left, d_outcome[...], preferred_element_type=F32).reshape(4, 56, D)
        got = jnp.concatenate([got[:, :, :HID], got[:, :, HID:]], axis=1).astype(BF).reshape(4, BLOCKS, 16, HID)
        for part in PARTS:
            grads[part][2 + hi, :, core] = got[..., STARTS[part]:STARTS[part] + WIDTHS[part]]
    for hi in (0, 1):
        rows = [normed_t[pl.ds((hi * 8 + y * 2 + core) * BLOCKS, BLOCKS)] for y in range(4)]
        left = jnp.concatenate(rows, axis=0).reshape(448, SEQ)
        got = jnp.dot(left, d_values[...], preferred_element_type=F32).astype(BF).reshape(4, BLOCKS, 16, HID)
        for part in PARTS:
            grads[part][hi, :, core] = got[..., STARTS[part]:STARTS[part] + WIDTHS[part]]


def kernel(
    patches_hbm, queries_hbm, keys_hbm, upstream_hbm, value_rows, output_rows,
    value_grad, output_grad,
    patches, queries, keys, upstream, own, signal_mean, load_sem,
    full_a, full_b, full_c, grad_a, grad_b, grad_c, owned_a, owned_b, owned_c, out_a, out_b, out_c,
    normed, normed_t, attention, attention_t, base, values, output,
    mixed, mixed_t, outcome, d_outcome, d_values,
    sem_a, sem_b, sem_c, line_a, line_b, _, last_a, last_b, last_c, pair_a, pair_b, pair_c, *scratch,
):
    net = Net()
    greeted = net.greet()
    loads = []
    for i, pair in enumerate(((patches_hbm, patches), (queries_hbm, queries), (keys_hbm, keys), (upstream_hbm, upstream))):
        load = pltpu.make_async_copy(*pair, load_sem.at[i])
        load.start()
        loads.append(load)
    fulls, grads, outs = (full_a, full_b, full_c), (grad_a, grad_b, grad_c), (out_a, out_b, out_c)
    owned, sems, lines = (owned_a, owned_b, owned_c), (sem_a, sem_b), (line_a, line_b)

    @pl.when(net.x % 2 == 0)
    def _():
        own[...] = value_rows[...].astype(BF).reshape(BLOCKS, 16, HID)

    @pl.when(net.x % 2 == 1)
    def _():
        rows = jnp.concatenate([output_rows[:, :HID], output_rows[:, HID:]], axis=0)
        own[...] = rows.astype(BF).reshape(BLOCKS, 16, HID)

    for part in (0, 1):
        fulls[part][net.spot("x"), net.spot("y"), net.c] = own[:, :, STARTS[part]:STARTS[part] + WIDTHS[part]]

    @pl.when(net.z != 7)
    def _():
        full_c[net.spot("x"), net.spot("y"), net.c, net.z] = own[net.z, :, STARTS[2]:]

    net.meet(greeted)
    for part in (0, 1):
        for d in (2, 1, 3):
            second_copy(net, fulls, sems, part, d, False).start()
    ring = LineLast(net, full_c, sem_c)
    ring.start()

    def prepare():
        loads[0].wait()
        norm_patches(patches, normed, normed_t)

    def first_heads():
        for load in loads[1:]:
            load.wait()
        attend(queries, keys, attention, attention_t, range(3))
        mean_signal(upstream, signal_mean)

    gather_all(
        net, fulls, sems, ring,
        (
            prepare,
            first_heads,
            lambda: attend(queries, keys, attention, attention_t, range(3, 6)),
            lambda: attend(queries, keys, attention, attention_t, range(6, 8)),
        ),
    )
    set_output(fulls, output, None)

    def write_base(at, total):
        base[:, at] = total
        values[:, at] = total.astype(BF)

    project(normed, fulls, write_base)

    def back():
        backward(patches, upstream, signal_mean, attention, attention_t, output, values, mixed, mixed_t, outcome, d_outcome, d_values)

    def make(core):
        write_grads(core, normed_t, mixed_t, d_outcome, d_values, grads)

    back()
    drain = reduce_all(net, grads, outs, scratch, make)

    @pl.when(net.z != 7)
    def _():
        full_c[net.spot("x"), net.spot("y"), net.c, net.z] = out_c[...]

    ring.start()
    spread_line(net, fulls, outs, sems, lines, ring)
    gather_all(net, fulls, sems, ring, started=True)
    drain_line(net, fulls, lines)
    drain()
    mean_square = sum_squares(fulls) / (2.0 * D * HID)
    stretch = rho_scale / jnp.sqrt(mean_square + 1e-06)
    set_output(fulls, output, stretch)

    def write_values(at, total):
        values[:, at] = (base[:, at] + stretch * total).astype(BF)

    project(normed, fulls, write_values)
    back()
    drain = reduce_all(net, grads, outs, scratch, make)
    share_owned(net, outs, owned, (last_a, last_b, last_c), (pair_a, pair_b, pair_c))
    drain()
    for part in PARTS:
        w, at = WIDTHS[part], STARTS[part]
        value_grad[:, :, at:at + w] = owned[part][0]
        rows = owned[part][1].astype(F32).reshape(112, w)
        output_grad[:, at:at + w] = rows[:56]
        output_grad[:, HID + at:HID + at + w] = rows[56:]


def vmem(n):
    return [pl.BlockSpec(memory_space=pltpu.VMEM)] * n


def gradients(patches, queries, keys, upstream, value_weight, output_weight):
    rows = patches.shape[0]
    return pl.pallas_call(
        kernel,
        out_shape=(
            jax.ShapeDtypeStruct((BLOCKS, 16, HID), BF),
            jax.ShapeDtypeStruct((56, D), F32),
        ),
        in_specs=[pl.BlockSpec(memory_space=pl.ANY)] * 4 + vmem(2),
        out_specs=vmem(2),
        scratch_shapes=(
            [pltpu.VMEM((rows, w), BF) for w in (D, HID, HID, D)]
            + [pltpu.VMEM((BLOCKS, 16, HID), BF), pltpu.VMEM((rows, 128), F32), pltpu.SemaphoreType.DMA((4,))]
            + [pltpu.VMEM((4, 4, 2, BLOCKS, 16, w), BF) for w in WIDTHS]
            + [pltpu.VMEM((4, 4, 2, BLOCKS, 16, w), BF) for w in WIDTHS]
            + [pltpu.VMEM((2, BLOCKS, 16, w), BF) for w in WIDTHS]
            + [pltpu.VMEM((16, w), BF) for w in WIDTHS]
            + [
                pltpu.VMEM((rows, D), BF),
                pltpu.VMEM((112, 16, rows), BF),
                pltpu.VMEM((HEADS, SEQ, SEQ), BF),
                pltpu.VMEM((HEADS, SEQ, SEQ), BF),
                pltpu.VMEM((rows, HID), F32),
                pltpu.VMEM((rows, HID), BF),
                pltpu.VMEM((56, 16, D), BF),
                pltpu.VMEM((rows, HID), BF),
                pltpu.VMEM((112, 8, rows), F32),
                pltpu.VMEM((rows, D), F32),
                pltpu.VMEM((rows, D), BF),
                pltpu.VMEM((rows, HID), BF),
            ]
            + gather_scratch()
            + [pltpu.SemaphoreType.DMA((2, 7)) for _ in WIDTHS]
            + [pltpu.SemaphoreType.DMA((2, 7)) for _ in WIDTHS]
            + [pltpu.SemaphoreType.DMA((2, 8)) for _ in WIDTHS]
            + reduce_scratch()
        ),
        name="gradients",
        compiler_params=pltpu.CompilerParams(
            collective_id=0, has_side_effects=True, vmem_limit_bytes=60 * 2**20
        ),
    )(patches, queries, keys, upstream, value_weight, output_weight)


def adam_update(weight, first, second, gradient):
    first_new = beta_one * first + (1.0 - beta_one) * gradient
    second_new = beta_two * second + (1.0 - beta_two) * gradient * gradient
    update = (
        first_new / first_fix / (jnp.sqrt(second_new / second_fix) + adam_eps)
        + weight_decay * weight
    )
    return (weight - learn_rate * update, first_new, second_new)


def on_device(
    patches,
    queries,
    keys,
    upstream,
    value_weight,
    output_weight,
    value_first,
    output_first,
    value_second,
    output_second,
):
    value_grad, output_grad = gradients(patches, queries, keys, upstream, value_weight, output_weight)
    value_new, value_first_new, value_second_new = adam_update(
        value_weight, value_first, value_second, value_grad.reshape(112, HID).astype(F32)
    )
    output_new, output_first_new, output_second_new = adam_update(
        output_weight, output_first, output_second, output_grad
    )
    return (
        value_new,
        output_new,
        value_first_new,
        output_first_new,
        value_second_new,
        output_second_new,
    )


def solution(mesh):
    return jax.shard_map(
        on_device,
        mesh=mesh,
        in_specs=(P(("dp", "fsdp"), None),) * 4 + (P("fsdp", None),) * 6,
        out_specs=(P("fsdp", None),) * 6,
        check_vma=False,
    )
```

```python
import jax
import jax.numpy as jnp
from jax import lax
from jax.experimental import pallas as pl
from jax.experimental.pallas import tpu as pltpu
from jax.sharding import PartitionSpec as P

HEADS = 8
HD = 112
SEQ = 256
D = 1792
HID = 896
BLOCKS = 7
WIDTHS = (384, 384, 128)
PARTS = (0, 1, 2)
MESH = pl.DeviceIdType.MESH
BF = jnp.bfloat16
F32 = jnp.float32


learn_rate = 0.001
weight_decay = 0.1
beta_one = 0.9
beta_two = 0.999
adam_eps = 1e-08
first_fix = 0.9999734386011124
second_fix = 0.0952078528862911
rho_scale = 0.05


def place():
    dp = lax.axis_index("dp")
    fs = lax.axis_index("fsdp")
    return (fs // 8) * 2 + dp // 8, (fs // 2) % 4, dp % 8, fs % 2


def device(x, y, z, c):
    return ((x % 2) * 8 + z, (x // 2) * 8 + y * 2 + c)


def slot(x):
    return (x % 2) * 2 + x // 2


class Net:
    def __init__(self):
        self.x, self.y, self.z, self.c = place()

    def core(self):
        return device(self.x, self.y, self.z, 1 - self.c)

    def along(self, axis, step):
        if axis == "x":
            return device((self.x + step) % 4, self.y, self.z, self.c)
        if axis == "y":
            return device(self.x, (self.y + step) % 4, self.z, self.c)
        return device(self.x, self.y, (self.z + step) % 8, self.c)

    def across(self, i, j):
        return device((self.x + i) % 4, (self.y + j) % 4, self.z, self.c)

    def spot(self, axis, step=0):
        if axis == "x":
            return slot((self.x + step) % 4)
        if axis == "y":
            return (self.y + step) % 4
        return (self.z + step) % 8

    def greet(self):
        sem = pltpu.get_barrier_semaphore()
        targets = [self.core()]
        targets += [self.along("x", s) for s in (1, 2, 3)]
        targets += [self.along("y", s) for s in (1, 2, 3)]
        targets += [self.along("z", s) for s in range(1, 8)]
        targets += [self.across(i, j) for i in (1, 2, 3) for j in (1, 2, 3)]
        for t in targets:
            pl.semaphore_signal(sem, inc=1, device_id=t, device_id_type=MESH)
        return len(targets)

    def meet(self, count):
        pl.semaphore_wait(pltpu.get_barrier_semaphore(), count)


def push(src, dst, send, recv, target):
    copy = pltpu.make_async_remote_copy(
        src_ref=src, dst_ref=dst, send_sem=send, recv_sem=recv, device_id=target, device_id_type=MESH
    )
    copy.start()
    return copy


def add_blocks(count, write, *reads):
    def step(i, carry):
        total = reads[0](i).astype(F32)
        for read in reads[1:]:
            total = total + read(i).astype(F32)
        write(i, total.astype(BF))
        return carry

    lax.fori_loop(0, count, step, 0)


def ordered(part):
    return ("x", "y") if part == 0 else ("y", "x")


def grid_at(ref, part, first, second):
    return ref.at[first, second] if part == 0 else ref.at[second, first]


def reduce_scratch():
    shapes = []
    for w in WIDTHS[:2]:
        shapes += [
            pltpu.VMEM((4, 4, BLOCKS, 16, w), BF),
            pltpu.VMEM((4, 4, BLOCKS, 16, w), BF),
            pltpu.VMEM((2, 2, BLOCKS, 16, w), BF),
            pltpu.VMEM((2, 4, BLOCKS, 16, w), BF),
            pltpu.VMEM((4, BLOCKS, 16, w), BF),
            pltpu.VMEM((3, BLOCKS, 16, w), BF),
            pltpu.VMEM((BLOCKS, 16, w), BF),
            pltpu.VMEM((7, 16, w), BF),
            pltpu.SemaphoreType.DMA((2, 4 + 2 + 4 + 3 + 7 + 3)),
        ]
    w = WIDTHS[2]
    return shapes + [
        pltpu.VMEM((4, 4, BLOCKS, 16, w), BF),
        pltpu.VMEM((4, 4, BLOCKS, 16, w), BF),
        pltpu.VMEM((2, 2, 4, 16, w), BF),
        pltpu.VMEM((2, 3, 4, 4, 16, w), BF),
        pltpu.VMEM((4, 4, 16, w), BF),
        pltpu.VMEM((15, 16, w), BF),
        pltpu.SemaphoreType.DMA((2, 1 + 8 + 15)),
    ]


ACROSS = [(i, j) for i in range(4) for j in range(4) if (i, j) != (0, 0)]


class LineFirst:
    def __init__(self, net, grads, out, scratch):
        self.net, self.grads, self.out = net, grads, out
        self.other, self.sums, self.far, self.ring, self.plane, self.from_plane, self.sem = scratch

    def exchange(self):
        net = self.net
        self.core = push(self.grads.at[:, :, 1 - net.c], self.other, self.sem.at[0, 0], self.sem.at[1, 0], net.core())

    def add_cores(self):
        net = self.net
        self.core.wait_recv()
        g, other, sums = self.grads, self.other, self.sums

        def write(i, v):
            sums[i // 4, i % 4] = v

        add_blocks(16, write, lambda i: g[i // 4, i % 4, net.c], lambda i: other[i // 4, i % 4])

    def copy(self, k, way, j):
        j = jnp.minimum(j, 6)
        if k == 0:
            src, dst = self.sums.at[pl.ds(2 * way, 2), :, j], self.far.at[way]
        else:
            src, dst = self.sums.at[:, :, j], self.ring.at[way, k - 1]
        at = 1 + 2 * k + way
        return pltpu.make_async_remote_copy(
            src_ref=src, dst_ref=dst, send_sem=self.sem.at[0, at], recv_sem=self.sem.at[1, at],
            device_id=self.net.along("z", (1, 7)[way]), device_id_type=MESH,
        )

    def sent(self, k, way):
        return (self.net.z + ((4 - k) if way == 0 else (4 + k))) % 8

    def got(self, k, way):
        return (self.net.z + ((3 - k) if way == 0 else (5 + k))) % 8

    def send(self, k):
        for way in (0, 1):
            j = self.sent(k, way)

            @pl.when(j != 7)
            def _():
                self.copy(k, way, j).start()

    def receive(self, k):
        for way in (0, 1):
            j = self.got(k, way)
            at = jnp.minimum(j, 6)

            @pl.when(j != 7)
            def _():
                self.copy(k, way, j).wait_recv()
                if k == 0:
                    rows = slice(2 * way, 2 * way + 2)
                    self.sums[rows, :, at] = (self.sums[rows, :, at].astype(F32) + self.far[way].astype(F32)).astype(BF)
                elif k < 3:
                    self.sums[:, :, at] = (self.sums[:, :, at].astype(F32) + self.ring[way, k - 1].astype(F32)).astype(BF)

    def plane_copy(self, e):
        i, j = ACROSS[e]
        net = self.net
        return pltpu.make_async_remote_copy(
            src_ref=self.plane.at[net.spot("x", i), net.spot("y", j)], dst_ref=self.from_plane.at[e],
            send_sem=self.sem.at[0, 9 + e], recv_sem=self.sem.at[1, 9 + e], device_id=net.across(i, j), device_id_type=MESH,
        )

    def cross(self):
        net = self.net

        @pl.when(net.z != 7)
        def _():
            self.plane[...] = (
                self.sums[:, :, net.z].astype(F32) + self.ring[0, 2].astype(F32) + self.ring[1, 2].astype(F32)
            ).astype(BF)
            for e in range(15):
                self.plane_copy(e).start()

    def finish(self):
        net = self.net

        @pl.when(net.z != 7)
        def _():
            for e in range(15):
                self.plane_copy(e).wait_recv()
            total = self.plane[net.spot("x"), net.spot("y")].astype(F32)
            for e in range(15):
                total = total + self.from_plane[e].astype(F32)
            self.out[...] = total.astype(BF)

    def drain(self):
        self.core.wait_send()
        for k in range(4):
            for way in (0, 1):
                j = self.sent(k, way)

                @pl.when(j != 7)
                def _():
                    self.copy(k, way, j).wait_send()

        @pl.when(self.net.z != 7)
        def _():
            for e in range(15):
                self.plane_copy(e).wait_send()


def reduce_all(net, grads, outs, scratch, make):
    make(1 - net.c)
    ring = LineFirst(net, grads[2], outs[2], scratch[18:])
    state = []
    for part in (0, 1):
        state.append(scratch[part * 9:part * 9 + 9])
    cores = [[], []]
    for step in (2, 1, 3, 0):
        for part in (0, 1):
            other, sums, far, mine, _, _, _, _, sem = state[part]
            first = ordered(part)[0]
            i = net.spot(first, step)
            j = len(cores[part])
            if part == 0:
                src, dst = grads[part].at[i, :, 1 - net.c], other.at[i]
            else:
                src, dst = grads[part].at[:, i, 1 - net.c], other.at[:, i]
            cores[part].append(push(src, dst, sem.at[0, j], sem.at[1, j], net.core()))
        if step == 2:
            ring.exchange()
    make(net.c)

    def half_of(ref, part, i, h):
        return ref.at[i, pl.ds(2 * h, 2)] if part == 0 else ref.at[pl.ds(2 * h, 2), i]

    near = [[None] * 6, [None] * 6]
    for j, step in enumerate((2, 1, 3, 0)):
        for part in (0, 1):
            other, sums, far, mine, _, _, _, _, sem = state[part]
            first = ordered(part)[0]
            i = net.spot(first, step)
            cores[part][j].wait_recv()
            g = grads[part]
            if part == 0:
                def write(k, v):
                    sums[i, k] = v
                add_blocks(4, write, lambda k: g[i, k, net.c], lambda k: other[i, k])
            else:
                def write(k, v):
                    sums[k, i] = v
                add_blocks(4, write, lambda k: g[k, i, net.c], lambda k: other[k, i])
            right, left = net.along(first, 1), net.along(first, 3)
            if step == 2:
                near[part][0] = push(half_of(sums, part, i, 0), far.at[0], sem.at[0, 4], sem.at[1, 4], right)
                near[part][1] = push(half_of(sums, part, i, 1), far.at[1], sem.at[0, 5], sem.at[1, 5], left)
            if step == 1:
                near[part][2] = push(half_of(sums, part, i, 1), mine.at[0, pl.ds(2, 2)], sem.at[0, 6], sem.at[1, 6], right)
            if step == 3:
                near[part][3] = push(half_of(sums, part, i, 0), mine.at[1, pl.ds(0, 2)], sem.at[0, 7], sem.at[1, 7], left)
        if j == 0:
            ring.add_cores()
            ring.send(0)
        if j == 2:
            ring.receive(0)
            ring.send(1)
    for part in (0, 1):
        other, sums, far, mine, _, _, _, _, sem = state[part]
        first = ordered(part)[0]
        right, left = net.along(first, 1), net.along(first, 3)
        r, l = net.spot(first, 1), net.spot(first, 3)
        near[part][0].wait_recv()
        if part == 0:
            def write(k, v):
                sums[r, k] = v
            add_blocks(2, write, lambda k: sums[r, k], lambda k: far[0, k])
        else:
            def write(k, v):
                sums[k, r] = v
            add_blocks(2, write, lambda k: sums[k, r], lambda k: far[0, k])
        near[part][4] = push(half_of(sums, part, r, 0), mine.at[0, pl.ds(0, 2)], sem.at[0, 8], sem.at[1, 8], right)
        near[part][1].wait_recv()
        if part == 0:
            def write(k, v):
                sums[l, k + 2] = v
            add_blocks(2, write, lambda k: sums[l, k + 2], lambda k: far[1, k])
        else:
            def write(k, v):
                sums[k + 2, l] = v
            add_blocks(2, write, lambda k: sums[k + 2, l], lambda k: far[1, k])
        near[part][5] = push(half_of(sums, part, l, 1), mine.at[1, pl.ds(2, 2)], sem.at[0, 9], sem.at[1, 9], left)
    for k in (1, 2):
        ring.receive(k)
        ring.send(k + 1)
    second_copies = [[], []]
    for part in (0, 1):
        other, sums, far, mine, row, from_row, _, _, sem = state[part]
        first, second = ordered(part)
        me = net.spot(first)
        for k in (2, 3, 4, 5):
            near[part][k].wait_recv()

        def write(k, v):
            row[k] = v
        if part == 0:
            add_blocks(4, write, lambda k: sums[me, k], lambda k: mine[0, k], lambda k: mine[1, k])
        else:
            add_blocks(4, write, lambda k: sums[k, me], lambda k: mine[0, k], lambda k: mine[1, k])
        for g, blocks in enumerate((pl.ds(0, 4), pl.ds(4, 3))):
            for d in (2, 1, 3):
                at = (9 if g == 0 else 19) + d
                second_copies[part].append(
                    push(row.at[net.spot(second, d), blocks], from_row.at[d - 1, blocks], sem.at[0, at], sem.at[1, at], net.along(second, d))
                )
    ring.receive(3)
    ring.cross()
    for g, (start, count) in enumerate(((0, 4), (4, 3))):
        for part in (0, 1):
            other, sums, far, mine, row, from_row, line, from_line, sem = state[part]
            me = net.spot(ordered(part)[1])
            for copy in second_copies[part][3 * g:3 * g + 3]:
                copy.wait_recv()

            def write(k, v):
                line[start + k] = v
            add_blocks(
                count, write, lambda k: row[me, start + k], lambda k: from_row[0, start + k],
                lambda k: from_row[1, start + k], lambda k: from_row[2, start + k],
            )
            for d in (4, 3, 5, 2, 6, 1, 7):
                z = net.spot("z", d)

                @pl.when((z >= start) & (z < start + count))
                def _():
                    push(line.at[z], from_line.at[d - 1], sem.at[0, 12 + d], sem.at[1, 12 + d], net.along("z", d))
    ring.finish()
    for part in (0, 1):
        other, sums, far, mine, row, from_row, line, from_line, sem = state[part]

        @pl.when(net.z != 7)
        def _():
            for d in range(1, 8):
                pltpu.make_async_remote_copy(
                    src_ref=line.at[0], dst_ref=from_line.at[d - 1], send_sem=sem.at[0, 12 + d], recv_sem=sem.at[1, 12 + d],
                    device_id=net.along("z", d), device_id_type=MESH,
                ).wait_recv()
            total = line[net.z].astype(F32)
            for d in range(7):
                total = total + from_line[d].astype(F32)
            outs[part][...] = total.astype(BF)

    def drain():
        ring.drain()
        for part in (0, 1):
            other, sums, far, mine, row, from_row, line, from_line, sem = state[part]
            for copy in cores[part] + near[part] + second_copies[part]:
                copy.wait_send()
            for d in range(1, 8):
                @pl.when(net.spot("z", d) != 7)
                def _():
                    pltpu.make_async_remote_copy(
                        src_ref=line.at[0], dst_ref=from_line.at[d - 1], send_sem=sem.at[0, 12 + d], recv_sem=sem.at[1, 12 + d],
                        device_id=net.along("z", d), device_id_type=MESH,
                    ).wait_send()
    return drain


def gather_scratch():
    return [pltpu.SemaphoreType.DMA((2, 16)) for _ in WIDTHS[:2]] + [pltpu.SemaphoreType.DMA((2, 15 + 16 + 17))]


class LineLast:
    def __init__(self, net, full, sem):
        self.net, self.full, self.sem = net, full, sem

    def own(self, e):
        i, j = ACROSS[e]
        net = self.net
        block = self.full.at[net.spot("x"), net.spot("y"), net.c, jnp.minimum(net.z, 6)]
        return pltpu.make_async_remote_copy(
            src_ref=block, dst_ref=block, send_sem=self.sem.at[0, e], recv_sem=self.sem.at[1, e],
            device_id=net.across(i, j), device_id_type=MESH,
        )

    def start(self):
        @pl.when(self.net.z != 7)
        def _():
            for e in range(15):
                self.own(e).start()

    def block(self, j, h):
        return self.full.at[pl.ds(2 * h, 2), :, self.net.c, jnp.minimum(j, 6)]

    def copy(self, k, way, j, h):
        at = 15 + 4 * (k - 1) + 2 * way + h
        block = self.block(j, h)
        return pltpu.make_async_remote_copy(
            src_ref=block, dst_ref=block, send_sem=self.sem.at[0, at], recv_sem=self.sem.at[1, at],
            device_id=self.net.along("z", (1, 7)[way]), device_id_type=MESH,
        )

    def core(self, k, way, j, h):
        at = 31 if k == 0 else 32 + 4 * (k - 1) + 2 * way + h
        block = self.full.at[:, :, self.net.c, jnp.minimum(j, 6)] if k == 0 else self.block(j, h)
        return pltpu.make_async_remote_copy(
            src_ref=block, dst_ref=block, send_sem=self.sem.at[0, at], recv_sem=self.sem.at[1, at],
            device_id=self.net.core(), device_id_type=MESH,
        )

    def halves(self, k, way):
        return (way,) if k == 4 else (way, 1 - way)

    def sent(self, k, way):
        return (self.net.z + ((9 - k) if way == 0 else (k - 1))) % 8

    def got(self, k, way):
        return (self.net.z + ((8 - k) if way == 0 else k)) % 8

    def first(self):
        net = self.net

        @pl.when(net.z != 7)
        def _():
            for e in range(15):
                self.own(e).wait_recv()
            for at in (0, 1):
                for way in (0, 1):
                    self.copy(1, way, net.z, self.halves(1, way)[at]).start()
            self.core(0, 0, net.z, 0).start()

    def step(self, k):
        for at in range(len(self.halves(k, 0))):
            for way in (0, 1):
                h = self.halves(k, way)[at]
                j = self.got(k, way)

                @pl.when(j != 7)
                def _():
                    self.copy(k, way, j, h).wait_recv()
                    if k < 4 and h in self.halves(k + 1, way):
                        self.copy(k + 1, way, j, h).start()
                    self.core(k, way, j, h).start()

    def finish(self):
        net = self.net

        @pl.when(net.z != 7)
        def _():
            self.core(0, 0, net.z, 0).wait()
            for e in range(15):
                self.own(e).wait_send()

        for k in (1, 2, 3, 4):
            for way in (0, 1):
                for h in self.halves(k, way):
                    j, i = self.got(k, way), self.sent(k, way)

                    @pl.when(j != 7)
                    def _():
                        self.core(k, way, j, h).wait()

                    @pl.when(i != 7)
                    def _():
                        self.copy(k, way, i, h).wait_send()


def second_copy(net, fulls, sems, part, d, source):
    second = ordered(part)[1]
    x, y = net.spot("x"), net.spot("y")
    if source:
        x = net.spot("x", 4 - d) if second == "x" else x
        y = net.spot("y", 4 - d) if second == "y" else y
    chunk = fulls[part].at[x, y, net.c]
    return pltpu.make_async_remote_copy(
        src_ref=chunk, dst_ref=chunk, send_sem=sems[part].at[0, d - 1], recv_sem=sems[part].at[1, d - 1],
        device_id=net.along(second, d), device_id_type=MESH,
    )


def gather_all(net, fulls, sems, ring, between=(), started=False):
    between = list(between) + [lambda: None] * 4

    def piece(part, i, h):
        at = slice(None) if h is None else pl.ds(2 * h, 2)
        return fulls[part].at[i, at, net.c] if part == 0 else fulls[part].at[at, i, net.c]

    def send(part, step, h, at, to):
        block = piece(part, net.spot(ordered(part)[0], step), h)
        return push(block, block, sems[part].at[0, at], sems[part].at[1, at], to)

    def ends(part):
        first = ordered(part)[0]
        return net.along(first, 1), net.along(first, 3)

    rights, lefts, cores = [[], []], [[], []], [[], []]
    between[0]()
    if not started:
        ring.first()
    for part in (0, 1):
        right, left = ends(part)
        for d in (1, 2, 3):
            second_copy(net, fulls, sems, part, d, True).wait_recv()
        rights[part].append(send(part, 0, 0, 3, right))
        lefts[part].append(send(part, 0, 1, 4, left))
        rights[part].append(send(part, 0, 1, 5, right))
        lefts[part].append(send(part, 0, 0, 6, left))
        cores[part].append(send(part, 0, None, 9, net.core()))
    between[1]()
    ring.step(1)
    between[2]()
    if started:
        ring.step(2)
    for part in (0, 1):
        right, left = ends(part)
        rights[part][0].wait_recv()
        rights[part].append(send(part, 3, 0, 7, right))
        lefts[part][0].wait_recv()
        lefts[part].append(send(part, 1, 1, 8, left))
        cores[part].append(send(part, 3, 0, 10, net.core()))
        cores[part].append(send(part, 1, 1, 11, net.core()))
    if not started:
        ring.step(2)
    between[3]()
    ring.step(3)
    for part in (0, 1):
        rights[part][1].wait_recv()
        cores[part].append(send(part, 3, 1, 12, net.core()))
        lefts[part][1].wait_recv()
        cores[part].append(send(part, 1, 0, 13, net.core()))
    ring.step(4)
    for part in (0, 1):
        rights[part][2].wait_recv()
        cores[part].append(send(part, 2, 0, 14, net.core()))
        lefts[part][2].wait_recv()
        cores[part].append(send(part, 2, 1, 15, net.core()))
    for part in (0, 1):
        for copy in cores[part]:
            copy.wait_recv()
        for copy in rights[part] + lefts[part] + cores[part]:
            copy.wait_send()
        for d in (1, 2, 3):
            second_copy(net, fulls, sems, part, d, False).wait_send()
    ring.finish()


def line_copy(net, fulls, lines, part, d, z):
    block = fulls[part].at[net.spot("x"), net.spot("y"), net.c, jnp.minimum(z, 6)]
    return pltpu.make_async_remote_copy(
        src_ref=block, dst_ref=block, send_sem=lines[part].at[0, d - 1], recv_sem=lines[part].at[1, d - 1],
        device_id=net.along("z", d), device_id_type=MESH,
    )


def spread_line(net, fulls, outs, sems, lines, ring):
    def onward(part, z):
        block = fulls[part].at[net.spot("x"), net.spot("y"), net.c, jnp.minimum(z, 6)]
        for d in (2, 1, 3):
            push(block, block, sems[part].at[0, d - 1], sems[part].at[1, d - 1], net.along(ordered(part)[1], d))

    @pl.when(net.z != 7)
    def _():
        for part in (0, 1):
            fulls[part][net.spot("x"), net.spot("y"), net.c, net.z] = outs[part][...]
        for d in (4, 3, 5, 2, 6, 1, 7):
            for part in (0, 1):
                line_copy(net, fulls, lines, part, d, net.z).start()
        for part in (0, 1):
            onward(part, net.z)

    for d in (1, 7, 2, 6, 3, 5, 4):
        z = (net.z + 8 - d) % 8
        if d == 3:
            ring.first()

        @pl.when(z != 7)
        def _():
            for part in (0, 1):
                line_copy(net, fulls, lines, part, d, z).wait_recv()
                onward(part, z)


def drain_line(net, fulls, lines):
    @pl.when(net.z != 7)
    def _():
        for part in (0, 1):
            for d in range(1, 8):
                line_copy(net, fulls, lines, part, d, net.z).wait_send()


def share_owned(net, outs, owned, sems, pairs):
    half = net.x % 2
    partner = device(net.x + 1 - 2 * half, net.y, net.z, net.c)

    def block(part, z):
        return owned[part].at[half, jnp.minimum(z, 6)]

    def line_copy(part, d, z):
        return pltpu.make_async_remote_copy(
            src_ref=block(part, z), dst_ref=block(part, z), send_sem=sems[part].at[0, d - 1],
            recv_sem=sems[part].at[1, d - 1], device_id=net.along("z", d), device_id_type=MESH,
        )

    def pair_copy(part, d, z):
        return pltpu.make_async_remote_copy(
            src_ref=block(part, z), dst_ref=block(part, z), send_sem=pairs[part].at[0, d],
            recv_sem=pairs[part].at[1, d], device_id=partner, device_id_type=MESH,
        )

    for part in PARTS:
        @pl.when(net.z != 7)
        def _():
            owned[part][half, net.z] = outs[part][...]
            for d in (4, 3, 5, 2, 6, 1, 7):
                line_copy(part, d, net.z).start()
            pair_copy(part, 0, net.z).start()
    for d in (1, 7, 2, 6, 3, 5, 4):
        z = (net.z + 8 - d) % 8

        @pl.when(z != 7)
        def _():
            for part in PARTS:
                line_copy(part, d, z).wait_recv()
                pair_copy(part, d, z).start()
    for d in range(8):
        z = (net.z + 8 - d) % 8

        @pl.when(z != 7)
        def _():
            for part in PARTS:
                pair_copy(part, d, z).wait()
    for part in PARTS:
        @pl.when(net.z != 7)
        def _():
            for d in range(1, 8):
                line_copy(part, d, net.z).wait_send()


def loop(count, body):
    def step(i, carry):
        body(i)
        return carry

    lax.fori_loop(0, count, step, 0)


STARTS = (0, WIDTHS[0], WIDTHS[0] + WIDTHS[1])


def mean_signal(upstream, signal_mean):
    def step(i):
        at = pl.ds(pl.multiple_of(i * 64, 64), 64)
        mean = jnp.mean(upstream[at, :].astype(F32), axis=-1, keepdims=True)
        signal_mean[at, :] = jnp.broadcast_to(mean, (64, 128))

    loop(4, step)


def norm_patches(patches, normed, normed_t):
    def norm(i):
        at = pl.ds(pl.multiple_of(i * 32, 32), 32)
        rows = patches[at, :].astype(F32)
        centred = rows - jnp.mean(rows, axis=-1, keepdims=True)
        scale = lax.rsqrt(jnp.mean(centred * centred, axis=-1, keepdims=True) + 1e-06)
        normed[at, :] = (centred * scale).astype(BF)

    loop(8, norm)

    def turn(j):
        block = normed[:, pl.ds(pl.multiple_of(j * 128, 128), 128)]
        normed_t[pl.ds(j * 8, 8)] = block.T.reshape(8, 16, SEQ)

    loop(14, turn)


def attend(queries, keys, attention, attention_t, heads):
    for h in heads:
        q = queries[:, h * HD:(h + 1) * HD]
        k = keys[:, h * HD:(h + 1) * HD]
        scores = lax.dot_general(q, k, (((1,), (1,)), ((), ())), preferred_element_type=F32) * HD ** (-0.5)
        expo = jnp.exp(scores - jnp.max(scores, axis=-1, keepdims=True))
        weights = (expo / jnp.sum(expo, axis=-1, keepdims=True)).astype(BF)
        attention[h] = weights
        attention_t[h] = weights.T


def project(normed, fulls, write):
    for part in PARTS:
        w, at = WIDTHS[part], STARTS[part]
        total = jnp.dot(normed[:, :HID], fulls[part][0].reshape(HID, w), preferred_element_type=F32)
        total = total + jnp.dot(normed[:, HID:], fulls[part][1].reshape(HID, w), preferred_element_type=F32)
        write(slice(at, at + w), total)


def unfold(full, i):
    both = full[2 + i // 4, i % 4].astype(F32)
    both = both.reshape(2, 112, both.shape[-1])
    left = jnp.concatenate([both[0, :56], both[1, :56]], axis=0)
    right = jnp.concatenate([both[0, 56:], both[1, 56:]], axis=0)
    return left, right


def set_output(fulls, output, stretch):
    def step(i):
        for part in PARTS:
            w = WIDTHS[part]
            for half, rows in enumerate(unfold(fulls[part], i)):
                at = (pl.ds(i * BLOCKS, BLOCKS), slice(None), slice(half * HID + STARTS[part], half * HID + STARTS[part] + w))
                if stretch is not None:
                    rows = output[at].astype(F32).reshape(112, w) + stretch * rows
                output[at] = rows.astype(BF).reshape(BLOCKS, 16, w)

    loop(8, step)


def sum_squares(fulls):
    def step(i, totals):
        out = []
        for part in PARTS:
            block = fulls[part][i // 4, i % 4].astype(F32)
            block = block.reshape(2 * BLOCKS, 16, WIDTHS[part])
            out.append(totals[part] + jnp.sum(block * block, axis=0))
        return tuple(out)

    totals = lax.fori_loop(0, 16, step, tuple(jnp.zeros((16, w), F32) for w in WIDTHS))
    parts = [jnp.sum(jnp.sum(t, axis=0, keepdims=True), axis=1, keepdims=True) for t in totals]
    return parts[0] + parts[1] + parts[2]


def backward(patches, upstream, signal_mean, attention, attention_t, output, values, mixed, mixed_t, outcome, d_outcome, d_values):
    for h in range(HEADS):
        at = slice(h * HD, (h + 1) * HD)
        mixed[:, at] = jnp.dot(attention[h], values[:, at], preferred_element_type=F32).astype(BF)

    def turn(j):
        block = mixed[:, pl.ds(pl.multiple_of(j * 128, 128), 128)].astype(F32)
        mixed_t[pl.ds(j * 16, 16)] = block.T.reshape(16, 8, SEQ)

    loop(7, turn)

    outcome[...] = patches[...].astype(F32) + jnp.dot(
        mixed[...], output[...].reshape(HID, D), preferred_element_type=F32
    )

    def rows(i):
        at = pl.ds(pl.multiple_of(i * 128, 128), 128)
        tiles = [slice(j * 128, j * 128 + 128) for j in range(14)]
        total = outcome[at, tiles[0]]
        for tile in tiles[1:]:
            total = total + outcome[at, tile]
        mean = jnp.sum(total, axis=-1, keepdims=True) / D
        squares, cross = jnp.zeros((128, 128), F32), jnp.zeros((128, 128), F32)
        for tile in tiles:
            centred = outcome[at, tile] - mean
            squares = squares + centred * centred
            cross = cross + centred * upstream[at, tile].astype(F32)
        inverse = lax.rsqrt(jnp.sum(squares, axis=-1, keepdims=True) / D + 1e-06)
        slope = inverse * inverse * (jnp.sum(cross, axis=-1, keepdims=True) / D)
        level = signal_mean[at, 0:1]
        for tile in tiles:
            centred = outcome[at, tile] - mean
            d_outcome[at, tile] = (inverse * (upstream[at, tile].astype(F32) - level - centred * slope)).astype(BF)

    loop(2, rows)
    d_mixed = lax.dot_general(
        d_outcome[...], output[...].reshape(HID, D), (((1,), (1,)), ((), ())), preferred_element_type=F32
    ).astype(BF)
    values[...] = d_mixed
    for h in range(HEADS):
        at = slice(h * HD, (h + 1) * HD)
        d_values[:, at] = jnp.dot(attention_t[h], values[:, at], preferred_element_type=F32).astype(BF)


def write_grads(core, normed_t, mixed_t, d_outcome, d_values, grads):
    for hi in (0, 1):
        rows = [mixed_t[pl.ds((hi * 8 + y * 2 + core) * BLOCKS, BLOCKS)].reshape(56, SEQ) for y in range(4)]
        left = jnp.concatenate(rows, axis=0).astype(BF)
        got = jnp.dot(left, d_outcome[...], preferred_element_type=F32).reshape(4, 56, D)
        got = jnp.concatenate([got[:, :, :HID], got[:, :, HID:]], axis=1).astype(BF).reshape(4, BLOCKS, 16, HID)
        for part in PARTS:
            grads[part][2 + hi, :, core] = got[..., STARTS[part]:STARTS[part] + WIDTHS[part]]
    for hi in (0, 1):
        rows = [normed_t[pl.ds((hi * 8 + y * 2 + core) * BLOCKS, BLOCKS)] for y in range(4)]
        left = jnp.concatenate(rows, axis=0).reshape(448, SEQ)
        got = jnp.dot(left, d_values[...], preferred_element_type=F32).astype(BF).reshape(4, BLOCKS, 16, HID)
        for part in PARTS:
            grads[part][hi, :, core] = got[..., STARTS[part]:STARTS[part] + WIDTHS[part]]


def kernel(
    patches_hbm, queries_hbm, keys_hbm, upstream_hbm, value_rows, output_rows,
    value_grad, output_grad,
    patches, queries, keys, upstream, own, signal_mean, load_sem,
    full_a, full_b, full_c, grad_a, grad_b, grad_c, owned_a, owned_b, owned_c, out_a, out_b, out_c,
    normed, normed_t, attention, attention_t, base, values, output,
    mixed, mixed_t, outcome, d_outcome, d_values,
    sem_a, sem_b, sem_c, line_a, line_b, _, last_a, last_b, last_c, pair_a, pair_b, pair_c, *scratch,
):
    net = Net()
    greeted = net.greet()
    loads = []
    for i, pair in enumerate(((patches_hbm, patches), (queries_hbm, queries), (keys_hbm, keys), (upstream_hbm, upstream))):
        load = pltpu.make_async_copy(*pair, load_sem.at[i])
        load.start()
        loads.append(load)
    fulls, grads, outs = (full_a, full_b, full_c), (grad_a, grad_b, grad_c), (out_a, out_b, out_c)
    owned, sems, lines = (owned_a, owned_b, owned_c), (sem_a, sem_b), (line_a, line_b)

    @pl.when(net.x % 2 == 0)
    def _():
        own[...] = value_rows[...].astype(BF).reshape(BLOCKS, 16, HID)

    @pl.when(net.x % 2 == 1)
    def _():
        rows = jnp.concatenate([output_rows[:, :HID], output_rows[:, HID:]], axis=0)
        own[...] = rows.astype(BF).reshape(BLOCKS, 16, HID)

    for part in (0, 1):
        fulls[part][net.spot("x"), net.spot("y"), net.c] = own[:, :, STARTS[part]:STARTS[part] + WIDTHS[part]]

    @pl.when(net.z != 7)
    def _():
        full_c[net.spot("x"), net.spot("y"), net.c, net.z] = own[net.z, :, STARTS[2]:]

    net.meet(greeted)
    for part in (0, 1):
        for d in (2, 1, 3):
            second_copy(net, fulls, sems, part, d, False).start()
    ring = LineLast(net, full_c, sem_c)
    ring.start()

    def prepare():
        loads[0].wait()
        norm_patches(patches, normed, normed_t)

    def first_heads():
        for load in loads[1:]:
            load.wait()
        attend(queries, keys, attention, attention_t, range(3))
        mean_signal(upstream, signal_mean)

    gather_all(
        net, fulls, sems, ring,
        (
            prepare,
            first_heads,
            lambda: attend(queries, keys, attention, attention_t, range(3, 6)),
            lambda: attend(queries, keys, attention, attention_t, range(6, 8)),
        ),
    )
    set_output(fulls, output, None)

    def write_base(at, total):
        base[:, at] = total
        values[:, at] = total.astype(BF)

    project(normed, fulls, write_base)

    def back():
        backward(patches, upstream, signal_mean, attention, attention_t, output, values, mixed, mixed_t, outcome, d_outcome, d_values)

    def make(core):
        write_grads(core, normed_t, mixed_t, d_outcome, d_values, grads)

    back()
    drain = reduce_all(net, grads, outs, scratch, make)

    @pl.when(net.z != 7)
    def _():
        full_c[net.spot("x"), net.spot("y"), net.c, net.z] = out_c[...]

    ring.start()
    spread_line(net, fulls, outs, sems, lines, ring)
    gather_all(net, fulls, sems, ring, started=True)
    drain_line(net, fulls, lines)
    drain()
    mean_square = sum_squares(fulls) / (2.0 * D * HID)
    stretch = rho_scale / jnp.sqrt(mean_square + 1e-06)
    set_output(fulls, output, stretch)

    def write_values(at, total):
        values[:, at] = (base[:, at] + stretch * total).astype(BF)

    project(normed, fulls, write_values)
    back()
    drain = reduce_all(net, grads, outs, scratch, make)
    share_owned(net, outs, owned, (last_a, last_b, last_c), (pair_a, pair_b, pair_c))
    drain()
    for part in PARTS:
        w, at = WIDTHS[part], STARTS[part]
        value_grad[:, :, at:at + w] = owned[part][0]
        rows = owned[part][1].astype(F32).reshape(112, w)
        output_grad[:, at:at + w] = rows[:56]
        output_grad[:, HID + at:HID + at + w] = rows[56:]


def vmem(n):
    return [pl.BlockSpec(memory_space=pltpu.VMEM)] * n


def gradients(patches, queries, keys, upstream, value_weight, output_weight):
    rows = patches.shape[0]
    return pl.pallas_call(
        kernel,
        out_shape=(
            jax.ShapeDtypeStruct((BLOCKS, 16, HID), BF),
            jax.ShapeDtypeStruct((56, D), F32),
        ),
        in_specs=[pl.BlockSpec(memory_space=pl.ANY)] * 4 + vmem(2),
        out_specs=vmem(2),
        scratch_shapes=(
            [pltpu.VMEM((rows, w), BF) for w in (D, HID, HID, D)]
            + [pltpu.VMEM((BLOCKS, 16, HID), BF), pltpu.VMEM((rows, 128), F32), pltpu.SemaphoreType.DMA((4,))]
            + [pltpu.VMEM((4, 4, 2, BLOCKS, 16, w), BF) for w in WIDTHS]
            + [pltpu.VMEM((4, 4, 2, BLOCKS, 16, w), BF) for w in WIDTHS]
            + [pltpu.VMEM((2, BLOCKS, 16, w), BF) for w in WIDTHS]
            + [pltpu.VMEM((16, w), BF) for w in WIDTHS]
            + [
                pltpu.VMEM((rows, D), BF),
                pltpu.VMEM((112, 16, rows), BF),
                pltpu.VMEM((HEADS, SEQ, SEQ), BF),
                pltpu.VMEM((HEADS, SEQ, SEQ), BF),
                pltpu.VMEM((rows, HID), F32),
                pltpu.VMEM((rows, HID), BF),
                pltpu.VMEM((56, 16, D), BF),
                pltpu.VMEM((rows, HID), BF),
                pltpu.VMEM((112, 8, rows), F32),
                pltpu.VMEM((rows, D), F32),
                pltpu.VMEM((rows, D), BF),
                pltpu.VMEM((rows, HID), BF),
            ]
            + gather_scratch()
            + [pltpu.SemaphoreType.DMA((2, 7)) for _ in WIDTHS]
            + [pltpu.SemaphoreType.DMA((2, 7)) for _ in WIDTHS]
            + [pltpu.SemaphoreType.DMA((2, 8)) for _ in WIDTHS]
            + reduce_scratch()
        ),
        name="gradients",
        compiler_params=pltpu.CompilerParams(
            collective_id=0, has_side_effects=True, vmem_limit_bytes=60 * 2**20
        ),
    )(patches, queries, keys, upstream, value_weight, output_weight)


def adam_update(weight, first, second, gradient):
    first_new = beta_one * first + (1.0 - beta_one) * gradient
    second_new = beta_two * second + (1.0 - beta_two) * gradient * gradient
    update = (
        first_new / first_fix / (jnp.sqrt(second_new / second_fix) + adam_eps)
        + weight_decay * weight
    )
    return (weight - learn_rate * update, first_new, second_new)


def on_device(
    patches,
    queries,
    keys,
    upstream,
    value_weight,
    output_weight,
    value_first,
    output_first,
    value_second,
    output_second,
):
    value_grad, output_grad = gradients(patches, queries, keys, upstream, value_weight, output_weight)
    value_new, value_first_new, value_second_new = adam_update(
        value_weight, value_first, value_second, value_grad.reshape(112, HID).astype(F32)
    )
    output_new, output_first_new, output_second_new = adam_update(
        output_weight, output_first, output_second, output_grad
    )
    return (
        value_new,
        output_new,
        value_first_new,
        output_first_new,
        value_second_new,
        output_second_new,
    )


def solution(mesh):
    return jax.shard_map(
        on_device,
        mesh=mesh,
        in_specs=(P(("dp", "fsdp"), None),) * 4 + (P("fsdp", None),) * 6,
        out_specs=(P("fsdp", None),) * 6,
        check_vma=False,
    )
```

```python
import jax
import jax.numpy as jnp
from jax import lax
from jax.experimental import pallas as pl
from jax.experimental.pallas import tpu as pltpu
from jax.sharding import PartitionSpec as P

HEADS = 8
HD = 112
SEQ = 256
D = 1792
HID = 896
BLOCKS = 7
WIDTHS = (384, 384, 128)
PARTS = (0, 1, 2)
MESH = pl.DeviceIdType.MESH
BF = jnp.bfloat16
F32 = jnp.float32


learn_rate = 0.001
weight_decay = 0.1
beta_one = 0.9
beta_two = 0.999
adam_eps = 1e-08
first_fix = 0.9999734386011124
second_fix = 0.0952078528862911
rho_scale = 0.05


def place():
    dp = lax.axis_index("dp")
    fs = lax.axis_index("fsdp")
    return (fs // 8) * 2 + dp // 8, (fs // 2) % 4, dp % 8, fs % 2


def device(x, y, z, c):
    return ((x % 2) * 8 + z, (x // 2) * 8 + y * 2 + c)


def slot(x):
    return (x % 2) * 2 + x // 2


class Net:
    def __init__(self):
        self.x, self.y, self.z, self.c = place()

    def core(self):
        return device(self.x, self.y, self.z, 1 - self.c)

    def along(self, axis, step):
        if axis == "x":
            return device((self.x + step) % 4, self.y, self.z, self.c)
        if axis == "y":
            return device(self.x, (self.y + step) % 4, self.z, self.c)
        return device(self.x, self.y, (self.z + step) % 8, self.c)

    def across(self, i, j):
        return device((self.x + i) % 4, (self.y + j) % 4, self.z, self.c)

    def spot(self, axis, step=0):
        if axis == "x":
            return slot((self.x + step) % 4)
        if axis == "y":
            return (self.y + step) % 4
        return (self.z + step) % 8

    def greet(self):
        sem = pltpu.get_barrier_semaphore()
        targets = [self.core()]
        targets += [self.along("x", s) for s in (1, 2, 3)]
        targets += [self.along("y", s) for s in (1, 2, 3)]
        targets += [self.along("z", s) for s in range(1, 8)]
        targets += [self.across(i, j) for i in (1, 2, 3) for j in (1, 2, 3)]
        for t in targets:
            pl.semaphore_signal(sem, inc=1, device_id=t, device_id_type=MESH)
        return len(targets)

    def meet(self, count):
        pl.semaphore_wait(pltpu.get_barrier_semaphore(), count)


def push(src, dst, send, recv, target):
    copy = pltpu.make_async_remote_copy(
        src_ref=src, dst_ref=dst, send_sem=send, recv_sem=recv, device_id=target, device_id_type=MESH
    )
    copy.start()
    return copy


def add_blocks(count, write, *reads):
    def step(i, carry):
        total = reads[0](i).astype(F32)
        for read in reads[1:]:
            total = total + read(i).astype(F32)
        write(i, total.astype(BF))
        return carry

    lax.fori_loop(0, count, step, 0)


def ordered(part):
    return ("x", "y") if part == 0 else ("y", "x")


def grid_at(ref, part, first, second):
    return ref.at[first, second] if part == 0 else ref.at[second, first]


def reduce_scratch():
    shapes = []
    for w in WIDTHS[:2]:
        shapes += [
            pltpu.VMEM((4, 4, BLOCKS, 16, w), BF),
            pltpu.VMEM((4, 4, BLOCKS, 16, w), BF),
            pltpu.VMEM((2, 2, BLOCKS, 16, w), BF),
            pltpu.VMEM((2, 4, BLOCKS, 16, w), BF),
            pltpu.VMEM((4, BLOCKS, 16, w), BF),
            pltpu.VMEM((3, BLOCKS, 16, w), BF),
            pltpu.VMEM((BLOCKS, 16, w), BF),
            pltpu.VMEM((7, 16, w), BF),
            pltpu.SemaphoreType.DMA((2, 4 + 2 + 4 + 3 + 7 + 3)),
        ]
    w = WIDTHS[2]
    return shapes + [
        pltpu.VMEM((4, 4, BLOCKS, 16, w), BF),
        pltpu.VMEM((4, 4, BLOCKS, 16, w), BF),
        pltpu.VMEM((2, 2, 4, 16, w), BF),
        pltpu.VMEM((2, 3, 4, 4, 16, w), BF),
        pltpu.VMEM((4, 4, 16, w), BF),
        pltpu.VMEM((15, 16, w), BF),
        pltpu.SemaphoreType.DMA((2, 1 + 8 + 15)),
    ]


ACROSS = [(i, j) for i in range(4) for j in range(4) if (i, j) != (0, 0)]


class LineFirst:
    def __init__(self, net, grads, out, scratch):
        self.net, self.grads, self.out = net, grads, out
        self.other, self.sums, self.far, self.ring, self.plane, self.from_plane, self.sem = scratch

    def exchange(self):
        net = self.net
        self.core = push(self.grads.at[:, :, 1 - net.c], self.other, self.sem.at[0, 0], self.sem.at[1, 0], net.core())

    def add_cores(self):
        net = self.net
        self.core.wait_recv()
        g, other, sums = self.grads, self.other, self.sums

        def write(i, v):
            sums[i // 4, i % 4] = v

        add_blocks(16, write, lambda i: g[i // 4, i % 4, net.c], lambda i: other[i // 4, i % 4])

    def copy(self, k, way, j):
        j = jnp.minimum(j, 6)
        if k == 0:
            src, dst = self.sums.at[pl.ds(2 * way, 2), :, j], self.far.at[way]
        else:
            src, dst = self.sums.at[:, :, j], self.ring.at[way, k - 1]
        at = 1 + 2 * k + way
        return pltpu.make_async_remote_copy(
            src_ref=src, dst_ref=dst, send_sem=self.sem.at[0, at], recv_sem=self.sem.at[1, at],
            device_id=self.net.along("z", (1, 7)[way]), device_id_type=MESH,
        )

    def sent(self, k, way):
        return (self.net.z + ((4 - k) if way == 0 else (4 + k))) % 8

    def got(self, k, way):
        return (self.net.z + ((3 - k) if way == 0 else (5 + k))) % 8

    def send(self, k):
        for way in (0, 1):
            j = self.sent(k, way)

            @pl.when(j != 7)
            def _():
                self.copy(k, way, j).start()

    def receive(self, k):
        for way in (0, 1):
            j = self.got(k, way)
            at = jnp.minimum(j, 6)

            @pl.when(j != 7)
            def _():
                self.copy(k, way, j).wait_recv()
                if k == 0:
                    rows = slice(2 * way, 2 * way + 2)
                    self.sums[rows, :, at] = (self.sums[rows, :, at].astype(F32) + self.far[way].astype(F32)).astype(BF)
                elif k < 3:
                    self.sums[:, :, at] = (self.sums[:, :, at].astype(F32) + self.ring[way, k - 1].astype(F32)).astype(BF)

    def plane_copy(self, e):
        i, j = ACROSS[e]
        net = self.net
        return pltpu.make_async_remote_copy(
            src_ref=self.plane.at[net.spot("x", i), net.spot("y", j)], dst_ref=self.from_plane.at[e],
            send_sem=self.sem.at[0, 9 + e], recv_sem=self.sem.at[1, 9 + e], device_id=net.across(i, j), device_id_type=MESH,
        )

    def cross(self):
        net = self.net

        @pl.when(net.z != 7)
        def _():
            self.plane[...] = (
                self.sums[:, :, net.z].astype(F32) + self.ring[0, 2].astype(F32) + self.ring[1, 2].astype(F32)
            ).astype(BF)
            for e in range(15):
                self.plane_copy(e).start()

    def finish(self):
        net = self.net

        @pl.when(net.z != 7)
        def _():
            for e in range(15):
                self.plane_copy(e).wait_recv()
            total = self.plane[net.spot("x"), net.spot("y")].astype(F32)
            for e in range(15):
                total = total + self.from_plane[e].astype(F32)
            self.out[...] = total.astype(BF)

    def drain(self):
        self.core.wait_send()
        for k in range(4):
            for way in (0, 1):
                j = self.sent(k, way)

                @pl.when(j != 7)
                def _():
                    self.copy(k, way, j).wait_send()

        @pl.when(self.net.z != 7)
        def _():
            for e in range(15):
                self.plane_copy(e).wait_send()


def reduce_all(net, grads, outs, scratch, make):
    make(1 - net.c)
    ring = LineFirst(net, grads[2], outs[2], scratch[18:])
    state = []
    for part in (0, 1):
        state.append(scratch[part * 9:part * 9 + 9])
    cores = [[], []]
    for step in (2, 1, 3, 0):
        for part in (0, 1):
            other, sums, far, mine, _, _, _, _, sem = state[part]
            first = ordered(part)[0]
            i = net.spot(first, step)
            j = len(cores[part])
            if part == 0:
                src, dst = grads[part].at[i, :, 1 - net.c], other.at[i]
            else:
                src, dst = grads[part].at[:, i, 1 - net.c], other.at[:, i]
            cores[part].append(push(src, dst, sem.at[0, j], sem.at[1, j], net.core()))
        if step == 2:
            ring.exchange()
    make(net.c)

    def half_of(ref, part, i, h):
        return ref.at[i, pl.ds(2 * h, 2)] if part == 0 else ref.at[pl.ds(2 * h, 2), i]

    near = [[None] * 6, [None] * 6]
    for j, step in enumerate((2, 1, 3, 0)):
        for part in (0, 1):
            other, sums, far, mine, _, _, _, _, sem = state[part]
            first = ordered(part)[0]
            i = net.spot(first, step)
            cores[part][j].wait_recv()
            g = grads[part]
            if part == 0:
                def write(k, v):
                    sums[i, k] = v
                add_blocks(4, write, lambda k: g[i, k, net.c], lambda k: other[i, k])
            else:
                def write(k, v):
                    sums[k, i] = v
                add_blocks(4, write, lambda k: g[k, i, net.c], lambda k: other[k, i])
            right, left = net.along(first, 1), net.along(first, 3)
            if step == 2:
                near[part][0] = push(half_of(sums, part, i, 0), far.at[0], sem.at[0, 4], sem.at[1, 4], right)
                near[part][1] = push(half_of(sums, part, i, 1), far.at[1], sem.at[0, 5], sem.at[1, 5], left)
            if step == 1:
                near[part][2] = push(half_of(sums, part, i, 1), mine.at[0, pl.ds(2, 2)], sem.at[0, 6], sem.at[1, 6], right)
            if step == 3:
                near[part][3] = push(half_of(sums, part, i, 0), mine.at[1, pl.ds(0, 2)], sem.at[0, 7], sem.at[1, 7], left)
        if j == 0:
            ring.add_cores()
            ring.send(0)
        if j == 2:
            ring.receive(0)
            ring.send(1)
    for part in (0, 1):
        other, sums, far, mine, _, _, _, _, sem = state[part]
        first = ordered(part)[0]
        right, left = net.along(first, 1), net.along(first, 3)
        r, l = net.spot(first, 1), net.spot(first, 3)
        near[part][0].wait_recv()
        if part == 0:
            def write(k, v):
                sums[r, k] = v
            add_blocks(2, write, lambda k: sums[r, k], lambda k: far[0, k])
        else:
            def write(k, v):
                sums[k, r] = v
            add_blocks(2, write, lambda k: sums[k, r], lambda k: far[0, k])
        near[part][4] = push(half_of(sums, part, r, 0), mine.at[0, pl.ds(0, 2)], sem.at[0, 8], sem.at[1, 8], right)
        near[part][1].wait_recv()
        if part == 0:
            def write(k, v):
                sums[l, k + 2] = v
            add_blocks(2, write, lambda k: sums[l, k + 2], lambda k: far[1, k])
        else:
            def write(k, v):
                sums[k + 2, l] = v
            add_blocks(2, write, lambda k: sums[k + 2, l], lambda k: far[1, k])
        near[part][5] = push(half_of(sums, part, l, 1), mine.at[1, pl.ds(2, 2)], sem.at[0, 9], sem.at[1, 9], left)
    for k in (1, 2):
        ring.receive(k)
        ring.send(k + 1)
    second_copies = [[], []]
    for part in (0, 1):
        other, sums, far, mine, row, from_row, _, _, sem = state[part]
        first, second = ordered(part)
        me = net.spot(first)
        for k in (2, 3, 4, 5):
            near[part][k].wait_recv()

        def write(k, v):
            row[k] = v
        if part == 0:
            add_blocks(4, write, lambda k: sums[me, k], lambda k: mine[0, k], lambda k: mine[1, k])
        else:
            add_blocks(4, write, lambda k: sums[k, me], lambda k: mine[0, k], lambda k: mine[1, k])
        for g, blocks in enumerate((pl.ds(0, 4), pl.ds(4, 3))):
            for d in (2, 1, 3):
                at = (9 if g == 0 else 19) + d
                second_copies[part].append(
                    push(row.at[net.spot(second, d), blocks], from_row.at[d - 1, blocks], sem.at[0, at], sem.at[1, at], net.along(second, d))
                )
    ring.receive(3)
    ring.cross()
    for g, (start, count) in enumerate(((0, 4), (4, 3))):
        for part in (0, 1):
            other, sums, far, mine, row, from_row, line, from_line, sem = state[part]
            me = net.spot(ordered(part)[1])
            for copy in second_copies[part][3 * g:3 * g + 3]:
                copy.wait_recv()

            def write(k, v):
                line[start + k] = v
            add_blocks(
                count, write, lambda k: row[me, start + k], lambda k: from_row[0, start + k],
                lambda k: from_row[1, start + k], lambda k: from_row[2, start + k],
            )
            for d in (4, 3, 5, 2, 6, 1, 7):
                z = net.spot("z", d)

                @pl.when((z >= start) & (z < start + count))
                def _():
                    push(line.at[z], from_line.at[d - 1], sem.at[0, 12 + d], sem.at[1, 12 + d], net.along("z", d))
    ring.finish()
    for part in (0, 1):
        other, sums, far, mine, row, from_row, line, from_line, sem = state[part]

        @pl.when(net.z != 7)
        def _():
            for d in range(1, 8):
                pltpu.make_async_remote_copy(
                    src_ref=line.at[0], dst_ref=from_line.at[d - 1], send_sem=sem.at[0, 12 + d], recv_sem=sem.at[1, 12 + d],
                    device_id=net.along("z", d), device_id_type=MESH,
                ).wait_recv()
            total = line[net.z].astype(F32)
            for d in range(7):
                total = total + from_line[d].astype(F32)
            outs[part][...] = total.astype(BF)

    def drain():
        ring.drain()
        for part in (0, 1):
            other, sums, far, mine, row, from_row, line, from_line, sem = state[part]
            for copy in cores[part] + near[part] + second_copies[part]:
                copy.wait_send()
            for d in range(1, 8):
                @pl.when(net.spot("z", d) != 7)
                def _():
                    pltpu.make_async_remote_copy(
                        src_ref=line.at[0], dst_ref=from_line.at[d - 1], send_sem=sem.at[0, 12 + d], recv_sem=sem.at[1, 12 + d],
                        device_id=net.along("z", d), device_id_type=MESH,
                    ).wait_send()
    return drain


def gather_scratch():
    return [pltpu.SemaphoreType.DMA((2, 16)) for _ in WIDTHS[:2]] + [pltpu.SemaphoreType.DMA((2, 15 + 16 + 17))]


class LineLast:
    def __init__(self, net, full, sem):
        self.net, self.full, self.sem = net, full, sem

    def own(self, e):
        i, j = ACROSS[e]
        net = self.net
        block = self.full.at[net.spot("x"), net.spot("y"), net.c, jnp.minimum(net.z, 6)]
        return pltpu.make_async_remote_copy(
            src_ref=block, dst_ref=block, send_sem=self.sem.at[0, e], recv_sem=self.sem.at[1, e],
            device_id=net.across(i, j), device_id_type=MESH,
        )

    def start(self):
        @pl.when(self.net.z != 7)
        def _():
            for e in range(15):
                self.own(e).start()

    def block(self, j, h):
        return self.full.at[pl.ds(2 * h, 2), :, self.net.c, jnp.minimum(j, 6)]

    def copy(self, k, way, j, h):
        at = 15 + 4 * (k - 1) + 2 * way + h
        block = self.block(j, h)
        return pltpu.make_async_remote_copy(
            src_ref=block, dst_ref=block, send_sem=self.sem.at[0, at], recv_sem=self.sem.at[1, at],
            device_id=self.net.along("z", (1, 7)[way]), device_id_type=MESH,
        )

    def core(self, k, way, j, h):
        at = 31 if k == 0 else 32 + 4 * (k - 1) + 2 * way + h
        block = self.full.at[:, :, self.net.c, jnp.minimum(j, 6)] if k == 0 else self.block(j, h)
        return pltpu.make_async_remote_copy(
            src_ref=block, dst_ref=block, send_sem=self.sem.at[0, at], recv_sem=self.sem.at[1, at],
            device_id=self.net.core(), device_id_type=MESH,
        )

    def halves(self, k, way):
        return (way,) if k == 4 else (way, 1 - way)

    def sent(self, k, way):
        return (self.net.z + ((9 - k) if way == 0 else (k - 1))) % 8

    def got(self, k, way):
        return (self.net.z + ((8 - k) if way == 0 else k)) % 8

    def first(self):
        net = self.net

        @pl.when(net.z != 7)
        def _():
            for e in range(15):
                self.own(e).wait_recv()
            for at in (0, 1):
                for way in (0, 1):
                    self.copy(1, way, net.z, self.halves(1, way)[at]).start()
            self.core(0, 0, net.z, 0).start()

    def step(self, k):
        for at in range(len(self.halves(k, 0))):
            for way in (0, 1):
                h = self.halves(k, way)[at]
                j = self.got(k, way)

                @pl.when(j != 7)
                def _():
                    self.copy(k, way, j, h).wait_recv()
                    if k < 4 and h in self.halves(k + 1, way):
                        self.copy(k + 1, way, j, h).start()
                    self.core(k, way, j, h).start()

    def finish(self):
        net = self.net

        @pl.when(net.z != 7)
        def _():
            self.core(0, 0, net.z, 0).wait()
            for e in range(15):
                self.own(e).wait_send()

        for k in (1, 2, 3, 4):
            for way in (0, 1):
                for h in self.halves(k, way):
                    j, i = self.got(k, way), self.sent(k, way)

                    @pl.when(j != 7)
                    def _():
                        self.core(k, way, j, h).wait()

                    @pl.when(i != 7)
                    def _():
                        self.copy(k, way, i, h).wait_send()


def second_copy(net, fulls, sems, part, d, source):
    second = ordered(part)[1]
    x, y = net.spot("x"), net.spot("y")
    if source:
        x = net.spot("x", 4 - d) if second == "x" else x
        y = net.spot("y", 4 - d) if second == "y" else y
    chunk = fulls[part].at[x, y, net.c]
    return pltpu.make_async_remote_copy(
        src_ref=chunk, dst_ref=chunk, send_sem=sems[part].at[0, d - 1], recv_sem=sems[part].at[1, d - 1],
        device_id=net.along(second, d), device_id_type=MESH,
    )


def gather_all(net, fulls, sems, ring, between=(), started=False):
    between = list(between) + [lambda: None] * 4

    def piece(part, i, h):
        at = slice(None) if h is None else pl.ds(2 * h, 2)
        return fulls[part].at[i, at, net.c] if part == 0 else fulls[part].at[at, i, net.c]

    def send(part, step, h, at, to):
        block = piece(part, net.spot(ordered(part)[0], step), h)
        return push(block, block, sems[part].at[0, at], sems[part].at[1, at], to)

    def ends(part):
        first = ordered(part)[0]
        return net.along(first, 1), net.along(first, 3)

    rights, lefts, cores = [[], []], [[], []], [[], []]
    between[0]()
    if not started:
        ring.first()
    for part in (0, 1):
        right, left = ends(part)
        for d in (1, 2, 3):
            second_copy(net, fulls, sems, part, d, True).wait_recv()
        rights[part].append(send(part, 0, 0, 3, right))
        lefts[part].append(send(part, 0, 1, 4, left))
        rights[part].append(send(part, 0, 1, 5, right))
        lefts[part].append(send(part, 0, 0, 6, left))
        cores[part].append(send(part, 0, None, 9, net.core()))
    between[1]()
    ring.step(1)
    between[2]()
    if started:
        ring.step(2)
    for part in (0, 1):
        right, left = ends(part)
        rights[part][0].wait_recv()
        rights[part].append(send(part, 3, 0, 7, right))
        lefts[part][0].wait_recv()
        lefts[part].append(send(part, 1, 1, 8, left))
        cores[part].append(send(part, 3, 0, 10, net.core()))
        cores[part].append(send(part, 1, 1, 11, net.core()))
    if not started:
        ring.step(2)
    between[3]()
    ring.step(3)
    for part in (0, 1):
        rights[part][1].wait_recv()
        cores[part].append(send(part, 3, 1, 12, net.core()))
        lefts[part][1].wait_recv()
        cores[part].append(send(part, 1, 0, 13, net.core()))
    ring.step(4)
    for part in (0, 1):
        rights[part][2].wait_recv()
        cores[part].append(send(part, 2, 0, 14, net.core()))
        lefts[part][2].wait_recv()
        cores[part].append(send(part, 2, 1, 15, net.core()))
    for part in (0, 1):
        for copy in cores[part]:
            copy.wait_recv()
        for copy in rights[part] + lefts[part] + cores[part]:
            copy.wait_send()
        for d in (1, 2, 3):
            second_copy(net, fulls, sems, part, d, False).wait_send()
    ring.finish()


def line_copy(net, fulls, lines, part, d, z):
    block = fulls[part].at[net.spot("x"), net.spot("y"), net.c, jnp.minimum(z, 6)]
    return pltpu.make_async_remote_copy(
        src_ref=block, dst_ref=block, send_sem=lines[part].at[0, d - 1], recv_sem=lines[part].at[1, d - 1],
        device_id=net.along("z", d), device_id_type=MESH,
    )


def spread_line(net, fulls, outs, sems, lines, ring):
    def onward(part, z):
        block = fulls[part].at[net.spot("x"), net.spot("y"), net.c, jnp.minimum(z, 6)]
        for d in (2, 1, 3):
            push(block, block, sems[part].at[0, d - 1], sems[part].at[1, d - 1], net.along(ordered(part)[1], d))

    @pl.when(net.z != 7)
    def _():
        for part in (0, 1):
            fulls[part][net.spot("x"), net.spot("y"), net.c, net.z] = outs[part][...]
        for d in (4, 3, 5, 2, 6, 1, 7):
            for part in (0, 1):
                line_copy(net, fulls, lines, part, d, net.z).start()
        for part in (0, 1):
            onward(part, net.z)

    for d in (1, 7, 2, 6, 3, 5, 4):
        z = (net.z + 8 - d) % 8
        if d == 3:
            ring.first()

        @pl.when(z != 7)
        def _():
            for part in (0, 1):
                line_copy(net, fulls, lines, part, d, z).wait_recv()
                onward(part, z)


def drain_line(net, fulls, lines):
    @pl.when(net.z != 7)
    def _():
        for part in (0, 1):
            for d in range(1, 8):
                line_copy(net, fulls, lines, part, d, net.z).wait_send()


def share_owned(net, outs, owned, lines, pairs):
    half = net.x % 2
    partner = device(net.x + 1 - 2 * half, net.y, net.z, net.c)

    def copy(sems, at, z, target):
        block = owned.at[half, jnp.minimum(z, 6)]
        return pltpu.make_async_remote_copy(
            src_ref=block, dst_ref=block, send_sem=sems.at[0, at], recv_sem=sems.at[1, at], device_id=target, device_id_type=MESH,
        )

    @pl.when(net.z != 7)
    def _():
        for part in PARTS:
            owned[half, net.z, :, STARTS[part]:STARTS[part] + WIDTHS[part]] = outs[part][...]
        for d in (4, 3, 5, 2, 6, 1, 7):
            copy(lines, d - 1, net.z, net.along("z", d)).start()
        copy(pairs, 0, net.z, partner).start()

    for d in (1, 7, 2, 6, 3, 5, 4):
        z = (net.z + 8 - d) % 8

        @pl.when(z != 7)
        def _():
            copy(lines, d - 1, z, net.along("z", d)).wait_recv()
            copy(pairs, d, z, partner).start()

    for d in range(8):
        z = (net.z + 8 - d) % 8

        @pl.when(z != 7)
        def _():
            copy(pairs, d, z, partner).wait()

    @pl.when(net.z != 7)
    def _():
        for d in range(1, 8):
            copy(lines, d - 1, net.z, net.along("z", d)).wait_send()


def loop(count, body):
    def step(i, carry):
        body(i)
        return carry

    lax.fori_loop(0, count, step, 0)


STARTS = (0, WIDTHS[0], WIDTHS[0] + WIDTHS[1])


def mean_signal(upstream, signal_mean):
    def step(i):
        at = pl.ds(pl.multiple_of(i * 64, 64), 64)
        mean = jnp.mean(upstream[at, :].astype(F32), axis=-1, keepdims=True)
        signal_mean[at, :] = jnp.broadcast_to(mean, (64, 128))

    loop(4, step)


def norm_patches(patches, normed, normed_t):
    def norm(i):
        at = pl.ds(pl.multiple_of(i * 32, 32), 32)
        rows = patches[at, :].astype(F32)
        centred = rows - jnp.mean(rows, axis=-1, keepdims=True)
        scale = lax.rsqrt(jnp.mean(centred * centred, axis=-1, keepdims=True) + 1e-06)
        normed[at, :] = (centred * scale).astype(BF)

    loop(8, norm)

    def turn(j):
        block = normed[:, pl.ds(pl.multiple_of(j * 128, 128), 128)]
        normed_t[pl.ds(j * 8, 8)] = block.T.reshape(8, 16, SEQ)

    loop(14, turn)


def attend(queries, keys, attention, attention_t, heads):
    for h in heads:
        q = queries[:, h * HD:(h + 1) * HD]
        k = keys[:, h * HD:(h + 1) * HD]
        scores = lax.dot_general(q, k, (((1,), (1,)), ((), ())), preferred_element_type=F32) * HD ** (-0.5)
        expo = jnp.exp(scores - jnp.max(scores, axis=-1, keepdims=True))
        weights = (expo / jnp.sum(expo, axis=-1, keepdims=True)).astype(BF)
        attention[h] = weights
        attention_t[h] = weights.T


def project(normed, fulls, write):
    for part in PARTS:
        w, at = WIDTHS[part], STARTS[part]
        total = jnp.dot(normed[:, :HID], fulls[part][0].reshape(HID, w), preferred_element_type=F32)
        total = total + jnp.dot(normed[:, HID:], fulls[part][1].reshape(HID, w), preferred_element_type=F32)
        write(slice(at, at + w), total)


def unfold(full, i):
    both = full[2 + i // 4, i % 4].astype(F32)
    both = both.reshape(2, 112, both.shape[-1])
    left = jnp.concatenate([both[0, :56], both[1, :56]], axis=0)
    right = jnp.concatenate([both[0, 56:], both[1, 56:]], axis=0)
    return left, right


def set_output(fulls, output, stretch):
    def step(i):
        for part in PARTS:
            w = WIDTHS[part]
            for half, rows in enumerate(unfold(fulls[part], i)):
                at = (pl.ds(i * BLOCKS, BLOCKS), slice(None), slice(half * HID + STARTS[part], half * HID + STARTS[part] + w))
                if stretch is not None:
                    rows = output[at].astype(F32).reshape(112, w) + stretch * rows
                output[at] = rows.astype(BF).reshape(BLOCKS, 16, w)

    loop(8, step)


def sum_squares(fulls):
    def step(i, totals):
        out = []
        for part in PARTS:
            block = fulls[part][i // 4, i % 4].astype(F32)
            block = block.reshape(2 * BLOCKS, 16, WIDTHS[part])
            out.append(totals[part] + jnp.sum(block * block, axis=0))
        return tuple(out)

    totals = lax.fori_loop(0, 16, step, tuple(jnp.zeros((16, w), F32) for w in WIDTHS))
    parts = [jnp.sum(jnp.sum(t, axis=0, keepdims=True), axis=1, keepdims=True) for t in totals]
    return parts[0] + parts[1] + parts[2]


def backward(patches, upstream, signal_mean, attention, attention_t, output, values, mixed, mixed_t, outcome, d_outcome, d_values):
    for h in range(HEADS):
        at = slice(h * HD, (h + 1) * HD)
        mixed[:, at] = jnp.dot(attention[h], values[:, at], preferred_element_type=F32).astype(BF)

    mixed_t[...] = mixed[...].T.astype(F32).reshape(112, 8, SEQ)
    outcome[...] = patches[...].astype(F32) + jnp.dot(
        mixed[...], output[...].reshape(HID, D), preferred_element_type=F32
    )

    def rows(i):
        at = pl.ds(pl.multiple_of(i * 128, 128), 128)
        tiles = [slice(j * 128, j * 128 + 128) for j in range(14)]
        total = outcome[at, tiles[0]]
        for tile in tiles[1:]:
            total = total + outcome[at, tile]
        mean = jnp.sum(total, axis=-1, keepdims=True) / D
        squares, cross = jnp.zeros((128, 128), F32), jnp.zeros((128, 128), F32)
        for tile in tiles:
            centred = outcome[at, tile] - mean
            squares = squares + centred * centred
            cross = cross + centred * upstream[at, tile].astype(F32)
        inverse = lax.rsqrt(jnp.sum(squares, axis=-1, keepdims=True) / D + 1e-06)
        slope = inverse * inverse * (jnp.sum(cross, axis=-1, keepdims=True) / D)
        level = signal_mean[at, 0:1]
        for tile in tiles:
            centred = outcome[at, tile] - mean
            d_outcome[at, tile] = (inverse * (upstream[at, tile].astype(F32) - level - centred * slope)).astype(BF)

    loop(2, rows)
    d_mixed = lax.dot_general(
        d_outcome[...], output[...].reshape(HID, D), (((1,), (1,)), ((), ())), preferred_element_type=F32
    ).astype(BF)
    values[...] = d_mixed
    for h in range(HEADS):
        at = slice(h * HD, (h + 1) * HD)
        d_values[:, at] = jnp.dot(attention_t[h], values[:, at], preferred_element_type=F32).astype(BF)


def write_grads(core, normed_t, mixed_t, d_outcome, d_values, grads):
    for hi in (0, 1):
        rows = [mixed_t[pl.ds((hi * 8 + y * 2 + core) * BLOCKS, BLOCKS)].reshape(56, SEQ) for y in range(4)]
        left = jnp.concatenate(rows, axis=0).astype(BF)
        got = jnp.dot(left, d_outcome[...], preferred_element_type=F32).reshape(4, 56, D)
        got = jnp.concatenate([got[:, :, :HID], got[:, :, HID:]], axis=1).astype(BF).reshape(4, BLOCKS, 16, HID)
        for part in PARTS:
            grads[part][2 + hi, :, core] = got[..., STARTS[part]:STARTS[part] + WIDTHS[part]]
    for hi in (0, 1):
        rows = [normed_t[pl.ds((hi * 8 + y * 2 + core) * BLOCKS, BLOCKS)] for y in range(4)]
        left = jnp.concatenate(rows, axis=0).reshape(448, SEQ)
        got = jnp.dot(left, d_values[...], preferred_element_type=F32).astype(BF).reshape(4, BLOCKS, 16, HID)
        for part in PARTS:
            grads[part][hi, :, core] = got[..., STARTS[part]:STARTS[part] + WIDTHS[part]]


def kernel(
    patches_hbm, queries_hbm, keys_hbm, upstream_hbm, value_rows, output_rows,
    value_grad, output_grad,
    patches, queries, keys, upstream, own, signal_mean, load_sem,
    full_a, full_b, full_c, grad_a, grad_b, grad_c, owned, out_a, out_b, out_c,
    normed, normed_t, attention, attention_t, base, values, output,
    mixed, mixed_t, outcome, d_outcome, d_values,
    sem_a, sem_b, sem_c, line_a, line_b, last, pairs, *scratch,
):
    net = Net()
    greeted = net.greet()
    loads = []
    for i, pair in enumerate(((patches_hbm, patches), (queries_hbm, queries), (keys_hbm, keys), (upstream_hbm, upstream))):
        load = pltpu.make_async_copy(*pair, load_sem.at[i])
        load.start()
        loads.append(load)
    fulls, grads, outs = (full_a, full_b, full_c), (grad_a, grad_b, grad_c), (out_a, out_b, out_c)
    sems, lines = (sem_a, sem_b), (line_a, line_b)

    @pl.when(net.x % 2 == 0)
    def _():
        own[...] = value_rows[...].astype(BF).reshape(BLOCKS, 16, HID)

    @pl.when(net.x % 2 == 1)
    def _():
        rows = jnp.concatenate([output_rows[:, :HID], output_rows[:, HID:]], axis=0)
        own[...] = rows.astype(BF).reshape(BLOCKS, 16, HID)

    for part in (0, 1):
        fulls[part][net.spot("x"), net.spot("y"), net.c] = own[:, :, STARTS[part]:STARTS[part] + WIDTHS[part]]

    @pl.when(net.z != 7)
    def _():
        full_c[net.spot("x"), net.spot("y"), net.c, net.z] = own[net.z, :, STARTS[2]:]

    net.meet(greeted)
    for part in (0, 1):
        for d in (2, 1, 3):
            second_copy(net, fulls, sems, part, d, False).start()
    ring = LineLast(net, full_c, sem_c)
    ring.start()

    def prepare():
        loads[0].wait()
        norm_patches(patches, normed, normed_t)

    def first_heads():
        for load in loads[1:]:
            load.wait()
        attend(queries, keys, attention, attention_t, range(3))
        mean_signal(upstream, signal_mean)

    gather_all(
        net, fulls, sems, ring,
        (
            prepare,
            first_heads,
            lambda: attend(queries, keys, attention, attention_t, range(3, 6)),
            lambda: attend(queries, keys, attention, attention_t, range(6, 8)),
        ),
    )
    set_output(fulls, output, None)

    def write_base(at, total):
        base[:, at] = total
        values[:, at] = total.astype(BF)

    project(normed, fulls, write_base)

    def back():
        backward(patches, upstream, signal_mean, attention, attention_t, output, values, mixed, mixed_t, outcome, d_outcome, d_values)

    def make(core):
        write_grads(core, normed_t, mixed_t, d_outcome, d_values, grads)

    back()
    drain = reduce_all(net, grads, outs, scratch, make)

    @pl.when(net.z != 7)
    def _():
        full_c[net.spot("x"), net.spot("y"), net.c, net.z] = out_c[...]

    ring.start()
    spread_line(net, fulls, outs, sems, lines, ring)
    gather_all(net, fulls, sems, ring, started=True)
    drain_line(net, fulls, lines)
    drain()
    mean_square = sum_squares(fulls) / (2.0 * D * HID)
    stretch = rho_scale / jnp.sqrt(mean_square + 1e-06)
    set_output(fulls, output, stretch)

    def write_values(at, total):
        values[:, at] = (base[:, at] + stretch * total).astype(BF)

    project(normed, fulls, write_values)
    back()
    drain = reduce_all(net, grads, outs, scratch, make)
    share_owned(net, outs, owned, last, pairs)
    drain()
    value_grad[...] = owned[0]
    rows = owned[1].astype(F32).reshape(112, HID)
    output_grad[:, :HID] = rows[:56]
    output_grad[:, HID:] = rows[56:]


def vmem(n):
    return [pl.BlockSpec(memory_space=pltpu.VMEM)] * n


def gradients(patches, queries, keys, upstream, value_weight, output_weight):
    rows = patches.shape[0]
    return pl.pallas_call(
        kernel,
        out_shape=(
            jax.ShapeDtypeStruct((BLOCKS, 16, HID), BF),
            jax.ShapeDtypeStruct((56, D), F32),
        ),
        in_specs=[pl.BlockSpec(memory_space=pl.ANY)] * 4 + vmem(2),
        out_specs=vmem(2),
        scratch_shapes=(
            [pltpu.VMEM((rows, w), BF) for w in (D, HID, HID, D)]
            + [pltpu.VMEM((BLOCKS, 16, HID), BF), pltpu.VMEM((rows, 128), F32), pltpu.SemaphoreType.DMA((4,))]
            + [pltpu.VMEM((4, 4, 2, BLOCKS, 16, w), BF) for w in WIDTHS]
            + [pltpu.VMEM((4, 4, 2, BLOCKS, 16, w), BF) for w in WIDTHS]
            + [pltpu.VMEM((2, BLOCKS, 16, HID), BF)]
            + [pltpu.VMEM((16, w), BF) for w in WIDTHS]
            + [
                pltpu.VMEM((rows, D), BF),
                pltpu.VMEM((112, 16, rows), BF),
                pltpu.VMEM((HEADS, SEQ, SEQ), BF),
                pltpu.VMEM((HEADS, SEQ, SEQ), BF),
                pltpu.VMEM((rows, HID), F32),
                pltpu.VMEM((rows, HID), BF),
                pltpu.VMEM((56, 16, D), BF),
                pltpu.VMEM((rows, HID), BF),
                pltpu.VMEM((112, 8, rows), F32),
                pltpu.VMEM((rows, D), F32),
                pltpu.VMEM((rows, D), BF),
                pltpu.VMEM((rows, HID), BF),
            ]
            + gather_scratch()
            + [pltpu.SemaphoreType.DMA((2, 7))] * 3
            + [pltpu.SemaphoreType.DMA((2, 8))]
            + reduce_scratch()
        ),
        name="gradients",
        compiler_params=pltpu.CompilerParams(
            collective_id=0, has_side_effects=True, vmem_limit_bytes=60 * 2**20
        ),
    )(patches, queries, keys, upstream, value_weight, output_weight)


def adam_update(weight, first, second, gradient):
    first_new = beta_one * first + (1.0 - beta_one) * gradient
    second_new = beta_two * second + (1.0 - beta_two) * gradient * gradient
    update = (
        first_new / first_fix / (jnp.sqrt(second_new / second_fix) + adam_eps)
        + weight_decay * weight
    )
    return (weight - learn_rate * update, first_new, second_new)


def on_device(
    patches,
    queries,
    keys,
    upstream,
    value_weight,
    output_weight,
    value_first,
    output_first,
    value_second,
    output_second,
):
    value_grad, output_grad = gradients(patches, queries, keys, upstream, value_weight, output_weight)
    value_new, value_first_new, value_second_new = adam_update(
        value_weight, value_first, value_second, value_grad.reshape(112, HID).astype(F32)
    )
    output_new, output_first_new, output_second_new = adam_update(
        output_weight, output_first, output_second, output_grad
    )
    return (
        value_new,
        output_new,
        value_first_new,
        output_first_new,
        value_second_new,
        output_second_new,
    )


def solution(mesh):
    return jax.shard_map(
        on_device,
        mesh=mesh,
        in_specs=(P(("dp", "fsdp"), None),) * 4 + (P("fsdp", None),) * 6,
        out_specs=(P("fsdp", None),) * 6,
        check_vma=False,
    )
```
